512 devices in a mesh: lm: 16 (over z), prow: 4 (over y_lo, core), pcol: 8 (over x, y_hi).
Axes of the slice: x: 4, y: 4 (y_hi: 2, y_lo: 2; y = y_hi * 2 + y_lo), z: 16, core: 2. Of those that a mesh axis runs over, the one named last changes fastest.
Arguments:
- queries: bfloat16 [2048, 4096], P('lm', ('prow', 'pcol')), may hold values from -8 to 8
- keys: bfloat16 [2048, 4096], P('lm', ('prow', 'pcol')), may hold values from -6 to 6
- values: bfloat16 [2048, 4096], P('lm', ('prow', 'pcol')), may hold values from -8 to 8
- residual: bfloat16 [2048, 5120], P('lm', ('prow', 'pcol')), may hold values from -2 to 2
- out_proj: bfloat16 [4096, 5120], P(('prow', 'pcol')), may hold values from -0.1875 to 0.1875
- pair_proj: bfloat16 [5120, 256], P(('prow', 'pcol')), may hold values from -0.078125 to 0.078125
- chain_bias: float32 [2, 128], replicated, may hold values from -4 to 4
- ln_gain: float32 [128], replicated, may hold values from 0.1 to 1.9
- w_in: bfloat16 [128, 512], replicated, may hold values from -0.5 to 0.5
- w_out: bfloat16 [512, 128], replicated, may hold values from -0.25 to 0.25
- pair_cot: bfloat16 [1024, 2048, 128], P(('lm', 'prow'), 'pcol'), may hold values from -6 to 6
- residue_mask: int32 [2048], replicated, may hold values from 0 to 1, as said below
- chain_ids: int32 [2048], replicated, may hold values from 0 to 7, never falling along the last dimension, each value on 1 to 1024 neighbouring positions
- slab_start: int32 [1], replicated, may hold values from 0 to 1024
Outputs:
- pair_out: bfloat16 [1024, 2048, 128], P(('lm', 'prow'), 'pcol')
- lm_grad: bfloat16 [2048, 5120], P('lm', ('prow', 'pcol'))
The draws below stay inside these ranges and needn't reach their ends.
Inputs may be any that keep to these rules, and one draw needn't show every extreme that they name: `residue_mask`: residue 0 is always a residue.
All inputs are finite; a program needn't handle non-finite values.
Results may differ from the reference program's by a relative error of at most 0.035.
Values may be sent and summed in bfloat16 or wider, within the bound.
A program may use at most 64 MiB of HBM per device.

```python
import math
import jax
import jax.numpy as jnp
import numpy as np
from jax import lax

D = 5120
E = 128
HEADS = 32
C = 128
FFP = 512
CHAINS = 8
SLAB_DEV = 16
L = 2048
SLAB = 1024


def draw_queries(key, part):
    key = jax.random.fold_in(key, 11)
    sample = jnp.clip(2.0 * jax.random.normal(key, (L, HEADS * E), jnp.float32), -8.0, 8.0)
    return sample.astype(jnp.bfloat16)


def draw_keys(key, part):
    key = jax.random.fold_in(key, 13)
    sample = jnp.clip(jax.random.normal(key, (L, HEADS * E), jnp.float32), -6.0, 6.0)
    return sample.astype(jnp.bfloat16)


def draw_residue_mask(key, part):
    key = jax.random.fold_in(key, 17)
    marks = (jax.random.randint(key, (L,), 0, 16) != 0).astype(jnp.int32)
    return marks.at[0].set(1)


def raised(values, stream_key, source, target, parts, factor):
    def block_of(dim):
        return (jnp.arange(values.shape[dim]) // (values.shape[dim] // parts)).reshape((-1,) + (1,) * (values.ndim - 1 - dim))

    first = jax.random.permutation(stream_key, parts)[block_of(target)]
    far = (block_of(target) + parts // 2) % parts
    return jnp.where((block_of(source) == first) | (block_of(source) == far), factor * values, values)


def block_levels(key, dims, split, smallest, high):
    level, own = 1.0, jax.random.fold_in(key, 6)
    for dim, shards_of in split:
        heights = jnp.exp(jax.random.uniform(jax.random.fold_in(own, dim), (shards_of,), jnp.float32, smallest / len(split), high / len(split)))
        level = level * jnp.repeat(heights, dims[dim] // shards_of).reshape([-1 if axis == dim else 1 for axis in range(len(dims))])
    return level


def length_profile(number_of, total, limit, slope):
    portions = [(1 << 20) // math.isqrt(rank ** slope) + 1 for rank in range(2, number_of + 1)]
    surplus, counts = total - limit - (number_of - 1), [1] * (number_of - 1)
    while surplus > 0:
        free = [i for i in range(number_of - 1) if counts[i] < limit]
        mass, remaining = sum([portions[i] for i in free]), surplus
        for i in free:
            addition = min(limit - counts[i], max(1, remaining * portions[i] // mass), surplus)
            counts[i] = counts[i] + addition
            surplus = surplus - addition
    return np.array([limit] + counts)


def uneven(rng, number_of, total, most, lean):
    if number_of == 2:
        one = jax.random.randint(rng, (), max(1, total - most), min(most, total - 1) + 1)
        return jnp.stack([one, total - one])
    tallies = jnp.asarray(length_profile(number_of, total, most, lean), jnp.int32)
    couples = (number_of - 1) // 2
    donor, taker = tallies[1:1 + 2 * couples:2], tallies[2:2 + 2 * couples:2]
    room = jnp.minimum(donor - 1, most - taker)
    moved = jax.random.randint(jax.random.fold_in(rng, 1), (couples,), 0, 1 << 20) % (room + 1)
    tallies = tallies.at[1:1 + 2 * couples:2].set(donor - moved).at[2:2 + 2 * couples:2].set(taker + moved)
    return tallies[jax.random.permutation(jax.random.fold_in(rng, 2), number_of)]


def bell_draw(rng, dims, spread, most, shards=(), kind=jnp.bfloat16):
    values = spread * jax.random.normal(rng, dims, jnp.float32)
    if shards:
        values = values * block_levels(rng, dims, shards, -0.22, 0.18)
    return jnp.clip(values, -most, most).astype(kind)


def bell_draw_with(key, shape, spread, reach, pieces, heavy, dtype=jnp.bfloat16):
    values = spread * jax.random.normal(key, shape, jnp.float32)
    if pieces:
        values = values * block_levels(key, shape, pieces, -0.22, 0.18)
    return jnp.clip(raised(values, jax.random.fold_in(key, 3), *heavy), -reach, reach).astype(dtype)


def setup_inputs(seed: int = 0) -> dict:
    key_of = jax.random.split(jax.random.key(seed), 15)
    return {
        "queries": draw_queries(jax.random.fold_in(key_of[14], 71), 0),
        "keys": draw_keys(jax.random.fold_in(key_of[14], 71), 0),
        "values": bell_draw(key_of[2], (L, HEADS * E), 2.0, 8.0, ((0, 16), (1, 32))),
        "residual": bell_draw(key_of[3], (L, D), 0.3, 2.0, ((0, 16), (1, 32))),
        "out_proj": bell_draw_with(key_of[4], (HEADS * E, D), (HEADS * E) ** -0.5, 0.1875, ((0, 32),), (0, 1, 32, 2.75)),
        "pair_proj": bell_draw(key_of[5], (D, 2 * C), D ** -0.5, 0.078125, ((0, 32),)),
        "chain_bias": bell_draw(key_of[6], (2, C), 1.0, 4.0, (), jnp.float32),
        "ln_gain": jnp.clip(1.0 + 0.18 * jax.random.normal(key_of[7], (C,), jnp.float32), 0.1, 1.9),
        "w_in": bell_draw(key_of[8], (C, FFP), C ** -0.5, 0.5),
        "w_out": bell_draw(key_of[9], (FFP, C), FFP ** -0.5, 0.25),
        "pair_cot": bell_draw(key_of[10], (SLAB, L, C), 1.0, 6.0, ((0, 64), (1, 8))),
        "residue_mask": draw_residue_mask(jax.random.fold_in(key_of[14], 71), 0),
        "chain_ids": jnp.searchsorted(jnp.cumsum(uneven(key_of[12], CHAINS, L, L // 2, 0)), jnp.arange(L), side="right").astype(jnp.int32),
        "slab_start": jax.random.randint(key_of[13], (1,), 0, L - SLAB + 1).astype(jnp.int32),
    }


def pair_terms(a_rows, b_columns, live_rows, live_columns, chain_rows, chain_columns, chain_bias, ln_gain, w_in, w_out, pair_cot):
    row_count = a_rows.shape[0]
    column_count = b_columns.shape[0]
    width = a_rows.shape[1]
    a_float = a_rows.astype(jnp.float32)
    b_float = b_columns.astype(jnp.float32)
    live_pair = live_rows[:, None] * live_columns[None, :]
    same_chain = chain_rows[:, None] == chain_columns[None, :]
    bias = jnp.where(same_chain[:, :, None], chain_bias[1][None, None, :], chain_bias[0][None, None, :])
    pair_seed = live_pair[:, :, None] * (a_float[:, None, :] * b_float[None, :, :] + bias)
    centre = pair_seed - lax.optimization_barrier(jnp.mean(pair_seed, axis=2, keepdims=True))
    inverse = lax.rsqrt(lax.optimization_barrier(jnp.mean(centre * centre, axis=2, keepdims=True)) + 1e-05)
    normed = centre * inverse
    scaled = (normed * ln_gain[None, None, :]).astype(jnp.bfloat16).reshape(row_count * column_count, width)
    hidden = jnp.dot(scaled, w_in, preferred_element_type=jnp.float32)
    sigmoid = jax.nn.sigmoid(hidden)
    act = (hidden * sigmoid).astype(jnp.bfloat16)
    result = pair_seed + jnp.dot(act, w_out, preferred_element_type=jnp.float32).reshape(row_count, column_count, width)
    flat_cot = pair_cot.reshape(row_count * column_count, width)
    d_act = lax.dot_general(flat_cot, w_out, (((1,), (1,)), ((), ())), preferred_element_type=jnp.float32)
    d_hidden = (d_act * sigmoid * (1.0 + hidden * (1.0 - sigmoid))).astype(jnp.bfloat16)
    d_scaled = lax.dot_general(d_hidden, w_in, (((1,), (1,)), ((), ())), preferred_element_type=jnp.float32)
    d_normed = d_scaled.reshape(row_count, column_count, width) * ln_gain[None, None, :]
    d_seed = pair_cot.astype(jnp.float32) + inverse * (d_normed - lax.optimization_barrier(jnp.mean(d_normed, axis=2, keepdims=True)) - normed * lax.optimization_barrier(jnp.mean(d_normed * normed, axis=2, keepdims=True)))
    d_prod = d_seed * live_pair[:, :, None]
    grad_rows = lax.optimization_barrier(jnp.sum(d_prod * b_float[None, :, :], axis=1))
    grad_columns = lax.optimization_barrier(jnp.sum(d_prod * a_float[:, None, :], axis=0))
    return (result.astype(jnp.bfloat16), grad_rows, grad_columns)

def reference(queries, keys, values, residual, out_proj, pair_proj, chain_bias, ln_gain, w_in, w_out, pair_cot, residue_mask, chain_ids, slab_start):
    live = residue_mask.astype(jnp.float32)
    scale = 1.0 / math.sqrt(E)
    query_heads = jnp.moveaxis(queries.reshape(L, HEADS, E), 1, 0)
    key_heads = jnp.moveaxis(keys.reshape(L, HEADS, E), 1, 0)
    value_heads = jnp.moveaxis(values.reshape(L, HEADS, E), 1, 0)

    def one_head(triple):
        query_head, key_head, value_head = triple
        scores = lax.dot_general(query_head, key_head, (((1,), (1,)), ((), ())), preferred_element_type=jnp.float32) * scale
        scores = jnp.where(live[None, :] > 0, scores, -1e+30)
        highest = lax.optimization_barrier(jnp.max(scores, axis=1, keepdims=True))
        shifted = jnp.exp(scores - highest) * live[None, :]
        denominator = lax.optimization_barrier(jnp.sum(shifted, axis=1, keepdims=True))
        summed = jnp.dot(shifted.astype(jnp.bfloat16), value_head, preferred_element_type=jnp.float32)
        return (summed / denominator).astype(jnp.bfloat16)
    attended = lax.map(one_head, (query_heads, key_heads, value_heads))
    attended = jnp.moveaxis(attended, 0, 1).reshape(L, HEADS * E)
    stream = (residual.astype(jnp.float32) + jnp.dot(attended, out_proj, preferred_element_type=jnp.float32)).astype(jnp.bfloat16)
    projected = jnp.dot(stream, pair_proj, preferred_element_type=jnp.float32).astype(jnp.bfloat16)
    left_all = projected[:, :C]
    right_all = projected[:, C:]
    first = slab_start[0].astype(jnp.int32)
    left_slab = lax.dynamic_slice_in_dim(left_all, first, SLAB, 0)
    live_slab = lax.dynamic_slice_in_dim(live, first, SLAB, 0)
    chain_slab = lax.dynamic_slice_in_dim(chain_ids, first, SLAB, 0)
    block = SLAB_DEV
    blocks = SLAB // block

    def step(grad_right, inputs):
        left_rows, live_rows, chain_rows, cot_rows = inputs
        out_rows, grad_rows, grad_part = pair_terms(left_rows, right_all, live_rows, live, chain_rows, chain_ids, chain_bias, ln_gain, w_in, w_out, cot_rows)
        return (grad_right + grad_part, (out_rows, grad_rows))
    start_grad = jnp.zeros((L, C), jnp.float32)
    grad_right, (out_blocks, grad_left) = lax.scan(step, start_grad, (left_slab.reshape(blocks, block, C), live_slab.reshape(blocks, block), chain_slab.reshape(blocks, block), pair_cot.reshape(blocks, block, L, C)))
    pair_out = out_blocks.reshape(SLAB, L, C)
    left_full = lax.dynamic_update_slice(jnp.zeros((L, C), jnp.float32), grad_left.reshape(SLAB, C), (first, jnp.zeros((), jnp.int32)))
    proj_grad = jnp.concatenate([left_full, grad_right], axis=1).astype(jnp.bfloat16)
    lm_grad = lax.dot_general(proj_grad, pair_proj, (((1,), (1,)), ((), ())), preferred_element_type=jnp.float32).astype(jnp.bfloat16)
    return (pair_out, lm_grad)
```

```python
import functools
import math

import jax
import jax.numpy as jnp
from jax import lax
from jax.experimental import pallas as pl
from jax.experimental.pallas import tpu as pltpu
from jax.sharding import PartitionSpec as P

BF = jnp.bfloat16
F32 = jnp.float32
MESH = pl.DeviceIdType.MESH
E = 128
W = 256


def nn(a, b):
    return lax.dot_general(a, b, (((1,), (0,)), ((), ())), preferred_element_type=F32)


def nt(a, b):
    return lax.dot_general(a, b, (((1,), (1,)), ((), ())), preferred_element_type=F32)


def grid_of(rows, columns):
    row = lax.broadcasted_iota(jnp.int32, (rows, columns), 0)
    column = lax.broadcasted_iota(jnp.int32, (rows, columns), 1)
    return row, column


def one_hot(hit):
    return jnp.where(hit, 1.0, 0.0).astype(BF)


def bits(n):
    return n.bit_length() - 1


class Place:
    def __init__(self, sizes):
        self.nz, self.pr, self.pc = sizes
        self.np = self.pr * self.pc
        self.z = lax.axis_index("lm")
        self.prow = lax.axis_index("prow")
        self.pcol = lax.axis_index("pcol")
        self.q = self.prow * self.pc + self.pcol

    def plane_peer(self, i):
        peer = lax.rem(self.q + i, self.np)
        return peer, (self.z, peer // self.pc, lax.rem(peer, self.pc))

    def z_peer(self, i):
        peer = lax.rem(self.z + i, self.nz)
        return peer, (peer, self.prow, self.pcol)

    def signal_all(self, barrier):
        def plane(i, carry):
            pl.semaphore_signal(
                barrier, inc=1, device_id=self.plane_peer(i)[1], device_id_type=MESH
            )
            return carry

        def column(i, carry):
            pl.semaphore_signal(barrier, inc=1, device_id=self.z_peer(i)[1], device_id_type=MESH)
            return carry

        lax.fori_loop(1, self.np, plane, 0)
        lax.fori_loop(1, self.nz, column, 0)

    def wait_all(self, barrier):
        pl.semaphore_wait(barrier, self.np + self.nz - 2)

    def to_plane(self, source, target, send_sem, recv_sem):
        def step(i, carry):
            peer, device = self.plane_peer(i)
            pltpu.make_async_remote_copy(
                src_ref=source(peer),
                dst_ref=target.at[self.q],
                send_sem=send_sem,
                recv_sem=recv_sem,
                device_id=device,
                device_id_type=MESH,
            ).start()
            return carry

        lax.fori_loop(1, self.np, step, 0)

    def to_column(self, source, target, send_sem, recv_sem):
        def step(i, carry):
            peer, device = self.z_peer(i)
            pltpu.make_async_remote_copy(
                src_ref=source(peer),
                dst_ref=target.at[self.z],
                send_sem=send_sem,
                recv_sem=recv_sem,
                device_id=device,
                device_id_type=MESH,
            ).start()
            return carry

        lax.fori_loop(1, self.nz, step, 0)


def wait_bytes(buffer, count, sem):
    part = buffer.at[pl.ds(0, count)]
    pltpu.make_async_copy(part, part, sem).wait()


def forward_kernel(
    sizes,
    start_ref,
    mask_ref,
    q_ref,
    k_ref,
    v_ref,
    res_ref,
    op_hbm,
    pp_ref,
    ab_ref,
    op,
    kbuf,
    vbuf,
    sbuf,
    perm,
    pick,
    place_rows,
    presidual,
    ppmsg,
    ppg,
    w2acc,
    w2msg,
    w2g,
    pmsg,
    pbuf,
    tmsg,
    zbuf,
    msg,
    rbuf,
    op_sem,
    ring_send,
    ring_recv,
    send_sem,
    recv_sem,
):
    me = Place(sizes)
    nz, pr, pc, np_ = me.nz, me.pr, me.pc, me.np
    z, q = me.z, me.q
    rb = q_ref.shape[0]
    fd = pp_ref.shape[0]
    wz = W // nz
    columns = 8 * np_
    slab_plane = 2 * np_
    slab_tile = slab_plane // pr
    log_np = bits(np_)

    barrier = pltpu.get_barrier_semaphore()
    me.signal_all(barrier)
    fetch = pltpu.make_async_copy(op_hbm, op, op_sem)
    fetch.start()
    kbuf[z] = k_ref[...]
    vbuf[z] = v_ref[...]

    row, column = grid_of(wz, W)
    mine = one_hot(column == row + z * wz)
    piece = nt(mine, pp_ref[...]).astype(BF)
    row, column = grid_of(fd, W)
    shift = one_hot(column == row + ((fd * q) & 127))
    piece = nn(piece, shift).astype(BF)
    ppmsg[...] = piece
    ppg[q] = piece

    me.wait_all(barrier)

    def ring(chain, s):
        buf = kbuf if chain < 2 else vbuf
        way = 1 if chain % 2 == 0 else -1
        block = lax.rem(z - way * s + nz, nz)
        peer = lax.rem(z + way + nz, nz)
        return pltpu.make_async_remote_copy(
            src_ref=buf.at[block],
            dst_ref=buf.at[block],
            send_sem=ring_send.at[chain, s],
            recv_sem=ring_recv.at[chain, s],
            device_id=(peer, me.prow, me.pcol),
            device_id_type=MESH,
        )

    steps = (nz // 2, nz - 1 - nz // 2)
    for chain in range(4):
        if steps[chain % 2] > 0:
            ring(chain, 0).start()
    me.to_plane(lambda peer: ppmsg, ppg, send_sem.at[0], recv_sem.at[0])

    scale = 1.0 / math.sqrt(E)

    def score(block):
        raw = nt(q_ref[...], kbuf[block]) * scale
        live = mask_ref[pl.ds(block, 1), :]
        sbuf[block] = jnp.where(live > 0, raw, -1e30)

    row, column = grid_of(8 * np_, rb)
    perm[...] = one_hot(column == (row & 3) * np_ + (row >> 3))
    w0 = start_ref[0] + z * slab_plane
    r0 = w0 + ((q - w0) & (np_ - 1))
    k0 = r0 >> log_np
    row, column = grid_of(pc * 16, 8 * nz)
    sub = row & 15
    right_hit = (sub < 8) & (column == (2 * (row >> 4) + (sub >> 2)) * 8 + 4 + (sub & 3))
    kk = k0 + (sub - 8)
    left_hit = ((sub == 8) | (sub == 9)) & (column == (kk >> 2) * 8 + (kk & 3))
    pick[...] = one_hot(right_hit | left_hit)
    row, column = grid_of(columns + slab_tile, 16 * np_)
    first = w0 + me.prow * slab_tile
    second_half = jnp.where(me.prow >= pr // 2, 1, 0)
    right_hit = (row < columns) & (column == (row & (np_ - 1)) * 16 + (row >> log_np))
    left_hit = (row >= columns) & (
        column == ((first + row - columns) & (np_ - 1)) * 16 + 8 + second_half
    )
    place_rows[...] = one_hot(right_hit | left_hit)
    rows_twice = nn(perm[...], res_ref[...]).astype(BF)
    both = nn(rows_twice, pp_ref[...])
    row, column = grid_of(8 * np_, E)
    is_left = (row & 7) < 4
    presidual[...] = jnp.where(is_left, both[:, :E], both[:, E:])

    score(z)
    w2acc[...] = jnp.zeros_like(w2acc)
    groups = min(4, np_)
    per_group = np_ // groups

    def w2_group(g):
        total = w2acc[...]
        for i in range(per_group):
            chunk = g * per_group + i
            at = pl.multiple_of(((fd * chunk) >> 7) << 7, 128)
            total = total + nt(op[:, pl.ds(at, W)], ppg[chunk])
        w2acc[...] = total

    def ring_step(s):
        for chain in (0, 1):
            if s < steps[chain]:
                ring(chain, s).wait_recv()
                if s + 1 < steps[chain]:
                    ring(chain, s + 1).start()
        for chain in (2, 3):
            if s < steps[chain % 2]:
                ring(chain, s).wait_recv()
                if s + 1 < steps[chain % 2]:
                    ring(chain, s + 1).start()
        if s < steps[0]:
            score(lax.rem(z - 1 - s + nz, nz))
        if s < steps[1]:
            score(lax.rem(z + 1 + s, nz))

    def w2_send():
        w2 = w2acc[...].astype(BF)
        row, column = grid_of(wz, wz)
        turned = nt(one_hot(row == column), w2).astype(BF)
        w2msg[...] = turned
        w2g[z] = turned
        me.to_column(lambda peer: w2msg, w2g, send_sem.at[1], recv_sem.at[1])

    done = 0
    for s in range(steps[0]):
        ring_step(s)
        if s == 0:
            fetch.wait()
            wait_bytes(ppg, np_ - 1, recv_sem.at[0])
        while done < groups and (done < s + 1 or s + 1 == steps[0]):
            w2_group(done)
            done += 1
            if done == groups:
                w2_send()

    def widest(b, carry):
        return jnp.maximum(carry, sbuf[b])

    top = lax.fori_loop(0, nz, widest, jnp.full((rb, rb), -1e30, F32))
    top = jnp.max(top, axis=1, keepdims=True)

    def soften(b, carry):
        below, above = carry
        shifted = jnp.exp(sbuf[b] - top)
        return below + shifted, above + nn(shifted.astype(BF), vbuf[b])

    below, above = lax.fori_loop(
        0, nz, soften, (jnp.zeros((rb, rb), F32), jnp.zeros((rb, E), F32))
    )
    attended = (above / jnp.sum(below, axis=1, keepdims=True)).astype(BF)

    wait_bytes(w2g, nz - 1, recv_sem.at[1])
    twice = nn(perm[...], attended).astype(BF)
    w2 = w2g[...].reshape(W, E)
    both = nt(twice, w2)
    row, column = grid_of(8 * np_, E)
    is_left = (row & 7) < 4
    terms = jnp.where(is_left, both[:, :E], both[:, E:]) + presidual[...]
    pmsg[...] = terms.reshape(np_, 8, E)
    me.to_plane(lambda peer: pmsg.at[peer], pbuf, send_sem.at[2], recv_sem.at[2])
    pbuf[q] = pmsg[q]
    wait_bytes(pbuf, np_ - 1, recv_sem.at[2])
    projected = jnp.sum(pbuf[...], axis=0).astype(BF).astype(F32)
    tmsg[...] = projected
    zbuf[z] = projected
    me.to_column(lambda peer: tmsg, zbuf, send_sem.at[3], recv_sem.at[3])
    wait_bytes(zbuf, nz - 1, recv_sem.at[3])
    chosen = nn(pick[...], zbuf[...].reshape(8 * nz, E).astype(BF)).astype(BF)
    msg[...] = chosen.reshape(pc, 16, E)
    me.to_plane(
        lambda peer: msg.at[lax.rem(peer, pc)], rbuf, send_sem.at[4], recv_sem.at[4]
    )
    rbuf[q] = msg[me.pcol]
    wait_bytes(rbuf, np_ - 1, recv_sem.at[4])
    ab_ref[...] = nn(place_rows[...], rbuf[...].reshape(16 * np_, E))

    for chain in range(4):
        for s in range(steps[chain % 2]):
            ring(chain, s).wait_send()
    wait_bytes(ppg, np_ - 1, send_sem.at[0])
    wait_bytes(w2g, nz - 1, send_sem.at[1])
    wait_bytes(pbuf, np_ - 1, send_sem.at[2])
    wait_bytes(zbuf, nz - 1, send_sem.at[3])
    wait_bytes(rbuf, np_ - 1, send_sem.at[4])


def forward(sizes, start, mask, queries, keys, values, residual, out_proj, pair_proj):
    nz, pr, pc = sizes
    np_ = pr * pc
    rb = queries.shape[0]
    d = out_proj.shape[1]
    columns = 8 * np_
    tile = 2 * np_ // pr
    wz = W // nz
    vmem = pl.BlockSpec(memory_space=pltpu.VMEM)
    return pl.pallas_call(
        functools.partial(forward_kernel, sizes),
        out_shape=jax.ShapeDtypeStruct((columns + tile, E), F32),
        in_specs=[pl.BlockSpec(memory_space=pltpu.SMEM)]
        + [vmem] * 5
        + [pl.BlockSpec(memory_space=pl.ANY), vmem],
        out_specs=vmem,
        scratch_shapes=[
            pltpu.VMEM((E, d), BF),
            pltpu.VMEM((nz, rb, E), BF),
            pltpu.VMEM((nz, rb, E), BF),
            pltpu.VMEM((nz, rb, rb), F32),
            pltpu.VMEM((8 * np_, rb), BF),
            pltpu.VMEM((pc * 16, 8 * nz), BF),
            pltpu.VMEM((columns + tile, 16 * np_), BF),
            pltpu.VMEM((8 * np_, E), F32),
            pltpu.VMEM((wz, W), BF),
            pltpu.VMEM((np_, wz, W), BF),
            pltpu.VMEM((E, wz), F32),
            pltpu.VMEM((wz, E), BF),
            pltpu.VMEM((nz, wz, E), BF),
            pltpu.VMEM((np_, 8, E), F32),
            pltpu.VMEM((np_, 8, E), F32),
            pltpu.VMEM((8, E), F32),
            pltpu.VMEM((nz, 8, E), F32),
            pltpu.VMEM((pc, 16, E), BF),
            pltpu.VMEM((np_, 16, E), BF),
            pltpu.SemaphoreType.DMA,
            pltpu.SemaphoreType.DMA((4, max(1, nz // 2))),
            pltpu.SemaphoreType.DMA((4, max(1, nz // 2))),
            pltpu.SemaphoreType.DMA((5,)),
            pltpu.SemaphoreType.DMA((5,)),
        ],
        compiler_params=pltpu.CompilerParams(
            collective_id=0, has_side_effects=True, vmem_limit_bytes=32 << 20
        ),
        name="attend_and_project",
    )(start, mask, queries, keys, values, residual, out_proj, pair_proj)


def pair_kernel(
    rows_here,
    start_ref,
    mask_ref,
    chain_ref,
    ab_ref,
    live_ref,
    same_ref,
    bias_ref,
    gain_ref,
    w_in_ref,
    w_out_ref,
    cot_ref,
    out_ref,
    grad_ref,
    w_half,
    w_out_half,
):
    columns = cot_ref.shape[1]
    per_step = cot_ref.shape[0]
    step = pl.program_id(0)

    @pl.when(step == 0)
    def _():
        grad_ref[...] = jnp.zeros_like(grad_ref)
        w_half[...] = (w_in_ref[...].astype(F32) * 0.5).astype(BF)
        w_out_half[...] = (w_out_ref[...].astype(F32) * 0.5).astype(BF)

    first = start_ref[0] + (lax.axis_index("lm") * lax.axis_size("prow") + lax.axis_index("prow")) * rows_here
    right = ab_ref[pl.ds(0, columns), :]
    live_columns = live_ref[...]
    gain = gain_ref[...]
    for i in range(per_step):
        t = step * per_step + i
        left = ab_ref[pl.ds(columns + t, 1), :]
        live = live_columns * mask_ref[first + t].astype(F32)
        bias = jnp.where(same_ref[...] == chain_ref[first + t], bias_ref[1:2, :], bias_ref[0:1, :])
        seed = live * (left * right + bias)
        centre = seed - jnp.mean(seed, axis=1, keepdims=True)
        inverse = lax.rsqrt(jnp.mean(centre * centre, axis=1, keepdims=True) + 1e-05)
        normed = centre * inverse
        scaled = (normed * gain).astype(BF)
        half = nn(scaled, w_half[...])
        turned = jnp.tanh(half)
        raised = 1.0 + turned
        act = half * raised
        cot = cot_ref[i]
        d_act = nt(cot, w_out_half[...])
        d_hidden = (d_act * (raised + act * (1.0 - turned))).astype(BF)
        out_ref[i] = (seed + nn(act.astype(BF), w_out_ref[...])).astype(BF)
        d_normed = nt(d_hidden, w_in_ref[...]) * gain
        d_seed = cot.astype(F32) + inverse * (
            d_normed
            - jnp.mean(d_normed, axis=1, keepdims=True)
            - normed * jnp.mean(d_normed * normed, axis=1, keepdims=True)
        )
        d_prod = d_seed * live
        grad_ref[pl.ds(0, columns), :] += d_prod * left
        grad_ref[pl.ds(columns + t, 1), :] = jnp.sum(d_prod * right, axis=0, keepdims=True)


def pair(start, mask, chain, ab, live_columns, chain_columns, chain_bias, gain, w_in, w_out, cot):
    rows, columns, width = cot.shape
    per_step = 2
    hidden = w_in.shape[1]
    smem = pl.BlockSpec(memory_space=pltpu.SMEM)

    def whole(a):
        return pl.BlockSpec(a.shape, lambda i: (0,) * a.ndim)

    block = pl.BlockSpec((per_step, columns, width), lambda i: (i, 0, 0))
    return pl.pallas_call(
        functools.partial(pair_kernel, rows),
        grid=(rows // per_step,),
        out_shape=(
            jax.ShapeDtypeStruct(cot.shape, BF),
            jax.ShapeDtypeStruct((columns + rows, width), F32),
        ),
        in_specs=[smem, smem, smem]
        + [whole(a) for a in (ab, live_columns, chain_columns, chain_bias, gain, w_in, w_out)]
        + [block],
        out_specs=(block, pl.BlockSpec((columns + rows, width), lambda i: (0, 0))),
        scratch_shapes=[pltpu.VMEM((width, hidden), BF), pltpu.VMEM((hidden, width), BF)],
        compiler_params=pltpu.CompilerParams(vmem_limit_bytes=32 << 20),
        name="pair_transition",
    )(start, mask, chain, ab, live_columns, chain_columns, chain_bias, gain, w_in, w_out, cot)


def backward_kernel(
    sizes,
    start_ref,
    grad_ref,
    pp_ref,
    lm_ref,
    msg,
    gbuf,
    zmsg,
    hbuf,
    fmsg,
    fbuf,
    send_sem,
    recv_sem,
):
    me = Place(sizes)
    nz, pr, pc, np_ = me.nz, me.pr, me.pc, me.np
    z, q = me.z, me.q
    rb = lm_ref.shape[0]
    columns = 8 * np_
    slab_plane = 2 * np_
    slab_tile = slab_plane // pr
    log_np = bits(np_)
    barrier = pltpu.get_barrier_semaphore()
    me.signal_all(barrier)

    w0 = start_ref[0] + z * slab_plane
    r0 = w0 + ((q - w0) & (np_ - 1))
    k0 = r0 >> log_np
    first = w0 + me.prow * slab_tile
    second_half = jnp.where(me.prow >= pr // 2, 1, 0)
    row, column = grid_of(16 * np_, columns + slab_tile)
    sub = row & 15
    owner = row >> 4
    right_hit = (sub < 8) & (column == sub * np_ + owner)
    left_hit = (
        (sub == 8 + second_half)
        & (column >= columns)
        & (((first + column - columns) & (np_ - 1)) == owner)
    )
    spread = one_hot(right_hit | left_hit)
    msg[...] = nn(spread, grad_ref[...].astype(BF)).astype(BF).reshape(np_, 16, E)
    me.wait_all(barrier)
    me.to_plane(lambda peer: msg.at[peer], gbuf, send_sem.at[0], recv_sem.at[0])
    gbuf[q] = msg[q]
    wait_bytes(gbuf, np_ - 1, recv_sem.at[0])
    by_column = jnp.sum(gbuf[...].astype(F32).reshape(pr, pc, 16, E), axis=0)
    over_columns = jnp.sum(by_column, axis=0)
    left0 = over_columns[8:9, :]
    left1 = over_columns[9:10, :]
    sub, _ = grid_of(8, E)
    for other in range(nz):
        k = 4 * other + (sub & 3)
        lefts = jnp.where(k == k0, left0, jnp.where(k == k0 + 1, left1, 0.0))
        zmsg[other] = jnp.where((sub >> 2) == other % 2, by_column[other // 2, 0:8, :], lefts)
    me.to_column(lambda peer: zmsg.at[peer], hbuf, send_sem.at[1], recv_sem.at[1])
    hbuf[z] = zmsg[z]
    wait_bytes(hbuf, nz - 1, recv_sem.at[1])
    tile = jnp.sum(hbuf[...], axis=0).astype(BF).astype(F32)
    fmsg[...] = tile
    fbuf[q] = tile
    me.to_plane(lambda peer: fmsg, fbuf, send_sem.at[2], recv_sem.at[2])
    odd = z & 1
    row, column = grid_of(rb, 8 * np_)
    base = (row & (np_ - 1)) * 8 + (row >> log_np)
    left_pick = one_hot(column == base + 4 * (1 - odd))
    right_pick = one_hot(column == base + 4 * odd)
    wait_bytes(fbuf, np_ - 1, recv_sem.at[2])
    tiles = fbuf[...].reshape(8 * np_, E).astype(BF)
    left = nn(left_pick, tiles).astype(BF)
    right = nn(right_pick, tiles).astype(BF)
    lm_ref[...] = (nt(left, pp_ref[:, :E]) + nt(right, pp_ref[:, E:])).astype(BF)
    wait_bytes(gbuf, np_ - 1, send_sem.at[0])
    wait_bytes(hbuf, nz - 1, send_sem.at[1])
    wait_bytes(fbuf, np_ - 1, send_sem.at[2])


def backward(sizes, rb, start, grads, pair_proj):
    nz, pr, pc = sizes
    np_ = pr * pc
    vmem = pl.BlockSpec(memory_space=pltpu.VMEM)
    return pl.pallas_call(
        functools.partial(backward_kernel, sizes),
        out_shape=jax.ShapeDtypeStruct((rb, pair_proj.shape[0]), BF),
        in_specs=[pl.BlockSpec(memory_space=pltpu.SMEM), vmem, vmem],
        out_specs=vmem,
        scratch_shapes=[
            pltpu.VMEM((np_, 16, E), BF),
            pltpu.VMEM((np_, 16, E), BF),
            pltpu.VMEM((nz, 8, E), F32),
            pltpu.VMEM((nz, 8, E), F32),
            pltpu.VMEM((8, E), F32),
            pltpu.VMEM((np_, 8, E), F32),
            pltpu.SemaphoreType.DMA((3,)),
            pltpu.SemaphoreType.DMA((3,)),
        ],
        compiler_params=pltpu.CompilerParams(
            collective_id=1, has_side_effects=True, vmem_limit_bytes=32 << 20
        ),
        name="reduce_gradients",
    )(start, grads, pair_proj)


def body(
    sizes,
    queries,
    keys,
    values,
    residual,
    out_proj,
    pair_proj,
    chain_bias,
    ln_gain,
    w_in,
    w_out,
    pair_cot,
    residue_mask,
    chain_ids,
    slab_start,
):
    rb = queries.shape[0]
    columns = pair_cot.shape[1]
    first_column = lax.axis_index("pcol") * columns
    live = residue_mask.astype(F32)
    live_columns = jnp.broadcast_to(
        lax.dynamic_slice_in_dim(live, first_column, columns)[:, None], (columns, E)
    )
    chain_columns = jnp.broadcast_to(
        lax.dynamic_slice_in_dim(chain_ids, first_column, columns)[:, None], (columns, E)
    )
    ab = forward(
        sizes,
        slab_start,
        residue_mask.reshape(sizes[0], rb),
        queries,
        keys,
        values,
        residual,
        out_proj,
        pair_proj,
    )
    pair_out, grads = pair(
        slab_start,
        residue_mask,
        chain_ids,
        ab,
        live_columns,
        chain_columns,
        chain_bias,
        ln_gain.reshape(1, E),
        w_in,
        w_out,
        pair_cot,
    )
    lm_grad = backward(sizes, rb, slab_start, grads, pair_proj)
    return pair_out, lm_grad


def solution(mesh):
    sizes = tuple(mesh.shape[name] for name in ("lm", "prow", "pcol"))
    return jax.shard_map(
        functools.partial(body, sizes),
        mesh=mesh,
        in_specs=(
            P("lm", ("prow", "pcol")),
            P("lm", ("prow", "pcol")),
            P("lm", ("prow", "pcol")),
            P("lm", ("prow", "pcol")),
            P(("prow", "pcol"), None),
            P(("prow", "pcol"), None),
            P(),
            P(),
            P(),
            P(),
            P(("lm", "prow"), "pcol", None),
            P(),
            P(),
            P(),
        ),
        out_specs=(P(("lm", "prow"), "pcol", None), P("lm", ("prow", "pcol"))),
        check_vma=False,
    )
```

```python
import functools
import math

import jax
import jax.numpy as jnp
from jax import lax
from jax.experimental import pallas as pl
from jax.experimental.pallas import tpu as pltpu
from jax.sharding import PartitionSpec as P

BF = jnp.bfloat16
F32 = jnp.float32
MESH = pl.DeviceIdType.MESH
E = 128
W = 256


def nn(a, b):
    return lax.dot_general(a, b, (((1,), (0,)), ((), ())), preferred_element_type=F32)


def nt(a, b):
    return lax.dot_general(a, b, (((1,), (1,)), ((), ())), preferred_element_type=F32)


def grid_of(rows, columns):
    row = lax.broadcasted_iota(jnp.int32, (rows, columns), 0)
    column = lax.broadcasted_iota(jnp.int32, (rows, columns), 1)
    return row, column


def one_hot(hit):
    return jnp.where(hit, 1.0, 0.0).astype(BF)


def bits(n):
    return n.bit_length() - 1


class Place:
    def __init__(self, sizes):
        self.nz, self.pr, self.pc = sizes
        self.np = self.pr * self.pc
        self.z = lax.axis_index("lm")
        self.prow = lax.axis_index("prow")
        self.pcol = lax.axis_index("pcol")
        self.q = self.prow * self.pc + self.pcol

    def plane_peer(self, i):
        peer = lax.rem(self.q + i, self.np)
        return peer, (self.z, peer // self.pc, lax.rem(peer, self.pc))

    def z_peer(self, i):
        peer = lax.rem(self.z + i, self.nz)
        return peer, (peer, self.prow, self.pcol)

    def signal_all(self, barrier):
        def plane(i, carry):
            pl.semaphore_signal(
                barrier, inc=1, device_id=self.plane_peer(i)[1], device_id_type=MESH
            )
            return carry

        def column(i, carry):
            pl.semaphore_signal(barrier, inc=1, device_id=self.z_peer(i)[1], device_id_type=MESH)
            return carry

        lax.fori_loop(1, self.np, plane, 0)
        lax.fori_loop(1, self.nz, column, 0)

    def wait_all(self, barrier):
        pl.semaphore_wait(barrier, self.np + self.nz - 2)

    def to_plane(self, source, target, send_sem, recv_sem):
        def step(i, carry):
            peer, device = self.plane_peer(i)
            pltpu.make_async_remote_copy(
                src_ref=source(peer),
                dst_ref=target.at[self.q],
                send_sem=send_sem,
                recv_sem=recv_sem,
                device_id=device,
                device_id_type=MESH,
            ).start()
            return carry

        lax.fori_loop(1, self.np, step, 0)

    def to_column(self, source, target, send_sem, recv_sem):
        def step(i, carry):
            peer, device = self.z_peer(i)
            pltpu.make_async_remote_copy(
                src_ref=source(peer),
                dst_ref=target.at[self.z],
                send_sem=send_sem,
                recv_sem=recv_sem,
                device_id=device,
                device_id_type=MESH,
            ).start()
            return carry

        lax.fori_loop(1, self.nz, step, 0)


def wait_bytes(buffer, count, sem):
    part = buffer.at[pl.ds(0, count)]
    pltpu.make_async_copy(part, part, sem).wait()


class Refs:
    def __init__(self, names, refs):
        for name, ref in zip(names, refs, strict=True):
            setattr(self, name, ref)


INPUTS = (
    "start",
    "q_hbm",
    "k_hbm",
    "v_hbm",
    "res_hbm",
    "op_hbm",
    "pp_hbm",
    "bias_hbm",
    "gain_hbm",
    "w_in_hbm",
    "w_out_hbm",
    "cot_hbm",
    "mask_hbm",
    "chain_hbm",
    "mask_flat_hbm",
    "chain_flat_hbm",
)
LOADS = (
    "k",
    "v",
    "pp",
    "q",
    "mask",
    "res",
    "chain",
    "bias",
    "gain",
    "w_in",
    "w_out",
    "op",
    "cot",
    "mask_flat",
    "chain_flat",
)


def pair_rows(r, i, per, columns, first):
    gain = r.gain[...]
    rows = [i * per + j for j in range(per)]
    lefts = [r.ab[pl.ds(columns + t, 1), :] for t in rows]
    right = r.ab[pl.ds(0, columns), :]
    spread = jnp.concatenate([jnp.broadcast_to(left, (E, E)) for left in lefts], axis=0)
    dots = nt(right.astype(BF), spread.astype(BF)) * (1.0 / E)
    seeds, centres = [], []
    for j, t in enumerate(rows):
        same = r.chain_column[...] == r.chain_flat[first + t].astype(F32)
        seed = lefts[j] * right + jnp.where(same, r.bias[1:2, :], r.bias[0:1, :])
        mean = dots[:, j * E : (j + 1) * E] + jnp.where(
            same, r.bias_mean[1:2, :], r.bias_mean[0:1, :]
        )
        seeds.append(seed)
        centres.append(seed - mean)
    inverses = []
    for j in range(0, per, 2):
        squares = jnp.concatenate([c * c for c in centres[j : j + 2]], axis=1).astype(BF)
        inverse = lax.rsqrt(nn(squares, r.means[...]) + 1e-05)
        inverses += [inverse[:, :E], inverse[:, E:]]
    normeds = [c * inverse for c, inverse in zip(centres, inverses)]
    scaled = jnp.concatenate([(n * gain).astype(BF) for n in normeds], axis=0)
    cots = [r.cot[t] for t in rows]
    half = nn(scaled, r.w_half[...])
    d_act = nt(jnp.concatenate(cots, axis=0), r.w_out_half[...])
    turned = jnp.tanh(half)
    raised = 1.0 + turned
    act = half * raised
    d_hidden = (d_act * (raised + act * (1.0 - turned))).astype(BF)
    y = nn(act.astype(BF), r.w_out[...])
    d_scaled = nt(d_hidden, r.w_in[...])
    total = jnp.zeros((columns, E), F32)
    for j, t in enumerate(rows):
        live = r.mask_flat[first + t].astype(F32)
        block = slice(j * columns, (j + 1) * columns)
        r.out[t] = ((seeds[j] + y[block]) * (r.live_column[...] * live)).astype(BF)
        d_normed = d_scaled[block] * gain
        both = jnp.concatenate([d_normed, d_normed * normeds[j]], axis=1).astype(BF)
        both = nn(both, r.means[...])
        d_seed = cots[j].astype(F32) + inverses[j] * (
            d_normed - both[:, :E] - normeds[j] * both[:, E:]
        )
        total = total + d_seed * (lefts[j] * live)
        r.grads[pl.ds(columns + t, 1), :] = live * jnp.sum(
            d_seed * r.right_live[...], axis=0, keepdims=True
        )
    r.grads[pl.ds(0, columns), :] += total


def kernel(sizes, names, *refs):
    r = Refs(names, refs)
    me = Place(sizes)
    nz, pr, pc, np_ = me.nz, me.pr, me.pc, me.np
    z, q = me.z, me.q
    rb = r.q.shape[0]
    fd = r.pp.shape[0]
    wz = W // nz
    columns = 8 * np_
    slab_plane = 2 * np_
    slab_tile = slab_plane // pr
    log_np = bits(np_)

    barrier = pltpu.get_barrier_semaphore()
    loads = {}
    for i, name in enumerate(LOADS):
        target = getattr(r, name)
        if name in ("k", "v"):
            target = target.at[z]
        loads[name] = pltpu.make_async_copy(getattr(r, name + "_hbm"), target, r.load_sem.at[i])
        loads[name].start()
    me.signal_all(barrier)

    loads["pp"].wait()
    row, column = grid_of(wz, W)
    piece = nt(one_hot(column == row + z * wz), r.pp[...]).astype(BF)
    row, column = grid_of(fd, W)
    piece = nn(piece, one_hot(column == row + ((fd * q) & 127))).astype(BF)
    r.ppmsg[...] = piece
    r.ppg[q] = piece
    loads["k"].wait()
    loads["v"].wait()
    me.wait_all(barrier)

    furthest = (nz // 2, nz - 1 - nz // 2)

    def ring(chain, distance, hop):
        buf = r.k if chain < 2 else r.v
        way = 1 if chain % 2 == 0 else -1
        block = lax.rem(z - way * (distance - hop) + nz, nz)
        peer = lax.rem(z + way * hop + nz, nz)
        return pltpu.make_async_remote_copy(
            src_ref=buf.at[block],
            dst_ref=buf.at[block],
            send_sem=r.ring_send.at[chain, distance - 1],
            recv_sem=r.ring_recv.at[chain, distance - 1],
            device_id=(peer, me.prow, me.pcol),
            device_id_type=MESH,
        )

    def pass_on(chain, held):
        for hop in (2, 1):
            if held + hop <= furthest[chain % 2]:
                ring(chain, held + hop, hop).start()

    for chain in range(4):
        pass_on(chain, 0)
    me.to_plane(lambda peer: r.ppmsg, r.ppg, r.send_sem.at[0], r.recv_sem.at[0])

    row, column = grid_of(8 * np_, rb)
    r.perm[...] = one_hot(column == (row & 3) * np_ + (row >> 3))
    loads["res"].wait()
    rows_twice = nt(r.perm[...], r.res[...]).astype(BF)
    both = nn(rows_twice, r.pp[...])
    row, column = grid_of(8 * np_, E)
    is_left = (row & 7) < 4
    r.presidual[...] = jnp.where(is_left, both[:, :E], both[:, E:])
    loads["q"].wait()
    loads["mask"].wait()

    scale = 1.0 / math.sqrt(E)

    def score(block):
        raw = nt(r.q[...], r.k[block]) * scale
        live = r.mask[pl.ds(block, 1), :]
        r.scores[block] = jnp.where(live > 0, raw, -1e30)

    score(z)

    def arrive(chain, distance):
        if distance <= furthest[chain % 2]:
            ring(chain, distance, 1 if distance % 2 else 2).wait_recv()
            if distance % 2 == 0:
                pass_on(chain, distance)

    def score_at(distance):
        if distance <= furthest[0]:
            score(lax.rem(z - distance + nz, nz))
        if distance <= furthest[1]:
            score(lax.rem(z + distance, nz))

    w0 = r.start[0] + z * slab_plane
    r0 = w0 + ((q - w0) & (np_ - 1))
    k0 = r0 >> log_np
    first = w0 + me.prow * slab_tile
    second_half = jnp.where(me.prow >= pr // 2, 1, 0)

    def make_w2():
        loads["op"].wait()
        wait_bytes(r.ppg, np_ - 1, r.recv_sem.at[0])
        total = jnp.zeros((E, wz), F32)
        for chunk in range(np_):
            at = ((fd * chunk) >> 7) << 7
            total = total + nt(r.op[:, at : at + W], r.ppg[chunk])
        row, column = grid_of(wz, wz)
        turned = nt(one_hot(row == column), total.astype(BF)).astype(BF)
        r.w2msg[...] = turned
        r.w2g[z] = turned
        me.to_column(lambda peer: r.w2msg, r.w2g, r.send_sem.at[1], r.recv_sem.at[1])

    def make_picks():
        row, column = grid_of(pc * 16, 8 * nz)
        sub = row & 15
        right_hit = (sub < 8) & (column == (2 * (row >> 4) + (sub >> 2)) * 8 + 4 + (sub & 3))
        kk = k0 + (sub - 8)
        left_hit = ((sub == 8) | (sub == 9)) & (column == (kk >> 2) * 8 + (kk & 3))
        r.pick[...] = one_hot(right_hit | left_hit)
        row, column = grid_of(columns + slab_tile, 16 * np_)
        right_hit = (row < columns) & (column == (row & (np_ - 1)) * 16 + (row >> log_np))
        left_hit = (row >= columns) & (
            column == ((first + row - columns) & (np_ - 1)) * 16 + 8 + second_half
        )
        r.place_rows[...] = one_hot(right_hit | left_hit)
        row, column = grid_of(16 * np_, columns + slab_tile)
        sub = row & 15
        owner = row >> 4
        right_hit = (sub < 8) & (column == sub * np_ + owner)
        left_hit = (
            (sub == 8 + second_half)
            & (column >= columns)
            & (((first + column - columns) & (np_ - 1)) == owner)
        )
        r.spread_rows[...] = one_hot(right_hit | left_hit)

    def make_pair_constants():
        for name in ("chain", "bias", "gain", "w_in", "w_out", "mask_flat", "chain_flat"):
            loads[name].wait()
        r.w_half[...] = (r.w_in[...].astype(F32) * 0.5).astype(BF)
        r.w_out_half[...] = (r.w_out[...].astype(F32) * 0.5).astype(BF)
        row, column = grid_of(2 * E, 2 * E)
        r.means[...] = jnp.where((row >> 7) == (column >> 7), 1.0 / E, 0.0).astype(BF)
        r.bias_mean[...] = jnp.broadcast_to(jnp.mean(r.bias[...], axis=1, keepdims=True), (2, E))
        row, column = grid_of(rb, rb)
        unit = one_hot(row == column)
        for half in range(2):
            at = pl.ds(2 * me.pcol + half, 1)
            to = pl.ds(half * rb, rb)
            for source, target in ((r.mask, r.live_column), (r.chain, r.chain_column)):
                lanes = jnp.broadcast_to(source[at, :].astype(F32), (E, rb)).astype(BF)
                target[to, :] = nt(unit, lanes)

    for distance in range(2, nz // 2 + 1, 2):
        for chain in range(4):
            arrive(chain, distance)
        if distance == 2:
            make_w2()
        if distance == 4 or nz // 2 < 4:
            make_picks()
        if distance == 6 or nz // 2 < 6:
            make_pair_constants()
        if distance < nz // 2:
            for near in (distance - 1, distance):
                for chain in range(2):
                    if near % 2:
                        arrive(chain, near)
                score_at(near)
    last = nz // 2
    for chain in range(2):
        arrive(chain, last - 1)
    score_at(last - 1)
    score_at(last)

    top = r.scores[0]
    for b in range(1, nz):
        top = jnp.maximum(top, r.scores[b])
    top = jnp.max(top, axis=1, keepdims=True)
    for distance in range(1, last + 1, 2):
        for chain in (2, 3):
            arrive(chain, distance)
    below = jnp.zeros((rb, rb), F32)
    above = jnp.zeros((rb, E), F32)
    for b in range(0, nz, 2):
        shifted = [jnp.exp(r.scores[b + i] - top) for i in range(2)]
        below = below + shifted[0] + shifted[1]
        weights = jnp.concatenate(shifted, axis=1).astype(BF)
        above = above + nn(weights, r.v[pl.ds(b, 2)].reshape(2 * rb, E))
    attended = (above / jnp.sum(below, axis=1, keepdims=True)).astype(BF)

    twice = nn(r.perm[...], attended).astype(BF)
    wait_bytes(r.w2g, nz - 1, r.recv_sem.at[1])
    both = nt(twice, r.w2g[...].reshape(W, E))
    terms = jnp.where(is_left, both[:, :E], both[:, E:]) + r.presidual[...]
    r.pmsg[...] = terms.reshape(np_, 8, E)
    me.to_plane(lambda peer: r.pmsg.at[peer], r.pbuf, r.send_sem.at[2], r.recv_sem.at[2])
    r.pbuf[q] = r.pmsg[q]
    wait_bytes(r.pbuf, np_ - 1, r.recv_sem.at[2])
    projected = jnp.sum(r.pbuf[...], axis=0).astype(BF).astype(F32)
    r.tmsg[...] = projected
    r.zbuf[z] = projected
    me.to_column(lambda peer: r.tmsg, r.zbuf, r.send_sem.at[3], r.recv_sem.at[3])
    wait_bytes(r.zbuf, nz - 1, r.recv_sem.at[3])
    chosen = nn(r.pick[...], r.zbuf[...].reshape(8 * nz, E).astype(BF)).astype(BF)
    r.msg[...] = chosen.reshape(pc, 16, E)
    me.to_plane(
        lambda peer: r.msg.at[lax.rem(peer, pc)], r.rbuf, r.send_sem.at[4], r.recv_sem.at[4]
    )
    r.rbuf[q] = r.msg[me.pcol]
    loads["cot"].wait()
    wait_bytes(r.rbuf, np_ - 1, r.recv_sem.at[4])
    r.ab[...] = nn(r.place_rows[...], r.rbuf[...].reshape(16 * np_, E))

    r.right_live[...] = r.ab[pl.ds(0, columns), :] * r.live_column[...]
    r.grads[...] = jnp.zeros_like(r.grads)
    per = min(PER, slab_tile)

    def store(i):
        part = pl.ds(i * per, per)
        return pltpu.make_async_copy(r.out.at[part], r.out_hbm.at[part], r.store_sem)

    def pair_step(i, carry):
        pair_rows(r, i, per, columns, first)
        store(i).start()
        return carry

    lax.fori_loop(0, slab_tile // per, pair_step, 0)

    r.grads[pl.ds(0, columns), :] = r.grads[pl.ds(0, columns), :] * r.live_column[...]
    gathered = nn(r.spread_rows[...], r.grads[...].astype(BF)).astype(BF)
    r.gmsg[...] = gathered.reshape(np_, 16, E)
    me.to_plane(lambda peer: r.gmsg.at[peer], r.gbuf, r.send_sem.at[5], r.recv_sem.at[5])
    r.gbuf[q] = r.gmsg[q]
    wait_bytes(r.gbuf, np_ - 1, r.recv_sem.at[5])
    by_column = jnp.sum(r.gbuf[...].astype(F32).reshape(pr, pc, 16, E), axis=0)
    over_columns = jnp.sum(by_column, axis=0)
    left0 = over_columns[8:9, :]
    left1 = over_columns[9:10, :]
    sub, _ = grid_of(8, E)
    for other in range(nz):
        k = 4 * other + (sub & 3)
        lefts = jnp.where(k == k0, left0, jnp.where(k == k0 + 1, left1, 0.0))
        r.zmsg[other] = jnp.where((sub >> 2) == other % 2, by_column[other // 2, 0:8, :], lefts)
    me.to_column(lambda peer: r.zmsg.at[peer], r.hbuf, r.send_sem.at[6], r.recv_sem.at[6])
    r.hbuf[z] = r.zmsg[z]
    wait_bytes(r.hbuf, nz - 1, r.recv_sem.at[6])
    tile = jnp.sum(r.hbuf[...], axis=0).astype(BF).astype(F32)
    r.fmsg[...] = tile
    r.fbuf[q] = tile
    me.to_plane(lambda peer: r.fmsg, r.fbuf, r.send_sem.at[7], r.recv_sem.at[7])
    odd = z & 1
    row, column = grid_of(rb, 8 * np_)
    base = (row & (np_ - 1)) * 8 + (row >> log_np)
    left_pick = one_hot(column == base + 4 * (1 - odd))
    right_pick = one_hot(column == base + 4 * odd)
    for chain in range(4):
        for distance in range(1, furthest[chain % 2] + 1):
            ring(chain, distance, 1 if distance % 2 else 2).wait_send()
    wait_bytes(r.ppg, np_ - 1, r.send_sem.at[0])
    wait_bytes(r.w2g, nz - 1, r.send_sem.at[1])
    wait_bytes(r.pbuf, np_ - 1, r.send_sem.at[2])
    wait_bytes(r.zbuf, nz - 1, r.send_sem.at[3])
    wait_bytes(r.rbuf, np_ - 1, r.send_sem.at[4])
    wait_bytes(r.gbuf, np_ - 1, r.send_sem.at[5])
    wait_bytes(r.hbuf, nz - 1, r.send_sem.at[6])
    pltpu.make_async_copy(r.out, r.out_hbm, r.store_sem).wait()
    wait_bytes(r.fbuf, np_ - 1, r.recv_sem.at[7])
    tiles = r.fbuf[...].reshape(8 * np_, E).astype(BF)
    left = nn(left_pick, tiles).astype(BF)
    right = nn(right_pick, tiles).astype(BF)
    r.lm[...] = (nt(r.pp[:, :E], left) + nt(r.pp[:, E:], right)).astype(BF)
    wait_bytes(r.fbuf, np_ - 1, r.send_sem.at[7])


PER = 8


def fused(sizes, start, operands):
    nz, pr, pc = sizes
    np_ = pr * pc
    q, k, v, res, op, pp, bias, gain, w_in, w_out, cot, mask, chain, mask_flat, chain_flat = operands
    rb = q.shape[0]
    columns = 8 * np_
    tile = 2 * np_ // pr
    wz = W // nz
    vmem, dma = pltpu.VMEM, pltpu.SemaphoreType.DMA
    steps = max(1, nz // 2)
    scratch = {
        "q": vmem(q.shape, BF),
        "k": vmem((nz, rb, E), BF),
        "v": vmem((nz, rb, E), BF),
        "res": vmem(res.shape, BF),
        "op": vmem(op.shape, BF),
        "pp": vmem(pp.shape, BF),
        "bias": vmem(bias.shape, F32),
        "gain": vmem(gain.shape, F32),
        "w_in": vmem(w_in.shape, BF),
        "w_out": vmem(w_out.shape, BF),
        "cot": vmem(cot.shape, BF),
        "mask": vmem(mask.shape, jnp.int32),
        "chain": vmem(chain.shape, jnp.int32),
        "mask_flat": pltpu.SMEM(mask_flat.shape, jnp.int32),
        "chain_flat": pltpu.SMEM(chain_flat.shape, jnp.int32),
        "scores": vmem((nz, rb, rb), F32),
        "perm": vmem((8 * np_, rb), BF),
        "pick": vmem((pc * 16, 8 * nz), BF),
        "place_rows": vmem((columns + tile, 16 * np_), BF),
        "spread_rows": vmem((16 * np_, columns + tile), BF),
        "presidual": vmem((8 * np_, E), F32),
        "ppmsg": vmem((wz, W), BF),
        "ppg": vmem((np_, wz, W), BF),
        "w2msg": vmem((wz, E), BF),
        "w2g": vmem((nz, wz, E), BF),
        "pmsg": vmem((np_, 8, E), F32),
        "pbuf": vmem((np_, 8, E), F32),
        "tmsg": vmem((8, E), F32),
        "zbuf": vmem((nz, 8, E), F32),
        "msg": vmem((pc, 16, E), BF),
        "rbuf": vmem((np_, 16, E), BF),
        "ab": vmem((columns + tile, E), F32),
        "w_half": vmem(w_in.shape, BF),
        "w_out_half": vmem(w_out.shape, BF),
        "means": vmem((2 * E, 2 * E), BF),
        "bias_mean": vmem((2, E), F32),
        "live_column": vmem((columns, E), F32),
        "chain_column": vmem((columns, E), F32),
        "right_live": vmem((columns, E), F32),
        "out": vmem(cot.shape, BF),
        "grads": vmem((columns + tile, E), F32),
        "gmsg": vmem((np_, 16, E), BF),
        "gbuf": vmem((np_, 16, E), BF),
        "zmsg": vmem((nz, 8, E), F32),
        "hbuf": vmem((nz, 8, E), F32),
        "fmsg": vmem((8, E), F32),
        "fbuf": vmem((np_, 8, E), F32),
        "load_sem": dma((len(LOADS),)),
        "store_sem": dma,
        "ring_send": dma((4, steps)),
        "ring_recv": dma((4, steps)),
        "send_sem": dma((8,)),
        "recv_sem": dma((8,)),
    }
    hbm = pl.BlockSpec(memory_space=pltpu.HBM)
    return pl.pallas_call(
        functools.partial(kernel, sizes, INPUTS + ("out_hbm", "lm") + tuple(scratch)),
        out_shape=(
            jax.ShapeDtypeStruct(cot.shape, BF),
            jax.ShapeDtypeStruct((pp.shape[0], rb), BF),
        ),
        in_specs=[pl.BlockSpec(memory_space=pltpu.SMEM)] + [hbm] * len(operands),
        out_specs=(hbm, pl.BlockSpec(memory_space=pltpu.VMEM)),
        scratch_shapes=list(scratch.values()),
        compiler_params=pltpu.CompilerParams(
            collective_id=0, has_side_effects=True, vmem_limit_bytes=56 << 20
        ),
        name="attend_pair_and_gradient",
    )(start, *operands)


def body(
    sizes,
    queries,
    keys,
    values,
    residual,
    out_proj,
    pair_proj,
    chain_bias,
    ln_gain,
    w_in,
    w_out,
    pair_cot,
    residue_mask,
    chain_ids,
    slab_start,
):
    nz, rb = sizes[0], queries.shape[0]
    operands = (
        queries,
        keys,
        values,
        residual.T,
        out_proj,
        pair_proj,
        chain_bias,
        ln_gain.reshape(1, E),
        w_in,
        w_out,
        pair_cot,
        residue_mask.reshape(nz, rb),
        chain_ids.reshape(nz, rb),
        residue_mask,
        chain_ids,
    )
    pair_out, lm_grad = fused(sizes, slab_start, operands)
    return pair_out, lm_grad.T


def solution(mesh):
    sizes = tuple(mesh.shape[name] for name in ("lm", "prow", "pcol"))
    return jax.shard_map(
        functools.partial(body, sizes),
        mesh=mesh,
        in_specs=(
            P("lm", ("prow", "pcol")),
            P("lm", ("prow", "pcol")),
            P("lm", ("prow", "pcol")),
            P("lm", ("prow", "pcol")),
            P(("prow", "pcol"), None),
            P(("prow", "pcol"), None),
            P(),
            P(),
            P(),
            P(),
            P(("lm", "prow"), "pcol", None),
            P(),
            P(),
            P(),
        ),
        out_specs=(P(("lm", "prow"), "pcol", None), P("lm", ("prow", "pcol"))),
        check_vma=False,
    )
```

```python
import functools
import math

import jax
import jax.numpy as jnp
from jax import lax
from jax.experimental import pallas as pl
from jax.experimental.pallas import tpu as pltpu
from jax.sharding import PartitionSpec as P

BF = jnp.bfloat16
F32 = jnp.float32
MESH = pl.DeviceIdType.MESH
E = 128
W = 256


def nn(a, b):
    return lax.dot_general(a, b, (((1,), (0,)), ((), ())), preferred_element_type=F32)


def nt(a, b):
    return lax.dot_general(a, b, (((1,), (1,)), ((), ())), preferred_element_type=F32)


def grid_of(rows, columns):
    row = lax.broadcasted_iota(jnp.int32, (rows, columns), 0)
    column = lax.broadcasted_iota(jnp.int32, (rows, columns), 1)
    return row, column


def one_hot(hit):
    return jnp.where(hit, 1.0, 0.0).astype(BF)


def bits(n):
    return n.bit_length() - 1


def plane_order(pr, pc):
    offsets = list(range(1, pr * pc))
    if (pr, pc) != (4, 8):
        return offsets
    ring = (0, 1, 2, 1)

    def hops(m):
        return ring[(m >> 1) & 3] + ring[((m & 1) << 1) | (m >> 4)]

    return sorted(offsets, key=lambda m: -hops(m))


def z_order(nz):
    return sorted(range(1, nz), key=lambda i: -min(i, nz - i))


class Place:
    def __init__(self, sizes):
        self.nz, self.pr, self.pc = sizes
        self.np = self.pr * self.pc
        self.z = lax.axis_index("lm")
        self.prow = lax.axis_index("prow")
        self.pcol = lax.axis_index("pcol")
        self.q = self.prow * self.pc + self.pcol

    def plane_peer(self, m):
        prow = lax.bitwise_xor(self.prow, m // self.pc)
        pcol = lax.bitwise_xor(self.pcol, m % self.pc)
        return lax.bitwise_xor(self.q, m), (self.z, prow, pcol)

    def z_peer(self, i):
        peer = lax.rem(self.z + i, self.nz)
        return peer, (peer, self.prow, self.pcol)

    def peers(self):
        for i in z_order(self.nz):
            yield self.z_peer(i)[1]
        for m in plane_order(self.pr, self.pc):
            yield self.plane_peer(m)[1]

    def signal_all(self, barrier):
        for device in self.peers():
            pl.semaphore_signal(barrier, inc=1, device_id=device, device_id_type=MESH)

    def wait_all(self, barrier):
        pl.semaphore_wait(barrier, self.np + self.nz - 2)

    def send(self, source, target, send_sem, recv_sem, device):
        pltpu.make_async_remote_copy(
            src_ref=source,
            dst_ref=target,
            send_sem=send_sem,
            recv_sem=recv_sem,
            device_id=device,
            device_id_type=MESH,
        ).start()

    def to_plane(self, source, target, send_sem, recv_sem):
        for m in plane_order(self.pr, self.pc):
            peer, device = self.plane_peer(m)
            self.send(source(peer), target.at[self.q], send_sem, recv_sem, device)

    def to_column(self, source, target, send_sem, recv_sem):
        for i in z_order(self.nz):
            peer, device = self.z_peer(i)
            self.send(source(peer), target.at[self.z], send_sem, recv_sem, device)


def wait_bytes(buffer, count, sem):
    part = buffer.at[pl.ds(0, count)]
    pltpu.make_async_copy(part, part, sem).wait()


class Refs:
    def __init__(self, names, refs):
        for name, ref in zip(names, refs, strict=True):
            setattr(self, name, ref)


INPUTS = (
    "start",
    "q_hbm",
    "k_hbm",
    "v_hbm",
    "res_hbm",
    "op_hbm",
    "pp_hbm",
    "bias_hbm",
    "gain_hbm",
    "w_in_hbm",
    "w_out_hbm",
    "cot_hbm",
    "mask_hbm",
    "chain_hbm",
    "mask_flat_hbm",
    "chain_flat_hbm",
)
LOADS = (
    "k",
    "v",
    "pp",
    "q",
    "mask",
    "res",
    "chain",
    "bias",
    "gain",
    "w_in",
    "w_out",
    "op",
    "cot",
    "mask_flat",
    "chain_flat",
)


class PairGroup:
    def __init__(self, r, rows, columns, first):
        self.r, self.rows, self.columns, self.first = r, rows, columns, first

    def norm_and_hidden(self):
        r, rows, columns = self.r, self.rows, self.columns
        gain = r.gain[...]
        self.lefts = [r.ab[pl.ds(columns + t, 1), :] for t in rows]
        right = r.ab[pl.ds(0, columns), :]
        spread = jnp.concatenate([jnp.broadcast_to(left, (E, E)) for left in self.lefts], axis=0)
        dots = nt(right.astype(BF), spread.astype(BF)) * (1.0 / E)
        self.seeds, centres = [], []
        for j, t in enumerate(rows):
            same = r.chain_column[...] == r.chain_flat[self.first + t].astype(F32)
            seed = self.lefts[j] * right + jnp.where(same, r.bias[1:2, :], r.bias[0:1, :])
            mean = dots[:, j * E : (j + 1) * E] + jnp.where(
                same, r.bias_mean[1:2, :], r.bias_mean[0:1, :]
            )
            self.seeds.append(seed)
            centres.append(seed - mean)
        self.inverses = []
        for j in range(0, len(rows), 2):
            squares = jnp.concatenate([c * c for c in centres[j : j + 2]], axis=1).astype(BF)
            inverse = lax.rsqrt(nn(squares, r.means[...]) + 1e-05)
            self.inverses += [inverse[:, :E], inverse[:, E:]]
        self.normeds = [c * inverse for c, inverse in zip(centres, self.inverses)]
        scaled = jnp.concatenate([(n * gain).astype(BF) for n in self.normeds], axis=0)
        self.half = nn(scaled, r.w_half[...])

    def activate(self):
        r = self.r
        d_act = jnp.concatenate([r.d_act[t] for t in self.rows], axis=0)
        turned = jnp.tanh(self.half)
        raised = 1.0 + turned
        act = self.half * raised
        d_hidden = (d_act * (raised + act * (1.0 - turned))).astype(BF)
        self.y = nn(act.astype(BF), r.w_out[...])
        self.d_scaled = nt(d_hidden, r.w_in[...])

    def finish(self, total):
        r, columns = self.r, self.columns
        gain = r.gain[...]
        for j, t in enumerate(self.rows):
            live = r.mask_flat[self.first + t].astype(F32)
            block = slice(j * columns, (j + 1) * columns)
            r.out[t] = ((self.seeds[j] + self.y[block]) * (r.live_column[...] * live)).astype(BF)
            d_normed = self.d_scaled[block] * gain
            both = jnp.concatenate([d_normed, d_normed * self.normeds[j]], axis=1).astype(BF)
            both = nn(both, r.means[...])
            d_seed = r.cot[t].astype(F32) + self.inverses[j] * (
                d_normed - both[:, :E] - self.normeds[j] * both[:, E:]
            )
            total = total + d_seed * (self.lefts[j] * live)
            r.grads[pl.ds(columns + t, 1), :] = live * jnp.sum(
                d_seed * r.right_live[...], axis=0, keepdims=True
            )
        return total


def pair_tile(r, tile, columns, first, done):
    per = min(4, tile)
    groups = [
        PairGroup(r, range(at, at + per), columns, first) for at in range(0, tile, per)
    ]
    total = jnp.zeros((columns, E), F32)
    for i in range(len(groups) + 2):
        if i < len(groups):
            groups[i].norm_and_hidden()
        if 0 <= i - 1 < len(groups):
            groups[i - 1].activate()
        if i >= 2:
            total = groups[i - 2].finish(total)
            done((i - 2) * per, per)
    return total


def kernel(sizes, names, *refs):
    r = Refs(names, refs)
    me = Place(sizes)
    nz, pr, pc, np_ = me.nz, me.pr, me.pc, me.np
    z, q = me.z, me.q
    rb = r.q.shape[0]
    fd = r.pp.shape[0]
    wz = W // nz
    columns = 8 * np_
    slab_plane = 2 * np_
    slab_tile = slab_plane // pr
    log_np = bits(np_)

    barrier = pltpu.get_barrier_semaphore()
    loads = {}
    for i, name in enumerate(LOADS):
        target = getattr(r, name)
        if name in ("k", "v"):
            target = target.at[z]
        loads[name] = pltpu.make_async_copy(getattr(r, name + "_hbm"), target, r.load_sem.at[i])
        loads[name].start()
    me.signal_all(barrier)

    loads["pp"].wait()
    row, column = grid_of(wz, W)
    piece = nt(one_hot(column == row + z * wz), r.pp[...]).astype(BF)
    row, column = grid_of(fd, W)
    piece = nn(piece, one_hot(column == row + ((fd * q) & 127))).astype(BF)
    r.ppmsg[...] = piece
    r.ppg[q] = piece
    loads["k"].wait()
    loads["v"].wait()
    me.wait_all(barrier)

    furthest = (nz // 2, nz - 1 - nz // 2)

    def ring(chain, distance, hop):
        buf = r.k if chain < 2 else r.v
        way = 1 if chain % 2 == 0 else -1
        block = lax.rem(z - way * (distance - hop) + nz, nz)
        peer = lax.rem(z + way * hop + nz, nz)
        return pltpu.make_async_remote_copy(
            src_ref=buf.at[block],
            dst_ref=buf.at[block],
            send_sem=r.ring_send.at[chain, distance - 1],
            recv_sem=r.ring_recv.at[chain, distance - 1],
            device_id=(peer, me.prow, me.pcol),
            device_id_type=MESH,
        )

    def pass_on(chain, held):
        for hop in (2, 1):
            if held + hop <= furthest[chain % 2]:
                ring(chain, held + hop, hop).start()

    for chain in range(4):
        pass_on(chain, 0)
    me.to_plane(lambda peer: r.ppmsg, r.ppg, r.send_sem.at[0], r.recv_sem.at[0])

    row, column = grid_of(8 * np_, rb)
    r.perm[...] = one_hot(column == (row & 3) * np_ + (row >> 3))
    loads["res"].wait()
    rows_twice = nt(r.perm[...], r.res[...]).astype(BF)
    both = nn(rows_twice, r.pp[...])
    row, column = grid_of(8 * np_, E)
    is_left = (row & 7) < 4
    r.presidual[...] = jnp.where(is_left, both[:, :E], both[:, E:])
    loads["q"].wait()
    loads["mask"].wait()

    scale = 1.0 / math.sqrt(E)

    def score(block):
        raw = nt(r.q[...], r.k[block]) * scale
        live = r.mask[pl.ds(block, 1), :]
        r.scores[block] = jnp.where(live > 0, raw, -1e30)

    score(z)

    def arrive(chain, distance):
        if distance <= furthest[chain % 2]:
            ring(chain, distance, 1 if distance % 2 else 2).wait_recv()
            if distance % 2 == 0:
                pass_on(chain, distance)

    def score_at(distance):
        if distance <= furthest[0]:
            score(lax.rem(z - distance + nz, nz))
        if distance <= furthest[1]:
            score(lax.rem(z + distance, nz))

    w0 = r.start[0] + z * slab_plane
    r0 = w0 + ((q - w0) & (np_ - 1))
    k0 = r0 >> log_np
    first = w0 + me.prow * slab_tile
    second_half = jnp.where(me.prow >= pr // 2, 1, 0)

    def make_w2():
        loads["op"].wait()
        wait_bytes(r.ppg, np_ - 1, r.recv_sem.at[0])
        total = jnp.zeros((E, wz), F32)
        for chunk in range(np_):
            at = ((fd * chunk) >> 7) << 7
            total = total + nt(r.op[:, at : at + W], r.ppg[chunk])
        row, column = grid_of(wz, wz)
        turned = nt(one_hot(row == column), total.astype(BF)).astype(BF)
        r.w2msg[...] = turned
        r.w2g[z] = turned
        me.to_column(lambda peer: r.w2msg, r.w2g, r.send_sem.at[1], r.recv_sem.at[1])

    def make_picks():
        row, column = grid_of(pc * 16, 8 * nz)
        sub = row & 15
        right_hit = (sub < 8) & (column == (2 * (row >> 4) + (sub >> 2)) * 8 + 4 + (sub & 3))
        kk = k0 + (sub - 8)
        left_hit = ((sub == 8) | (sub == 9)) & (column == (kk >> 2) * 8 + (kk & 3))
        r.pick[...] = one_hot(right_hit | left_hit)
        row, column = grid_of(columns + slab_tile, 16 * np_)
        right_hit = (row < columns) & (column == (row & (np_ - 1)) * 16 + (row >> log_np))
        left_hit = (row >= columns) & (
            column == ((first + row - columns) & (np_ - 1)) * 16 + 8 + second_half
        )
        r.place_rows[...] = one_hot(right_hit | left_hit)
        row, column = grid_of(16 * np_, columns + slab_tile)
        sub = row & 15
        owner = row >> 4
        right_hit = (sub < 8) & (column == sub * np_ + owner)
        left_hit = (
            (sub == 8 + second_half)
            & (column >= columns)
            & (((first + column - columns) & (np_ - 1)) == owner)
        )
        r.spread_rows[...] = one_hot(right_hit | left_hit)

    def make_pair_constants():
        for name in ("chain", "bias", "gain", "w_in", "w_out", "mask_flat", "chain_flat"):
            loads[name].wait()
        r.w_half[...] = (r.w_in[...].astype(F32) * 0.5).astype(BF)
        r.w_out_half[...] = (r.w_out[...].astype(F32) * 0.5).astype(BF)
        row, column = grid_of(2 * E, 2 * E)
        r.means[...] = jnp.where((row >> 7) == (column >> 7), 1.0 / E, 0.0).astype(BF)
        r.bias_mean[...] = jnp.broadcast_to(jnp.mean(r.bias[...], axis=1, keepdims=True), (2, E))
        row, column = grid_of(rb, rb)
        unit = one_hot(row == column)
        for half in range(2):
            at = pl.ds(2 * me.pcol + half, 1)
            to = pl.ds(half * rb, rb)
            for source, target in ((r.mask, r.live_column), (r.chain, r.chain_column)):
                lanes = jnp.broadcast_to(source[at, :].astype(F32), (E, rb)).astype(BF)
                target[to, :] = nt(unit, lanes)

    def make_d_act(first_row, end_row):
        for t in range(first_row, end_row):
            r.d_act[t] = nt(r.cot[t], r.w_out_half[...]).astype(r.d_act.dtype)

    last = nz // 2
    third = max(1, slab_tile // 4)
    chores = {
        0: (make_pair_constants, make_picks),
        2: (lambda: loads["cot"].wait(), lambda: make_d_act(0, third)),
        4: (make_w2,),
        6: (lambda: make_d_act(third, slab_tile),),
    }
    for chore in chores[0]:
        chore()
    for distance in range(2, last, 2):
        for chain in range(4):
            arrive(chain, distance)
        for chore in chores.pop(distance, ()):
            chore()
        for near in (distance - 1, distance):
            if near % 2:
                for chain in range(2):
                    arrive(chain, near)
            score_at(near)
    for stage in (2, 4, 6):
        for chore in chores.pop(stage, ()):
            chore()
    for chain in (0, 1):
        arrive(chain, last)
        arrive(chain, last - 1)
    score_at(last - 1)
    score_at(last)

    top = r.scores[0]
    for b in range(1, nz):
        top = jnp.maximum(top, r.scores[b])
    top = jnp.max(top, axis=1, keepdims=True)
    below = jnp.zeros((rb, rb), F32)
    above = jnp.zeros((rb, E), F32)
    for distance in range(1, last + 1):
        if distance % 2 or distance == last:
            for chain in (2, 3):
                arrive(chain, distance)
        left = lax.rem(z - distance + nz, nz)
        right = lax.rem(z + (distance if distance < last else 0), nz)
        shifted = [jnp.exp(r.scores[b] - top) for b in (left, right)]
        below = below + shifted[0] + shifted[1]
        weights = jnp.concatenate(shifted, axis=1).astype(BF)
        above = above + nn(weights, jnp.concatenate([r.v[left], r.v[right]], axis=0))
    attended = (above / jnp.sum(below, axis=1, keepdims=True)).astype(BF)

    twice = nn(r.perm[...], attended).astype(BF)
    wait_bytes(r.w2g, nz - 1, r.recv_sem.at[1])
    both = nt(twice, r.w2g[...].reshape(W, E))
    terms = jnp.where(is_left, both[:, :E], both[:, E:]) + r.presidual[...]
    r.pmsg[...] = terms.reshape(np_, 8, E)
    me.to_plane(lambda peer: r.pmsg.at[peer], r.pbuf, r.send_sem.at[2], r.recv_sem.at[2])
    r.pbuf[q] = r.pmsg[q]
    wait_bytes(r.pbuf, np_ - 1, r.recv_sem.at[2])
    projected = jnp.sum(r.pbuf[...], axis=0).astype(BF).astype(F32)
    r.tmsg[...] = projected
    r.zbuf[z] = projected
    me.to_column(lambda peer: r.tmsg, r.zbuf, r.send_sem.at[3], r.recv_sem.at[3])
    wait_bytes(r.zbuf, nz - 1, r.recv_sem.at[3])
    chosen = nn(r.pick[...], r.zbuf[...].reshape(8 * nz, E).astype(BF)).astype(BF)
    r.msg[...] = chosen.reshape(pc, 16, E)
    me.to_plane(
        lambda peer: r.msg.at[lax.rem(peer, pc)], r.rbuf, r.send_sem.at[4], r.recv_sem.at[4]
    )
    r.rbuf[q] = r.msg[me.pcol]
    wait_bytes(r.rbuf, np_ - 1, r.recv_sem.at[4])
    r.ab[...] = nn(r.place_rows[...], r.rbuf[...].reshape(16 * np_, E))

    r.right_live[...] = r.ab[pl.ds(0, columns), :] * r.live_column[...]

    def store(at, count):
        part = pl.ds(at, count)
        pltpu.make_async_copy(r.out.at[part], r.out_hbm.at[part], r.store_sem).start()

    total = pair_tile(r, slab_tile, columns, first, store)
    r.grads[pl.ds(0, columns), :] = total * r.live_column[...]
    gathered = nn(r.spread_rows[...], r.grads[...].astype(BF)).astype(BF)
    r.gmsg[...] = gathered.reshape(np_, 16, E)
    me.to_plane(lambda peer: r.gmsg.at[peer], r.gbuf, r.send_sem.at[5], r.recv_sem.at[5])
    r.gbuf[q] = r.gmsg[q]
    wait_bytes(r.gbuf, np_ - 1, r.recv_sem.at[5])
    by_column = jnp.sum(r.gbuf[...].astype(F32).reshape(pr, pc, 16, E), axis=0)
    over_columns = jnp.sum(by_column, axis=0)
    left0 = over_columns[8:9, :]
    left1 = over_columns[9:10, :]
    sub, _ = grid_of(8, E)
    for other in range(nz):
        k = 4 * other + (sub & 3)
        lefts = jnp.where(k == k0, left0, jnp.where(k == k0 + 1, left1, 0.0))
        r.zmsg[other] = jnp.where((sub >> 2) == other % 2, by_column[other // 2, 0:8, :], lefts)
    me.to_column(lambda peer: r.zmsg.at[peer], r.hbuf, r.send_sem.at[6], r.recv_sem.at[6])
    r.hbuf[z] = r.zmsg[z]
    wait_bytes(r.hbuf, nz - 1, r.recv_sem.at[6])
    tile = jnp.sum(r.hbuf[...], axis=0).astype(BF).astype(F32)
    r.fmsg[...] = tile
    r.fbuf[q] = tile
    me.to_plane(lambda peer: r.fmsg, r.fbuf, r.send_sem.at[7], r.recv_sem.at[7])
    odd = z & 1
    row, column = grid_of(rb, 8 * np_)
    base = (row & (np_ - 1)) * 8 + (row >> log_np)
    left_pick = one_hot(column == base + 4 * (1 - odd))
    right_pick = one_hot(column == base + 4 * odd)
    for chain in range(4):
        for distance in range(1, furthest[chain % 2] + 1):
            ring(chain, distance, 1 if distance % 2 else 2).wait_send()
    wait_bytes(r.ppg, np_ - 1, r.send_sem.at[0])
    wait_bytes(r.w2g, nz - 1, r.send_sem.at[1])
    wait_bytes(r.pbuf, np_ - 1, r.send_sem.at[2])
    wait_bytes(r.zbuf, nz - 1, r.send_sem.at[3])
    wait_bytes(r.rbuf, np_ - 1, r.send_sem.at[4])
    wait_bytes(r.gbuf, np_ - 1, r.send_sem.at[5])
    wait_bytes(r.hbuf, nz - 1, r.send_sem.at[6])
    wait_bytes(r.fbuf, np_ - 1, r.recv_sem.at[7])
    tiles = r.fbuf[...].reshape(8 * np_, E).astype(BF)
    pltpu.make_async_copy(r.out, r.out_hbm, r.store_sem).wait()
    left = nn(left_pick, tiles).astype(BF)
    right = nn(right_pick, tiles).astype(BF)
    r.lm[...] = (nt(r.pp[:, :E], left) + nt(r.pp[:, E:], right)).astype(BF)
    wait_bytes(r.fbuf, np_ - 1, r.send_sem.at[7])


D_ACT = F32


def fused(sizes, start, operands):
    nz, pr, pc = sizes
    np_ = pr * pc
    q, k, v, res, op, pp, bias, gain, w_in, w_out, cot, mask, chain, mask_flat, chain_flat = operands
    rb = q.shape[0]
    columns = 8 * np_
    tile = 2 * np_ // pr
    wz = W // nz
    vmem, dma = pltpu.VMEM, pltpu.SemaphoreType.DMA
    steps = max(1, nz // 2)
    scratch = {
        "q": vmem(q.shape, BF),
        "k": vmem((nz, rb, E), BF),
        "v": vmem((nz, rb, E), BF),
        "res": vmem(res.shape, BF),
        "op": vmem(op.shape, BF),
        "pp": vmem(pp.shape, BF),
        "bias": vmem(bias.shape, F32),
        "gain": vmem(gain.shape, F32),
        "w_in": vmem(w_in.shape, BF),
        "w_out": vmem(w_out.shape, BF),
        "cot": vmem(cot.shape, BF),
        "mask": vmem(mask.shape, jnp.int32),
        "chain": vmem(chain.shape, jnp.int32),
        "mask_flat": pltpu.SMEM(mask_flat.shape, jnp.int32),
        "chain_flat": pltpu.SMEM(chain_flat.shape, jnp.int32),
        "scores": vmem((nz, rb, rb), F32),
        "perm": vmem((8 * np_, rb), BF),
        "pick": vmem((pc * 16, 8 * nz), BF),
        "place_rows": vmem((columns + tile, 16 * np_), BF),
        "spread_rows": vmem((16 * np_, columns + tile), BF),
        "presidual": vmem((8 * np_, E), F32),
        "ppmsg": vmem((wz, W), BF),
        "ppg": vmem((np_, wz, W), BF),
        "w2msg": vmem((wz, E), BF),
        "w2g": vmem((nz, wz, E), BF),
        "pmsg": vmem((np_, 8, E), F32),
        "pbuf": vmem((np_, 8, E), F32),
        "tmsg": vmem((8, E), F32),
        "zbuf": vmem((nz, 8, E), F32),
        "msg": vmem((pc, 16, E), BF),
        "rbuf": vmem((np_, 16, E), BF),
        "ab": vmem((columns + tile, E), F32),
        "out": vmem(cot.shape, BF),
        "store_sem": dma,
        "w_half": vmem(w_in.shape, BF),
        "w_out_half": vmem(w_out.shape, BF),
        "means": vmem((2 * E, 2 * E), BF),
        "bias_mean": vmem((2, E), F32),
        "live_column": vmem((columns, E), F32),
        "chain_column": vmem((columns, E), F32),
        "right_live": vmem((columns, E), F32),
        "d_act": vmem(cot.shape[:2] + w_in.shape[1:], D_ACT),
        "grads": vmem((columns + tile, E), F32),
        "gmsg": vmem((np_, 16, E), BF),
        "gbuf": vmem((np_, 16, E), BF),
        "zmsg": vmem((nz, 8, E), F32),
        "hbuf": vmem((nz, 8, E), F32),
        "fmsg": vmem((8, E), F32),
        "fbuf": vmem((np_, 8, E), F32),
        "load_sem": dma((len(LOADS),)),
        "ring_send": dma((4, steps)),
        "ring_recv": dma((4, steps)),
        "send_sem": dma((8,)),
        "recv_sem": dma((8,)),
    }
    hbm = pl.BlockSpec(memory_space=pltpu.HBM)
    return pl.pallas_call(
        functools.partial(kernel, sizes, INPUTS + ("out_hbm", "lm") + tuple(scratch)),
        out_shape=(
            jax.ShapeDtypeStruct(cot.shape, BF),
            jax.ShapeDtypeStruct((pp.shape[0], rb), BF),
        ),
        in_specs=[pl.BlockSpec(memory_space=pltpu.SMEM)] + [hbm] * len(operands),
        out_specs=(hbm, pl.BlockSpec(memory_space=pltpu.VMEM)),
        scratch_shapes=list(scratch.values()),
        compiler_params=pltpu.CompilerParams(
            collective_id=0, has_side_effects=True, vmem_limit_bytes=58 << 20
        ),
        name="attend_pair_and_gradient",
    )(start, *operands)


def store_kernel(out, lm, out_hbm, lm_hbm, sem):
    parts = sem.shape[0] - 1
    rows = out.shape[0] // parts
    copies = [pltpu.make_async_copy(lm, lm_hbm, sem.at[parts])]
    for i in range(parts):
        part = pl.ds(i * rows, rows)
        copies.append(pltpu.make_async_copy(out.at[part], out_hbm.at[part], sem.at[i]))
    for copy in copies:
        copy.start()
    for copy in copies:
        copy.wait()


def store(out, lm):
    return pl.pallas_call(
        store_kernel,
        out_shape=tuple(jax.ShapeDtypeStruct(a.shape, a.dtype) for a in (out, lm)),
        in_specs=[pl.BlockSpec(memory_space=pltpu.HBM)] * 2,
        out_specs=(pl.BlockSpec(memory_space=pltpu.HBM),) * 2,
        scratch_shapes=[pltpu.SemaphoreType.DMA((min(8, out.shape[0]) + 1,))],
        compiler_params=pltpu.CompilerParams(vmem_limit_bytes=62 << 20),
        name="store_results",
    )(out, lm)


def body(
    sizes,
    queries,
    keys,
    values,
    residual,
    out_proj,
    pair_proj,
    chain_bias,
    ln_gain,
    w_in,
    w_out,
    pair_cot,
    residue_mask,
    chain_ids,
    slab_start,
):
    nz, rb = sizes[0], queries.shape[0]
    operands = (
        queries,
        keys,
        values,
        residual.T,
        out_proj,
        pair_proj,
        chain_bias,
        ln_gain.reshape(1, E),
        w_in,
        w_out,
        pair_cot,
        residue_mask.reshape(nz, rb),
        chain_ids.reshape(nz, rb),
        residue_mask,
        chain_ids,
    )
    pair_out, lm_grad = store(*fused(sizes, slab_start, operands))
    return pair_out, lm_grad.T


def solution(mesh):
    sizes = tuple(mesh.shape[name] for name in ("lm", "prow", "pcol"))
    return jax.shard_map(
        functools.partial(body, sizes),
        mesh=mesh,
        in_specs=(
            P("lm", ("prow", "pcol")),
            P("lm", ("prow", "pcol")),
            P("lm", ("prow", "pcol")),
            P("lm", ("prow", "pcol")),
            P(("prow", "pcol"), None),
            P(("prow", "pcol"), None),
            P(),
            P(),
            P(),
            P(),
            P(("lm", "prow"), "pcol", None),
            P(),
            P(),
            P(),
        ),
        out_specs=(P(("lm", "prow"), "pcol", None), P("lm", ("prow", "pcol"))),
        check_vma=False,
    )
```

```python
import functools
import math

import jax
import jax.numpy as jnp
from jax import lax
from jax.experimental import pallas as pl
from jax.experimental.pallas import tpu as pltpu
from jax.sharding import PartitionSpec as P

BF = jnp.bfloat16
F32 = jnp.float32
MESH = pl.DeviceIdType.MESH
E = 128
W = 256


def nn(a, b):
    return lax.dot_general(a, b, (((1,), (0,)), ((), ())), preferred_element_type=F32)


def nt(a, b):
    return lax.dot_general(a, b, (((1,), (1,)), ((), ())), preferred_element_type=F32)


def grid_of(rows, columns):
    row = lax.broadcasted_iota(jnp.int32, (rows, columns), 0)
    column = lax.broadcasted_iota(jnp.int32, (rows, columns), 1)
    return row, column


def one_hot(hit):
    return jnp.where(hit, 1.0, 0.0).astype(BF)


def bits(n):
    return n.bit_length() - 1


def plane_order(pr, pc):
    offsets = list(range(1, pr * pc))
    if (pr, pc) != (4, 8):
        return offsets
    ring = (0, 1, 2, 1)

    def hops(m):
        return ring[(m >> 1) & 3] + ring[((m & 1) << 1) | (m >> 4)]

    return sorted(offsets, key=lambda m: -hops(m))


def z_order(nz):
    return sorted(range(1, nz), key=lambda i: -min(i, nz - i))


class Place:
    def __init__(self, sizes):
        self.nz, self.pr, self.pc = sizes
        self.np = self.pr * self.pc
        self.z = lax.axis_index("lm")
        self.prow = lax.axis_index("prow")
        self.pcol = lax.axis_index("pcol")
        self.q = self.prow * self.pc + self.pcol

    def plane_peer(self, m):
        prow = lax.bitwise_xor(self.prow, m // self.pc)
        pcol = lax.bitwise_xor(self.pcol, m % self.pc)
        return lax.bitwise_xor(self.q, m), (self.z, prow, pcol)

    def z_peer(self, i):
        peer = lax.rem(self.z + i, self.nz)
        return peer, (peer, self.prow, self.pcol)

    def peers(self):
        for i in z_order(self.nz):
            yield self.z_peer(i)[1]
        for m in plane_order(self.pr, self.pc):
            yield self.plane_peer(m)[1]

    def signal_all(self, barrier):
        for device in self.peers():
            pl.semaphore_signal(barrier, inc=1, device_id=device, device_id_type=MESH)

    def wait_all(self, barrier):
        pl.semaphore_wait(barrier, self.np + self.nz - 2)

    def send(self, source, target, send_sem, recv_sem, device):
        pltpu.make_async_remote_copy(
            src_ref=source,
            dst_ref=target,
            send_sem=send_sem,
            recv_sem=recv_sem,
            device_id=device,
            device_id_type=MESH,
        ).start()

    def to_plane(self, source, target, send_sem, recv_sem):
        for m in plane_order(self.pr, self.pc):
            peer, device = self.plane_peer(m)
            self.send(source(peer), target.at[self.q], send_sem, recv_sem, device)

    def to_column(self, source, target, send_sem, recv_sem):
        for i in z_order(self.nz):
            peer, device = self.z_peer(i)
            self.send(source(peer), target.at[self.z], send_sem, recv_sem, device)


def wait_bytes(buffer, count, sem):
    part = buffer.at[pl.ds(0, count)]
    pltpu.make_async_copy(part, part, sem).wait()


class Refs:
    def __init__(self, names, refs):
        for name, ref in zip(names, refs, strict=True):
            setattr(self, name, ref)


INPUTS = (
    "start",
    "q_hbm",
    "k_hbm",
    "v_hbm",
    "res_hbm",
    "op_hbm",
    "pp_hbm",
    "bias_hbm",
    "gain_hbm",
    "w_in_hbm",
    "w_out_hbm",
    "cot_hbm",
    "mask_hbm",
    "chain_hbm",
    "mask_flat_hbm",
    "chain_flat_hbm",
)
LOADS = (
    "k",
    "v",
    "pp",
    "q",
    "mask",
    "res",
    "chain",
    "bias",
    "gain",
    "w_in",
    "w_out",
    "op",
    "cot",
    "mask_flat",
    "chain_flat",
)


class PairGroup:
    def __init__(self, r, rows, columns, first):
        self.r, self.rows, self.columns, self.first = r, rows, columns, first

    def norm_and_hidden(self):
        r, rows, columns = self.r, self.rows, self.columns
        gain = r.gain[...]
        self.lefts = [r.ab[pl.ds(columns + t, 1), :] for t in rows]
        right = r.ab[pl.ds(0, columns), :]
        spread = jnp.concatenate([jnp.broadcast_to(left, (E, E)) for left in self.lefts], axis=0)
        dots = nt(right.astype(BF), spread.astype(BF)) * (1.0 / E)
        self.seeds, centres = [], []
        for j, t in enumerate(rows):
            same = r.chain_column[...] == r.chain_flat[self.first + t].astype(F32)
            seed = self.lefts[j] * right + jnp.where(same, r.bias[1:2, :], r.bias[0:1, :])
            mean = dots[:, j * E : (j + 1) * E] + jnp.where(
                same, r.bias_mean[1:2, :], r.bias_mean[0:1, :]
            )
            self.seeds.append(seed)
            centres.append(seed - mean)
        self.inverses = []
        for j in range(0, len(rows), 2):
            squares = jnp.concatenate([c * c for c in centres[j : j + 2]], axis=1).astype(BF)
            inverse = lax.rsqrt(nn(squares, r.means[...]) + 1e-05)
            self.inverses += [inverse[:, :E], inverse[:, E:]]
        self.normeds = [c * inverse for c, inverse in zip(centres, self.inverses)]
        scaled = jnp.concatenate([(n * gain).astype(BF) for n in self.normeds], axis=0)
        self.half = nn(scaled, r.w_half[...])

    def activate(self):
        r = self.r
        d_act = jnp.concatenate([r.d_act[t] for t in self.rows], axis=0)
        turned = jnp.tanh(self.half)
        raised = 1.0 + turned
        act = self.half * raised
        d_hidden = (d_act * (raised + act * (1.0 - turned))).astype(BF)
        self.y = nn(act.astype(BF), r.w_out[...])
        self.d_scaled = nt(d_hidden, r.w_in[...])

    def finish(self, total):
        r, columns = self.r, self.columns
        gain = r.gain[...]
        for j, t in enumerate(self.rows):
            live = r.mask_flat[self.first + t].astype(F32)
            block = slice(j * columns, (j + 1) * columns)
            r.out[t] = ((self.seeds[j] + self.y[block]) * (r.live_column[...] * live)).astype(BF)
            d_normed = self.d_scaled[block] * gain
            both = jnp.concatenate([d_normed, d_normed * self.normeds[j]], axis=1).astype(BF)
            both = nn(both, r.means[...])
            d_seed = r.cot[t].astype(F32) + self.inverses[j] * (
                d_normed - both[:, :E] - self.normeds[j] * both[:, E:]
            )
            total = total + d_seed * (self.lefts[j] * live)
            r.grads[pl.ds(columns + t, 1), :] = live * jnp.sum(
                d_seed * r.right_live[...], axis=0, keepdims=True
            )
        return total


def pair_tile(r, tile, columns, first, done):
    per = min(4, tile)
    groups = [
        PairGroup(r, range(at, at + per), columns, first) for at in range(0, tile, per)
    ]
    total = jnp.zeros((columns, E), F32)
    for i in range(len(groups) + 2):
        if i < len(groups):
            groups[i].norm_and_hidden()
        if 0 <= i - 1 < len(groups):
            groups[i - 1].activate()
        if i >= 2:
            total = groups[i - 2].finish(total)
            done((i - 2) * per, per)
    return total


def kernel(sizes, names, *refs):
    r = Refs(names, refs)
    me = Place(sizes)
    nz, pr, pc, np_ = me.nz, me.pr, me.pc, me.np
    z, q = me.z, me.q
    rb = r.q.shape[0]
    fd = r.pp.shape[0]
    wz = W // nz
    columns = 8 * np_
    slab_plane = 2 * np_
    slab_tile = slab_plane // pr
    log_np = bits(np_)

    barrier = pltpu.get_barrier_semaphore()
    loads = {}
    for i, name in enumerate(LOADS):
        target = getattr(r, name)
        if name in ("k", "v"):
            target = target.at[z]
        loads[name] = pltpu.make_async_copy(getattr(r, name + "_hbm"), target, r.load_sem.at[i])
    for name in LOADS[:3]:
        loads[name].start()
    me.signal_all(barrier)
    for name in LOADS[3:]:
        loads[name].start()
    loads["k"].wait()
    loads["v"].wait()
    me.wait_all(barrier)

    furthest = (nz // 2, nz - 1 - nz // 2)

    def ring(chain, distance, hop):
        buf = r.k if chain < 2 else r.v
        way = 1 if chain % 2 == 0 else -1
        block = lax.rem(z - way * (distance - hop) + nz, nz)
        peer = lax.rem(z + way * hop + nz, nz)
        return pltpu.make_async_remote_copy(
            src_ref=buf.at[block],
            dst_ref=buf.at[block],
            send_sem=r.ring_send.at[chain, distance - 1],
            recv_sem=r.ring_recv.at[chain, distance - 1],
            device_id=(peer, me.prow, me.pcol),
            device_id_type=MESH,
        )

    def pass_on(chain, held):
        for hop in (2, 1):
            if held + hop <= furthest[chain % 2]:
                ring(chain, held + hop, hop).start()

    for chain in range(4):
        pass_on(chain, 0)

    loads["pp"].wait()
    row, column = grid_of(wz, W)
    piece = nt(one_hot(column == row + z * wz), r.pp[...]).astype(BF)
    row, column = grid_of(fd, W)
    piece = nn(piece, one_hot(column == row + ((fd * q) & 127))).astype(BF)
    r.ppmsg[...] = piece
    r.ppg[q] = piece
    me.to_plane(lambda peer: r.ppmsg, r.ppg, r.send_sem.at[0], r.recv_sem.at[0])

    row, column = grid_of(8 * np_, rb)
    r.perm[...] = one_hot(column == (row & 3) * np_ + (row >> 3))
    loads["res"].wait()
    rows_twice = nt(r.perm[...], r.res[...]).astype(BF)
    both = nn(rows_twice, r.pp[...])
    row, column = grid_of(8 * np_, E)
    is_left = (row & 7) < 4
    r.presidual[...] = jnp.where(is_left, both[:, :E], both[:, E:])
    loads["q"].wait()
    loads["mask"].wait()

    scale = 1.0 / math.sqrt(E)

    def score(block):
        raw = nt(r.q[...], r.k[block]) * scale
        live = r.mask[pl.ds(block, 1), :]
        r.scores[block] = jnp.where(live > 0, raw, -1e30)

    score(z)

    def arrive(chain, distance):
        if distance <= furthest[chain % 2]:
            ring(chain, distance, 1 if distance % 2 else 2).wait_recv()
            if distance % 2 == 0:
                pass_on(chain, distance)

    def score_at(distance):
        if distance <= furthest[0]:
            score(lax.rem(z - distance + nz, nz))
        if distance <= furthest[1]:
            score(lax.rem(z + distance, nz))

    w0 = r.start[0] + z * slab_plane
    r0 = w0 + ((q - w0) & (np_ - 1))
    k0 = r0 >> log_np
    first = w0 + me.prow * slab_tile
    second_half = jnp.where(me.prow >= pr // 2, 1, 0)

    def make_w2():
        loads["op"].wait()
        wait_bytes(r.ppg, np_ - 1, r.recv_sem.at[0])
        total = jnp.zeros((E, wz), F32)
        for chunk in range(np_):
            at = ((fd * chunk) >> 7) << 7
            total = total + nt(r.op[:, at : at + W], r.ppg[chunk])
        row, column = grid_of(wz, wz)
        turned = nt(one_hot(row == column), total.astype(BF)).astype(BF)
        r.w2msg[...] = turned
        r.w2g[z] = turned
        me.to_column(lambda peer: r.w2msg, r.w2g, r.send_sem.at[1], r.recv_sem.at[1])

    def make_picks():
        row, column = grid_of(pc * 16, 8 * nz)
        sub = row & 15
        right_hit = (sub < 8) & (column == (2 * (row >> 4) + (sub >> 2)) * 8 + 4 + (sub & 3))
        kk = k0 + (sub - 8)
        left_hit = ((sub == 8) | (sub == 9)) & (column == (kk >> 2) * 8 + (kk & 3))
        r.pick[...] = one_hot(right_hit | left_hit)
        row, column = grid_of(columns + slab_tile, 16 * np_)
        right_hit = (row < columns) & (column == (row & (np_ - 1)) * 16 + (row >> log_np))
        left_hit = (row >= columns) & (
            column == ((first + row - columns) & (np_ - 1)) * 16 + 8 + second_half
        )
        r.place_rows[...] = one_hot(right_hit | left_hit)
        row, column = grid_of(16 * np_, columns + slab_tile)
        sub = row & 15
        owner = row >> 4
        right_hit = (sub < 8) & (column == sub * np_ + owner)
        left_hit = (
            (sub == 8 + second_half)
            & (column >= columns)
            & (((first + column - columns) & (np_ - 1)) == owner)
        )
        r.spread_rows[...] = one_hot(right_hit | left_hit)

    def make_pair_constants():
        for name in ("chain", "bias", "gain", "w_in", "w_out", "mask_flat", "chain_flat"):
            loads[name].wait()
        r.w_half[...] = (r.w_in[...].astype(F32) * 0.5).astype(BF)
        r.w_out_half[...] = (r.w_out[...].astype(F32) * 0.5).astype(BF)
        row, column = grid_of(2 * E, 2 * E)
        r.means[...] = jnp.where((row >> 7) == (column >> 7), 1.0 / E, 0.0).astype(BF)
        r.bias_mean[...] = jnp.broadcast_to(jnp.mean(r.bias[...], axis=1, keepdims=True), (2, E))
        row, column = grid_of(rb, rb)
        unit = one_hot(row == column)
        for half in range(2):
            at = pl.ds(2 * me.pcol + half, 1)
            to = pl.ds(half * rb, rb)
            for source, target in ((r.mask, r.live_column), (r.chain, r.chain_column)):
                lanes = jnp.broadcast_to(source[at, :].astype(F32), (E, rb)).astype(BF)
                target[to, :] = nt(unit, lanes)

    def make_d_act(first_row, end_row):
        for t in range(first_row, end_row):
            r.d_act[t] = nt(r.cot[t], r.w_out_half[...]).astype(r.d_act.dtype)

    last = nz // 2
    third = max(1, slab_tile // 4)
    chores = {
        0: (make_pair_constants, make_picks),
        2: (lambda: loads["cot"].wait(), lambda: make_d_act(0, third)),
        4: (make_w2,),
        6: (lambda: make_d_act(third, slab_tile),),
    }
    for chore in chores[0]:
        chore()
    for distance in range(2, last, 2):
        for chain in range(4):
            arrive(chain, distance)
        for chore in chores.pop(distance, ()):
            chore()
        for near in (distance - 1, distance):
            if near % 2:
                for chain in range(2):
                    arrive(chain, near)
            score_at(near)
    for stage in (2, 4, 6):
        for chore in chores.pop(stage, ()):
            chore()
    for chain in (0, 1):
        arrive(chain, last)
        arrive(chain, last - 1)
    score_at(last - 1)
    score_at(last)

    top = r.scores[0]
    for b in range(1, nz):
        top = jnp.maximum(top, r.scores[b])
    top = jnp.max(top, axis=1, keepdims=True)
    below = jnp.zeros((rb, rb), F32)
    above = jnp.zeros((rb, E), F32)
    for distance in range(1, last + 1):
        if distance % 2 or distance == last:
            for chain in (2, 3):
                arrive(chain, distance)
        left = lax.rem(z - distance + nz, nz)
        right = lax.rem(z + (distance if distance < last else 0), nz)
        shifted = [jnp.exp(r.scores[b] - top) for b in (left, right)]
        below = below + shifted[0] + shifted[1]
        weights = jnp.concatenate(shifted, axis=1).astype(BF)
        above = above + nn(weights, jnp.concatenate([r.v[left], r.v[right]], axis=0))
    attended = (above / jnp.sum(below, axis=1, keepdims=True)).astype(BF)

    twice = nn(r.perm[...], attended).astype(BF)
    wait_bytes(r.w2g, nz - 1, r.recv_sem.at[1])
    both = nt(twice, r.w2g[...].reshape(W, E))
    terms = jnp.where(is_left, both[:, :E], both[:, E:]) + r.presidual[...]
    r.pmsg[...] = terms.reshape(np_, 8, E)
    me.to_plane(lambda peer: r.pmsg.at[peer], r.pbuf, r.send_sem.at[2], r.recv_sem.at[2])
    r.pbuf[q] = r.pmsg[q]
    wait_bytes(r.pbuf, np_ - 1, r.recv_sem.at[2])
    projected = jnp.sum(r.pbuf[...], axis=0).astype(BF).astype(F32)
    r.tmsg[...] = projected
    r.zbuf[z] = projected
    me.to_column(lambda peer: r.tmsg, r.zbuf, r.send_sem.at[3], r.recv_sem.at[3])
    wait_bytes(r.zbuf, nz - 1, r.recv_sem.at[3])
    chosen = nn(r.pick[...], r.zbuf[...].reshape(8 * nz, E).astype(BF)).astype(BF)
    r.msg[...] = chosen.reshape(pc, 16, E)
    me.to_plane(
        lambda peer: r.msg.at[lax.rem(peer, pc)], r.rbuf, r.send_sem.at[4], r.recv_sem.at[4]
    )
    r.rbuf[q] = r.msg[me.pcol]
    wait_bytes(r.rbuf, np_ - 1, r.recv_sem.at[4])
    r.ab[...] = nn(r.place_rows[...], r.rbuf[...].reshape(16 * np_, E))

    r.right_live[...] = r.ab[pl.ds(0, columns), :] * r.live_column[...]

    def store(at, count):
        part = pl.ds(at, count)
        pltpu.make_async_copy(r.out.at[part], r.out_hbm.at[part], r.store_sem).start()

    total = pair_tile(r, slab_tile, columns, first, store)
    r.grads[pl.ds(0, columns), :] = total * r.live_column[...]
    gathered = nn(r.spread_rows[...], r.grads[...].astype(BF)).astype(BF)
    r.gmsg[...] = gathered.reshape(np_, 16, E)
    me.to_plane(lambda peer: r.gmsg.at[peer], r.gbuf, r.send_sem.at[5], r.recv_sem.at[5])
    r.gbuf[q] = r.gmsg[q]
    wait_bytes(r.gbuf, np_ - 1, r.recv_sem.at[5])
    by_column = jnp.sum(r.gbuf[...].astype(F32).reshape(pr, pc, 16, E), axis=0)
    over_columns = jnp.sum(by_column, axis=0)
    left0 = over_columns[8:9, :]
    left1 = over_columns[9:10, :]
    sub, _ = grid_of(8, E)
    for other in range(nz):
        k = 4 * other + (sub & 3)
        lefts = jnp.where(k == k0, left0, jnp.where(k == k0 + 1, left1, 0.0))
        r.zmsg[other] = jnp.where((sub >> 2) == other % 2, by_column[other // 2, 0:8, :], lefts)
    me.to_column(lambda peer: r.zmsg.at[peer], r.hbuf, r.send_sem.at[6], r.recv_sem.at[6])
    r.hbuf[z] = r.zmsg[z]
    wait_bytes(r.hbuf, nz - 1, r.recv_sem.at[6])
    tile = jnp.sum(r.hbuf[...], axis=0).astype(BF).astype(F32)
    r.fmsg[...] = tile
    r.fbuf[q] = tile
    me.to_plane(lambda peer: r.fmsg, r.fbuf, r.send_sem.at[7], r.recv_sem.at[7])
    odd = z & 1
    row, column = grid_of(rb, 8 * np_)
    base = (row & (np_ - 1)) * 8 + (row >> log_np)
    left_pick = one_hot(column == base + 4 * (1 - odd))
    right_pick = one_hot(column == base + 4 * odd)
    for chain in range(4):
        for distance in range(1, furthest[chain % 2] + 1):
            ring(chain, distance, 1 if distance % 2 else 2).wait_send()
    wait_bytes(r.ppg, np_ - 1, r.send_sem.at[0])
    wait_bytes(r.w2g, nz - 1, r.send_sem.at[1])
    wait_bytes(r.pbuf, np_ - 1, r.send_sem.at[2])
    wait_bytes(r.zbuf, nz - 1, r.send_sem.at[3])
    wait_bytes(r.rbuf, np_ - 1, r.send_sem.at[4])
    wait_bytes(r.gbuf, np_ - 1, r.send_sem.at[5])
    wait_bytes(r.hbuf, nz - 1, r.send_sem.at[6])
    wait_bytes(r.fbuf, np_ - 1, r.recv_sem.at[7])
    tiles = r.fbuf[...].reshape(8 * np_, E).astype(BF)
    pltpu.make_async_copy(r.out, r.out_hbm, r.store_sem).wait()
    left = nn(left_pick, tiles).astype(BF)
    right = nn(right_pick, tiles).astype(BF)
    r.lm[...] = (nt(r.pp[:, :E], left) + nt(r.pp[:, E:], right)).astype(BF)
    wait_bytes(r.fbuf, np_ - 1, r.send_sem.at[7])


D_ACT = F32


def fused(sizes, start, operands):
    nz, pr, pc = sizes
    np_ = pr * pc
    q, k, v, res, op, pp, bias, gain, w_in, w_out, cot, mask, chain, mask_flat, chain_flat = operands
    rb = q.shape[0]
    columns = 8 * np_
    tile = 2 * np_ // pr
    wz = W // nz
    vmem, dma = pltpu.VMEM, pltpu.SemaphoreType.DMA
    steps = max(1, nz // 2)
    scratch = {
        "q": vmem(q.shape, BF),
        "k": vmem((nz, rb, E), BF),
        "v": vmem((nz, rb, E), BF),
        "res": vmem(res.shape, BF),
        "op": vmem(op.shape, BF),
        "pp": vmem(pp.shape, BF),
        "bias": vmem(bias.shape, F32),
        "gain": vmem(gain.shape, F32),
        "w_in": vmem(w_in.shape, BF),
        "w_out": vmem(w_out.shape, BF),
        "cot": vmem(cot.shape, BF),
        "mask": vmem(mask.shape, jnp.int32),
        "chain": vmem(chain.shape, jnp.int32),
        "mask_flat": pltpu.SMEM(mask_flat.shape, jnp.int32),
        "chain_flat": pltpu.SMEM(chain_flat.shape, jnp.int32),
        "scores": vmem((nz, rb, rb), F32),
        "perm": vmem((8 * np_, rb), BF),
        "pick": vmem((pc * 16, 8 * nz), BF),
        "place_rows": vmem((columns + tile, 16 * np_), BF),
        "spread_rows": vmem((16 * np_, columns + tile), BF),
        "presidual": vmem((8 * np_, E), F32),
        "ppmsg": vmem((wz, W), BF),
        "ppg": vmem((np_, wz, W), BF),
        "w2msg": vmem((wz, E), BF),
        "w2g": vmem((nz, wz, E), BF),
        "pmsg": vmem((np_, 8, E), F32),
        "pbuf": vmem((np_, 8, E), F32),
        "tmsg": vmem((8, E), F32),
        "zbuf": vmem((nz, 8, E), F32),
        "msg": vmem((pc, 16, E), BF),
        "rbuf": vmem((np_, 16, E), BF),
        "ab": vmem((columns + tile, E), F32),
        "out": vmem(cot.shape, BF),
        "store_sem": dma,
        "w_half": vmem(w_in.shape, BF),
        "w_out_half": vmem(w_out.shape, BF),
        "means": vmem((2 * E, 2 * E), BF),
        "bias_mean": vmem((2, E), F32),
        "live_column": vmem((columns, E), F32),
        "chain_column": vmem((columns, E), F32),
        "right_live": vmem((columns, E), F32),
        "d_act": vmem(cot.shape[:2] + w_in.shape[1:], D_ACT),
        "grads": vmem((columns + tile, E), F32),
        "gmsg": vmem((np_, 16, E), BF),
        "gbuf": vmem((np_, 16, E), BF),
        "zmsg": vmem((nz, 8, E), F32),
        "hbuf": vmem((nz, 8, E), F32),
        "fmsg": vmem((8, E), F32),
        "fbuf": vmem((np_, 8, E), F32),
        "load_sem": dma((len(LOADS),)),
        "ring_send": dma((4, steps)),
        "ring_recv": dma((4, steps)),
        "send_sem": dma((8,)),
        "recv_sem": dma((8,)),
    }
    hbm = pl.BlockSpec(memory_space=pltpu.HBM)
    return pl.pallas_call(
        functools.partial(kernel, sizes, INPUTS + ("out_hbm", "lm") + tuple(scratch)),
        out_shape=(
            jax.ShapeDtypeStruct(cot.shape, BF),
            jax.ShapeDtypeStruct((pp.shape[0], rb), BF),
        ),
        in_specs=[pl.BlockSpec(memory_space=pltpu.SMEM)] + [hbm] * len(operands),
        out_specs=(hbm, pl.BlockSpec(memory_space=pltpu.VMEM)),
        scratch_shapes=list(scratch.values()),
        compiler_params=pltpu.CompilerParams(
            collective_id=0, has_side_effects=True, vmem_limit_bytes=58 << 20
        ),
        name="attend_pair_and_gradient",
    )(start, *operands)


def store_kernel(out, lm, out_hbm, lm_hbm, out_vmem, lm_vmem, load_sem, save_sem):
    parts = load_sem.shape[0] - 1
    rows = out.shape[0] // parts
    ways = [(lm, lm_vmem, lm_hbm)]
    for i in range(parts):
        part = pl.ds(i * rows, rows)
        ways.append((out.at[part], out_vmem.at[part], out_hbm.at[part]))
    loads = [pltpu.make_async_copy(w[0], w[1], load_sem.at[i]) for i, w in enumerate(ways)]
    saves = [pltpu.make_async_copy(w[1], w[2], save_sem.at[i]) for i, w in enumerate(ways)]
    for load in loads:
        load.start()
    for load, save in zip(loads, saves):
        load.wait()
        save.start()
    for save in saves:
        save.wait()


def store(out, lm):
    parts = min(8, out.shape[0]) + 1
    return pl.pallas_call(
        store_kernel,
        out_shape=tuple(jax.ShapeDtypeStruct(a.shape, a.dtype) for a in (out, lm)),
        in_specs=[pl.BlockSpec(memory_space=pltpu.HBM)] * 2,
        out_specs=(pl.BlockSpec(memory_space=pltpu.HBM),) * 2,
        scratch_shapes=[
            pltpu.VMEM(out.shape, out.dtype),
            pltpu.VMEM(lm.shape, lm.dtype),
            pltpu.SemaphoreType.DMA((parts,)),
            pltpu.SemaphoreType.DMA((parts,)),
        ],
        compiler_params=pltpu.CompilerParams(vmem_limit_bytes=62 << 20),
        name="store_results",
    )(out, lm)


def body(
    sizes,
    queries,
    keys,
    values,
    residual,
    out_proj,
    pair_proj,
    chain_bias,
    ln_gain,
    w_in,
    w_out,
    pair_cot,
    residue_mask,
    chain_ids,
    slab_start,
):
    nz, rb = sizes[0], queries.shape[0]
    operands = (
        queries,
        keys,
        values,
        residual.T,
        out_proj,
        pair_proj,
        chain_bias,
        ln_gain.reshape(1, E),
        w_in,
        w_out,
        pair_cot,
        residue_mask.reshape(nz, rb),
        chain_ids.reshape(nz, rb),
        residue_mask,
        chain_ids,
    )
    pair_out, lm_grad = store(*fused(sizes, slab_start, operands))
    return pair_out, lm_grad.T


def solution(mesh):
    sizes = tuple(mesh.shape[name] for name in ("lm", "prow", "pcol"))
    return jax.shard_map(
        functools.partial(body, sizes),
        mesh=mesh,
        in_specs=(
            P("lm", ("prow", "pcol")),
            P("lm", ("prow", "pcol")),
            P("lm", ("prow", "pcol")),
            P("lm", ("prow", "pcol")),
            P(("prow", "pcol"), None),
            P(("prow", "pcol"), None),
            P(),
            P(),
            P(),
            P(),
            P(("lm", "prow"), "pcol", None),
            P(),
            P(),
            P(),
        ),
        out_specs=(P(("lm", "prow"), "pcol", None), P("lm", ("prow", "pcol"))),
        check_vma=False,
    )
```

```python
import functools
import math

import jax
import jax.numpy as jnp
from jax import lax
from jax.experimental import pallas as pl
from jax.experimental.pallas import tpu as pltpu
from jax.sharding import PartitionSpec as P

BF = jnp.bfloat16
F32 = jnp.float32
MESH = pl.DeviceIdType.MESH
E = 128
W = 256


def nn(a, b):
    return lax.dot_general(a, b, (((1,), (0,)), ((), ())), preferred_element_type=F32)


def nt(a, b):
    return lax.dot_general(a, b, (((1,), (1,)), ((), ())), preferred_element_type=F32)


def grid_of(rows, columns):
    row = lax.broadcasted_iota(jnp.int32, (rows, columns), 0)
    column = lax.broadcasted_iota(jnp.int32, (rows, columns), 1)
    return row, column


def one_hot(hit):
    return jnp.where(hit, 1.0, 0.0).astype(BF)


def bits(n):
    return n.bit_length() - 1


def plane_order(pr, pc):
    offsets = list(range(1, pr * pc))
    if (pr, pc) != (4, 8):
        return offsets
    ring = (0, 1, 2, 1)

    def hops(m):
        return ring[(m >> 1) & 3] + ring[((m & 1) << 1) | (m >> 4)]

    return sorted(offsets, key=lambda m: -hops(m))


def group_of(nz):
    return min(8, nz)


def z_order(nz):
    return sorted(range(1, nz), key=lambda i: -min(i, nz - i))


class Place:
    def __init__(self, sizes):
        self.nz, self.pr, self.pc = sizes
        self.np = self.pr * self.pc
        self.z = lax.axis_index("lm")
        self.prow = lax.axis_index("prow")
        self.pcol = lax.axis_index("pcol")
        self.q = self.prow * self.pc + self.pcol

    def plane_peer(self, m):
        prow = lax.bitwise_xor(self.prow, m // self.pc)
        pcol = lax.bitwise_xor(self.pcol, m % self.pc)
        return lax.bitwise_xor(self.q, m), (self.z, prow, pcol)

    def z_peer(self, i):
        peer = lax.rem(self.z + i, self.nz)
        return peer, (peer, self.prow, self.pcol)

    def near(self):
        reach = max(2, group_of(self.nz) // 2)
        return sorted({way * d % self.nz for d in range(1, reach + 1) for way in (1, -1)} - {0})

    def greeted(self):
        for i in self.near():
            yield self.z_peer(i)[1]
        for m in plane_order(self.pr, self.pc):
            yield self.plane_peer(m)[1]

    def signal_all(self, barrier):
        for device in self.greeted():
            pl.semaphore_signal(barrier, inc=1, device_id=device, device_id_type=MESH)

    def wait_all(self, barrier):
        pl.semaphore_wait(barrier, self.np - 1 + len(self.near()))

    def send(self, source, target, send_sem, recv_sem, device):
        pltpu.make_async_remote_copy(
            src_ref=source,
            dst_ref=target,
            send_sem=send_sem,
            recv_sem=recv_sem,
            device_id=device,
            device_id_type=MESH,
        ).start()

    def to_plane(self, source, target, send_sem, recv_sem):
        for m in plane_order(self.pr, self.pc):
            peer, device = self.plane_peer(m)
            self.send(source(peer), target.at[self.q], send_sem, recv_sem, device)

    def to_group(self, source, target, send_sem, recv_sem):
        group = group_of(self.nz)
        slot = lax.rem(self.z, group)
        for i in range(-(group // 2), group // 2):
            if i:
                device = self.z_peer(i % self.nz)[1]
                self.send(source, target.at[slot], send_sem, recv_sem, device)

    def to_column(self, source, target, send_sem, recv_sem):
        for i in z_order(self.nz):
            peer, device = self.z_peer(i)
            self.send(source(peer), target.at[self.z], send_sem, recv_sem, device)


def wait_bytes(buffer, count, sem):
    part = buffer.at[pl.ds(0, count)]
    pltpu.make_async_copy(part, part, sem).wait()


class Refs:
    def __init__(self, names, refs):
        for name, ref in zip(names, refs, strict=True):
            setattr(self, name, ref)


INPUTS = (
    "start",
    "q_hbm",
    "k_hbm",
    "v_hbm",
    "res_hbm",
    "op_hbm",
    "pp_hbm",
    "bias_hbm",
    "gain_hbm",
    "w_in_hbm",
    "w_out_hbm",
    "cot_hbm",
    "mask_hbm",
    "chain_hbm",
    "mask_flat_hbm",
    "chain_flat_hbm",
)
LOADS = (
    "k",
    "v",
    "pp",
    "q",
    "mask",
    "res",
    "chain",
    "bias",
    "gain",
    "w_in",
    "w_out",
    "op",
    "cot",
    "mask_flat",
    "chain_flat",
)


class PairGroup:
    def __init__(self, r, rows, columns, first):
        self.r, self.rows, self.columns, self.first = r, rows, columns, first

    def norm_and_hidden(self):
        r, rows, columns = self.r, self.rows, self.columns
        gain = r.gain[...]
        self.lefts = [r.ab[pl.ds(columns + t, 1), :] for t in rows]
        right = r.ab[pl.ds(0, columns), :]
        spread = jnp.concatenate([jnp.broadcast_to(left, (E, E)) for left in self.lefts], axis=0)
        dots = nt(right.astype(BF), spread.astype(BF)) * (1.0 / E)
        self.seeds, centres = [], []
        for j, t in enumerate(rows):
            same = r.chain_column[...] == r.chain_flat[self.first + t].astype(F32)
            seed = self.lefts[j] * right + jnp.where(same, r.bias[1:2, :], r.bias[0:1, :])
            mean = dots[:, j * E : (j + 1) * E] + jnp.where(
                same, r.bias_mean[1:2, :], r.bias_mean[0:1, :]
            )
            self.seeds.append(seed)
            centres.append(seed - mean)
        self.inverses = [
            lax.rsqrt(jnp.mean(c * c, axis=1, keepdims=True) + 1e-05) for c in centres
        ]
        self.normeds = [c * inverse for c, inverse in zip(centres, self.inverses)]
        scaled = jnp.concatenate([(n * gain).astype(BF) for n in self.normeds], axis=0)
        self.half = nn(scaled, r.w_half[...])

    def activate(self):
        r = self.r
        d_act = jnp.concatenate([r.d_act[t] for t in self.rows], axis=0)
        half = self.half.astype(D_ACT)
        turned = jnp.tanh(half)
        raised = 1.0 + turned
        act = half * raised
        d_hidden = (d_act * (raised + act * (1.0 - turned))).astype(BF)
        self.y = nn(act.astype(BF), r.w_out[...])
        self.d_scaled = nt(d_hidden, r.w_in[...])

    def finish(self, total):
        r, columns = self.r, self.columns
        gain = r.gain[...]
        for j, t in enumerate(self.rows):
            live = r.mask_flat[self.first + t].astype(F32)
            block = slice(j * columns, (j + 1) * columns)
            r.out[t] = ((self.seeds[j] + self.y[block]) * (r.live_column[...] * live)).astype(BF)
            d_normed = self.d_scaled[block] * gain
            both = jnp.concatenate([d_normed, d_normed * self.normeds[j]], axis=1).astype(BF)
            both = nn(both, r.means[...])
            d_seed = r.cot[t].astype(F32) + self.inverses[j] * (
                d_normed - both[:, :E] - self.normeds[j] * both[:, E:]
            )
            total = total + d_seed * (self.lefts[j] * live)
            r.grads[pl.ds(columns + t, 1), :] = live * jnp.sum(
                d_seed * r.right_live[...], axis=0, keepdims=True
            )
        return total


def pair_tile(r, tile, columns, first, done):
    per = min(4, tile)
    groups = [
        PairGroup(r, range(at, at + per), columns, first) for at in range(0, tile, per)
    ]
    total = jnp.zeros((columns, E), F32)
    for i in range(len(groups) + 2):
        if i < len(groups):
            groups[i].norm_and_hidden()
        if 0 <= i - 1 < len(groups):
            groups[i - 1].activate()
        if i >= 2:
            total = groups[i - 2].finish(total)
            done((i - 2) * per, per)
    return total


def kernel(sizes, names, *refs):
    r = Refs(names, refs)
    me = Place(sizes)
    nz, pr, pc, np_ = me.nz, me.pr, me.pc, me.np
    z, q = me.z, me.q
    rb = r.q.shape[0]
    fd = r.pp.shape[0]
    group = group_of(nz)
    wz = W // group
    columns = 8 * np_
    slab_plane = 2 * np_
    slab_tile = slab_plane // pr
    log_np = bits(np_)

    barrier = pltpu.get_barrier_semaphore()
    loads = {}
    for i, name in enumerate(LOADS):
        target = getattr(r, name)
        if name in ("k", "v"):
            target = target.at[z]
        loads[name] = pltpu.make_async_copy(getattr(r, name + "_hbm"), target, r.load_sem.at[i])
    for name in LOADS[:3]:
        loads[name].start()
    me.signal_all(barrier)
    for name in LOADS[3:]:
        loads[name].start()
    loads["k"].wait()
    loads["v"].wait()
    me.wait_all(barrier)

    furthest = (nz // 2, nz - 1 - nz // 2, nz - 1 - nz // 2, nz // 2)

    def ring(chain, distance, hop):
        buf = r.k if chain < 2 else r.v
        way = 1 if chain % 2 == 0 else -1
        block = lax.rem(z - way * (distance - hop) + nz, nz)
        peer = lax.rem(z + way * hop + nz, nz)
        return pltpu.make_async_remote_copy(
            src_ref=buf.at[block],
            dst_ref=buf.at[block],
            send_sem=r.ring_send.at[chain, distance - 1],
            recv_sem=r.ring_recv.at[chain, distance - 1],
            device_id=(peer, me.prow, me.pcol),
            device_id_type=MESH,
        )

    def pass_on(chain, held):
        for hop in (2, 1):
            if held + hop <= furthest[chain]:
                ring(chain, held + hop, hop).start()

    for chain in range(4):
        pass_on(chain, 0)

    loads["pp"].wait()
    row, column = grid_of(wz, W)
    piece = nt(one_hot(column == row + lax.rem(z, group) * wz), r.pp[...]).astype(BF)
    row, column = grid_of(fd, W)
    piece = nn(piece, one_hot(column == row + ((fd * q) & 127))).astype(BF)
    r.ppmsg[...] = piece
    r.ppg[q] = piece
    me.to_plane(lambda peer: r.ppmsg, r.ppg, r.send_sem.at[0], r.recv_sem.at[0])

    row, column = grid_of(8 * np_, rb)
    r.perm[...] = one_hot(column == (row & 3) * np_ + (row >> 3))
    loads["res"].wait()
    rows_twice = nt(r.perm[...], r.res[...]).astype(BF)
    both = nn(rows_twice, r.pp[...])
    row, column = grid_of(8 * np_, E)
    is_left = (row & 7) < 4
    r.presidual[...] = jnp.where(is_left, both[:, :E], both[:, E:])
    loads["q"].wait()
    loads["mask"].wait()

    scale = 1.0 / math.sqrt(E)

    def score(block):
        raw = nt(r.q[...], r.k[block]) * scale
        live = r.mask[pl.ds(block, 1), :]
        r.scores[block] = jnp.where(live > 0, raw, -1e30)

    score(z)

    def arrive(chain, distance):
        if distance <= furthest[chain]:
            ring(chain, distance, 1 if distance % 2 else 2).wait_recv()
            if distance % 2 == 0:
                pass_on(chain, distance)

    def score_at(distance):
        if distance <= furthest[0]:
            score(lax.rem(z - distance + nz, nz))
        if distance <= furthest[1]:
            score(lax.rem(z + distance, nz))

    w0 = r.start[0] + z * slab_plane
    r0 = w0 + ((q - w0) & (np_ - 1))
    k0 = r0 >> log_np
    first = w0 + me.prow * slab_tile
    second_half = jnp.where(me.prow >= pr // 2, 1, 0)

    def make_w2():
        loads["op"].wait()
        wait_bytes(r.ppg, np_ - 1, r.recv_sem.at[0])
        total = jnp.zeros((E, wz), F32)
        for chunk in range(np_):
            at = ((fd * chunk) >> 7) << 7
            total = total + nt(r.op[:, at : at + W], r.ppg[chunk])
        row, column = grid_of(wz, wz)
        turned = nt(one_hot(row == column), total.astype(BF)).astype(BF)
        r.w2msg[...] = turned
        r.w2g[lax.rem(z, group)] = turned
        me.to_group(r.w2msg, r.w2g, r.send_sem.at[1], r.recv_sem.at[1])

    def make_picks():
        row, column = grid_of(pc * 16, 8 * nz)
        sub = row & 15
        right_hit = (sub < 8) & (column == (2 * (row >> 4) + (sub >> 2)) * 8 + 4 + (sub & 3))
        kk = k0 + (sub - 8)
        left_hit = ((sub == 8) | (sub == 9)) & (column == (kk >> 2) * 8 + (kk & 3))
        r.pick[...] = one_hot(right_hit | left_hit)
        row, column = grid_of(columns + slab_tile, 16 * np_)
        right_hit = (row < columns) & (column == (row & (np_ - 1)) * 16 + (row >> log_np))
        left_hit = (row >= columns) & (
            column == ((first + row - columns) & (np_ - 1)) * 16 + 8 + second_half
        )
        r.place_rows[...] = one_hot(right_hit | left_hit)
        row, column = grid_of(16 * np_, columns + slab_tile)
        sub = row & 15
        owner = row >> 4
        right_hit = (sub < 8) & (column == sub * np_ + owner)
        left_hit = (
            (sub == 8 + second_half)
            & (column >= columns)
            & (((first + column - columns) & (np_ - 1)) == owner)
        )
        r.spread_rows[...] = one_hot(right_hit | left_hit)

    def make_pair_constants():
        for name in ("chain", "bias", "gain", "w_in", "w_out", "mask_flat", "chain_flat"):
            loads[name].wait()
        r.w_half[...] = (r.w_in[...].astype(F32) * 0.5).astype(BF)
        r.w_out_half[...] = (r.w_out[...].astype(F32) * 0.5).astype(BF)
        row, column = grid_of(2 * E, 2 * E)
        r.means[...] = jnp.where((row >> 7) == (column >> 7), 1.0 / E, 0.0).astype(BF)
        r.bias_mean[...] = jnp.broadcast_to(jnp.mean(r.bias[...], axis=1, keepdims=True), (2, E))
        row, column = grid_of(rb, rb)
        unit = one_hot(row == column)
        for half in range(2):
            at = pl.ds(2 * me.pcol + half, 1)
            to = pl.ds(half * rb, rb)
            for source, target in ((r.mask, r.live_column), (r.chain, r.chain_column)):
                lanes = jnp.broadcast_to(source[at, :].astype(F32), (E, rb)).astype(BF)
                target[to, :] = nt(unit, lanes)

    def make_d_act(first_row, end_row):
        for t in range(first_row, end_row):
            r.d_act[t] = nt(r.cot[t], r.w_out_half[...]).astype(r.d_act.dtype)

    last = nz // 2
    third = max(1, slab_tile // 4)
    chores = {
        0: (make_pair_constants, make_picks),
        2: (lambda: loads["cot"].wait(), lambda: make_d_act(0, third)),
        4: (make_w2,),
        6: (lambda: make_d_act(third, slab_tile),),
    }
    for chore in chores[0]:
        chore()
    for distance in range(2, last, 2):
        for chain in range(4):
            arrive(chain, distance)
        for chore in chores.pop(distance, ()):
            chore()
        for near in (distance - 1, distance):
            if near % 2:
                for chain in range(2):
                    arrive(chain, near)
            score_at(near)
    for stage in (2, 4, 6):
        for chore in chores.pop(stage, ()):
            chore()
    for chain in (0, 1):
        arrive(chain, last)
        arrive(chain, last - 1)
    score_at(last - 1)
    score_at(last)

    top = r.scores[0]
    for b in range(1, nz):
        top = jnp.maximum(top, r.scores[b])
    top = jnp.max(top, axis=1, keepdims=True)
    below = jnp.zeros((rb, rb), F32)
    above = jnp.zeros((rb, E), F32)
    for distance in range(1, last + 1):
        if distance % 2 or distance == last:
            for chain in (2, 3):
                arrive(chain, distance)
        left = lax.rem(z - distance + nz, nz)
        right = lax.rem(z + (distance if distance < last else 0), nz)
        shifted = [jnp.exp(r.scores[b] - top) for b in (left, right)]
        below = below + shifted[0] + shifted[1]
        weights = jnp.concatenate(shifted, axis=1).astype(BF)
        above = above + nn(weights, jnp.concatenate([r.v[left], r.v[right]], axis=0))
    attended = (above / jnp.sum(below, axis=1, keepdims=True)).astype(BF)

    twice = nn(r.perm[...], attended).astype(BF)
    wait_bytes(r.w2g, group - 1, r.recv_sem.at[1])
    both = nt(twice, r.w2g[...].reshape(W, E))
    terms = jnp.where(is_left, both[:, :E], both[:, E:]) + r.presidual[...]
    r.pmsg[...] = terms.reshape(np_, 8, E)
    me.to_plane(lambda peer: r.pmsg.at[peer], r.pbuf, r.send_sem.at[2], r.recv_sem.at[2])
    r.pbuf[q] = r.pmsg[q]
    wait_bytes(r.pbuf, np_ - 1, r.recv_sem.at[2])
    projected = jnp.sum(r.pbuf[...], axis=0).astype(BF).astype(F32)
    r.tmsg[...] = projected
    r.zbuf[z] = projected
    me.to_column(lambda peer: r.tmsg, r.zbuf, r.send_sem.at[3], r.recv_sem.at[3])
    wait_bytes(r.zbuf, nz - 1, r.recv_sem.at[3])
    chosen = nn(r.pick[...], r.zbuf[...].reshape(8 * nz, E).astype(BF)).astype(BF)
    r.msg[...] = chosen.reshape(pc, 16, E)
    me.to_plane(
        lambda peer: r.msg.at[lax.rem(peer, pc)], r.rbuf, r.send_sem.at[4], r.recv_sem.at[4]
    )
    r.rbuf[q] = r.msg[me.pcol]
    wait_bytes(r.rbuf, np_ - 1, r.recv_sem.at[4])
    r.ab[...] = nn(r.place_rows[...], r.rbuf[...].reshape(16 * np_, E))

    r.right_live[...] = r.ab[pl.ds(0, columns), :] * r.live_column[...]

    def store(at, count):
        part = pl.ds(at, count)
        pltpu.make_async_copy(r.out.at[part], r.out_hbm.at[part], r.store_sem).start()

    total = pair_tile(r, slab_tile, columns, first, store)
    r.grads[pl.ds(0, columns), :] = total * r.live_column[...]
    gathered = nn(r.spread_rows[...], r.grads[...].astype(BF)).astype(BF)
    r.gmsg[...] = gathered.reshape(np_, 16, E)
    me.to_plane(lambda peer: r.gmsg.at[peer], r.gbuf, r.send_sem.at[5], r.recv_sem.at[5])
    r.gbuf[q] = r.gmsg[q]
    wait_bytes(r.gbuf, np_ - 1, r.recv_sem.at[5])
    by_column = jnp.sum(r.gbuf[...].astype(F32).reshape(pr, pc, 16, E), axis=0)
    over_columns = jnp.sum(by_column, axis=0)
    left0 = over_columns[8:9, :]
    left1 = over_columns[9:10, :]
    sub, _ = grid_of(8, E)
    for other in range(nz):
        k = 4 * other + (sub & 3)
        lefts = jnp.where(k == k0, left0, jnp.where(k == k0 + 1, left1, 0.0))
        r.zmsg[other] = jnp.where((sub >> 2) == other % 2, by_column[other // 2, 0:8, :], lefts)
    me.to_column(lambda peer: r.zmsg.at[peer], r.hbuf, r.send_sem.at[6], r.recv_sem.at[6])
    r.hbuf[z] = r.zmsg[z]
    wait_bytes(r.hbuf, nz - 1, r.recv_sem.at[6])
    tile = jnp.sum(r.hbuf[...], axis=0).astype(BF).astype(F32)
    r.fmsg[...] = tile
    r.fbuf[q] = tile
    me.to_plane(lambda peer: r.fmsg, r.fbuf, r.send_sem.at[7], r.recv_sem.at[7])
    odd = z & 1
    row, column = grid_of(rb, 8 * np_)
    base = (row & (np_ - 1)) * 8 + (row >> log_np)
    left_pick = one_hot(column == base + 4 * (1 - odd))
    right_pick = one_hot(column == base + 4 * odd)
    for chain in range(4):
        for distance in range(1, furthest[chain] + 1):
            ring(chain, distance, 1 if distance % 2 else 2).wait_send()
    wait_bytes(r.ppg, np_ - 1, r.send_sem.at[0])
    wait_bytes(r.w2g, group - 1, r.send_sem.at[1])
    wait_bytes(r.pbuf, np_ - 1, r.send_sem.at[2])
    wait_bytes(r.zbuf, nz - 1, r.send_sem.at[3])
    wait_bytes(r.rbuf, np_ - 1, r.send_sem.at[4])
    wait_bytes(r.gbuf, np_ - 1, r.send_sem.at[5])
    wait_bytes(r.hbuf, nz - 1, r.send_sem.at[6])
    wait_bytes(r.fbuf, np_ - 1, r.recv_sem.at[7])
    tiles = r.fbuf[...].reshape(8 * np_, E).astype(BF)
    pltpu.make_async_copy(r.out, r.out_hbm, r.store_sem).wait()
    left = nn(left_pick, tiles).astype(BF)
    right = nn(right_pick, tiles).astype(BF)
    r.lm[...] = (nt(r.pp[:, :E], left) + nt(r.pp[:, E:], right)).astype(BF)
    wait_bytes(r.fbuf, np_ - 1, r.send_sem.at[7])


D_ACT = BF


def fused(sizes, start, operands):
    nz, pr, pc = sizes
    np_ = pr * pc
    q, k, v, res, op, pp, bias, gain, w_in, w_out, cot, mask, chain, mask_flat, chain_flat = operands
    rb = q.shape[0]
    columns = 8 * np_
    tile = 2 * np_ // pr
    group = group_of(nz)
    wz = W // group
    vmem, dma = pltpu.VMEM, pltpu.SemaphoreType.DMA
    steps = max(1, nz // 2)
    scratch = {
        "q": vmem(q.shape, BF),
        "k": vmem((nz, rb, E), BF),
        "v": vmem((nz, rb, E), BF),
        "res": vmem(res.shape, BF),
        "op": vmem(op.shape, BF),
        "pp": vmem(pp.shape, BF),
        "bias": vmem(bias.shape, F32),
        "gain": vmem(gain.shape, F32),
        "w_in": vmem(w_in.shape, BF),
        "w_out": vmem(w_out.shape, BF),
        "cot": vmem(cot.shape, BF),
        "mask": vmem(mask.shape, jnp.int32),
        "chain": vmem(chain.shape, jnp.int32),
        "mask_flat": pltpu.SMEM(mask_flat.shape, jnp.int32),
        "chain_flat": pltpu.SMEM(chain_flat.shape, jnp.int32),
        "scores": vmem((nz, rb, rb), F32),
        "perm": vmem((8 * np_, rb), BF),
        "pick": vmem((pc * 16, 8 * nz), BF),
        "place_rows": vmem((columns + tile, 16 * np_), BF),
        "spread_rows": vmem((16 * np_, columns + tile), BF),
        "presidual": vmem((8 * np_, E), F32),
        "ppmsg": vmem((wz, W), BF),
        "ppg": vmem((np_, wz, W), BF),
        "w2msg": vmem((wz, E), BF),
        "w2g": vmem((group, wz, E), BF),
        "pmsg": vmem((np_, 8, E), F32),
        "pbuf": vmem((np_, 8, E), F32),
        "tmsg": vmem((8, E), F32),
        "zbuf": vmem((nz, 8, E), F32),
        "msg": vmem((pc, 16, E), BF),
        "rbuf": vmem((np_, 16, E), BF),
        "ab": vmem((columns + tile, E), F32),
        "out": vmem(cot.shape, BF),
        "store_sem": dma,
        "w_half": vmem(w_in.shape, BF),
        "w_out_half": vmem(w_out.shape, BF),
        "means": vmem((2 * E, 2 * E), BF),
        "bias_mean": vmem((2, E), F32),
        "live_column": vmem((columns, E), F32),
        "chain_column": vmem((columns, E), F32),
        "right_live": vmem((columns, E), F32),
        "d_act": vmem(cot.shape[:2] + w_in.shape[1:], D_ACT),
        "grads": vmem((columns + tile, E), F32),
        "gmsg": vmem((np_, 16, E), BF),
        "gbuf": vmem((np_, 16, E), BF),
        "zmsg": vmem((nz, 8, E), F32),
        "hbuf": vmem((nz, 8, E), F32),
        "fmsg": vmem((8, E), F32),
        "fbuf": vmem((np_, 8, E), F32),
        "load_sem": dma((len(LOADS),)),
        "ring_send": dma((4, steps)),
        "ring_recv": dma((4, steps)),
        "send_sem": dma((8,)),
        "recv_sem": dma((8,)),
    }
    hbm = pl.BlockSpec(memory_space=pltpu.HBM)
    return pl.pallas_call(
        functools.partial(kernel, sizes, INPUTS + ("out_hbm", "lm") + tuple(scratch)),
        out_shape=(
            jax.ShapeDtypeStruct(cot.shape, BF),
            jax.ShapeDtypeStruct((pp.shape[0], rb), BF),
        ),
        in_specs=[pl.BlockSpec(memory_space=pltpu.SMEM)] + [hbm] * len(operands),
        out_specs=(hbm, pl.BlockSpec(memory_space=pltpu.VMEM)),
        scratch_shapes=list(scratch.values()),
        compiler_params=pltpu.CompilerParams(
            collective_id=0, has_side_effects=True, vmem_limit_bytes=58 << 20
        ),
        name="attend_pair_and_gradient",
    )(start, *operands)


def store_kernel(out, lm, out_hbm, lm_hbm, out_vmem, lm_vmem, load_sem, save_sem):
    parts = load_sem.shape[0] - 1
    rows = out.shape[0] // parts
    ways = [(lm, lm_vmem, lm_hbm)]
    for i in range(parts):
        part = pl.ds(i * rows, rows)
        ways.append((out.at[part], out_vmem.at[part], out_hbm.at[part]))
    loads = [pltpu.make_async_copy(w[0], w[1], load_sem.at[i]) for i, w in enumerate(ways)]
    saves = [pltpu.make_async_copy(w[1], w[2], save_sem.at[i]) for i, w in enumerate(ways)]
    for load in loads:
        load.start()
    for load, save in zip(loads, saves):
        load.wait()
        save.start()
    for save in saves:
        save.wait()


def store(out, lm):
    parts = min(8, out.shape[0]) + 1
    return pl.pallas_call(
        store_kernel,
        out_shape=tuple(jax.ShapeDtypeStruct(a.shape, a.dtype) for a in (out, lm)),
        in_specs=[pl.BlockSpec(memory_space=pltpu.HBM)] * 2,
        out_specs=(pl.BlockSpec(memory_space=pltpu.HBM),) * 2,
        scratch_shapes=[
            pltpu.VMEM(out.shape, out.dtype),
            pltpu.VMEM(lm.shape, lm.dtype),
            pltpu.SemaphoreType.DMA((parts,)),
            pltpu.SemaphoreType.DMA((parts,)),
        ],
        compiler_params=pltpu.CompilerParams(vmem_limit_bytes=62 << 20),
        name="store_results",
    )(out, lm)


def body(
    sizes,
    queries,
    keys,
    values,
    residual,
    out_proj,
    pair_proj,
    chain_bias,
    ln_gain,
    w_in,
    w_out,
    pair_cot,
    residue_mask,
    chain_ids,
    slab_start,
):
    nz, rb = sizes[0], queries.shape[0]
    operands = (
        queries,
        keys,
        values,
        residual.T,
        out_proj,
        pair_proj,
        chain_bias,
        ln_gain.reshape(1, E),
        w_in,
        w_out,
        pair_cot,
        residue_mask.reshape(nz, rb),
        chain_ids.reshape(nz, rb),
        residue_mask,
        chain_ids,
    )
    pair_out, lm_grad = store(*fused(sizes, slab_start, operands))
    return pair_out, lm_grad.T


def solution(mesh):
    sizes = tuple(mesh.shape[name] for name in ("lm", "prow", "pcol"))
    return jax.shard_map(
        functools.partial(body, sizes),
        mesh=mesh,
        in_specs=(
            P("lm", ("prow", "pcol")),
            P("lm", ("prow", "pcol")),
            P("lm", ("prow", "pcol")),
            P("lm", ("prow", "pcol")),
            P(("prow", "pcol"), None),
            P(("prow", "pcol"), None),
            P(),
            P(),
            P(),
            P(),
            P(("lm", "prow"), "pcol", None),
            P(),
            P(),
            P(),
        ),
        out_specs=(P(("lm", "prow"), "pcol", None), P("lm", ("prow", "pcol"))),
        check_vma=False,
    )
```

```python
import functools
import math

import jax
import jax.numpy as jnp
from jax import lax
from jax.experimental import pallas as pl
from jax.experimental.pallas import tpu as pltpu
from jax.sharding import PartitionSpec as P

BF = jnp.bfloat16
F32 = jnp.float32
MESH = pl.DeviceIdType.MESH
E = 128
W = 256


def nn(a, b):
    return lax.dot_general(a, b, (((1,), (0,)), ((), ())), preferred_element_type=F32)


def nt(a, b):
    return lax.dot_general(a, b, (((1,), (1,)), ((), ())), preferred_element_type=F32)


def grid_of(rows, columns):
    row = lax.broadcasted_iota(jnp.int32, (rows, columns), 0)
    column = lax.broadcasted_iota(jnp.int32, (rows, columns), 1)
    return row, column


def one_hot(hit):
    return jnp.where(hit, 1.0, 0.0).astype(BF)


def bits(n):
    return n.bit_length() - 1


def plane_order(pr, pc):
    offsets = list(range(1, pr * pc))
    if (pr, pc) != (4, 8):
        return offsets
    ring = (0, 1, 2, 1)

    def hops(m):
        return ring[(m >> 1) & 3] + ring[((m & 1) << 1) | (m >> 4)]

    return sorted(offsets, key=lambda m: -hops(m))


def group_of(nz):
    return min(8, nz)


def z_order(nz):
    return sorted(range(1, nz), key=lambda i: -min(i, nz - i))


class Place:
    def __init__(self, sizes):
        self.nz, self.pr, self.pc = sizes
        self.np = self.pr * self.pc
        self.z = lax.axis_index("lm")
        self.prow = lax.axis_index("prow")
        self.pcol = lax.axis_index("pcol")
        self.q = self.prow * self.pc + self.pcol

    def plane_peer(self, m):
        prow = lax.bitwise_xor(self.prow, m // self.pc)
        pcol = lax.bitwise_xor(self.pcol, m % self.pc)
        return lax.bitwise_xor(self.q, m), (self.z, prow, pcol)

    def z_peer(self, i):
        peer = lax.rem(self.z + i, self.nz)
        return peer, (peer, self.prow, self.pcol)

    def near(self):
        reach = max(2, group_of(self.nz) // 2)
        return sorted({way * d % self.nz for d in range(1, reach + 1) for way in (1, -1)} - {0})

    def greeted(self):
        for i in self.near():
            yield self.z_peer(i)[1]
        for m in plane_order(self.pr, self.pc):
            yield self.plane_peer(m)[1]

    def signal_all(self, barrier):
        for device in self.greeted():
            pl.semaphore_signal(barrier, inc=1, device_id=device, device_id_type=MESH)

    def wait_all(self, barrier):
        pl.semaphore_wait(barrier, self.np - 1 + len(self.near()))

    def send(self, source, target, send_sem, recv_sem, device):
        pltpu.make_async_remote_copy(
            src_ref=source,
            dst_ref=target,
            send_sem=send_sem,
            recv_sem=recv_sem,
            device_id=device,
            device_id_type=MESH,
        ).start()

    def to_plane(self, source, target, send_sem, recv_sem):
        for m in plane_order(self.pr, self.pc):
            peer, device = self.plane_peer(m)
            self.send(source(peer), target.at[self.q], send_sem, recv_sem, device)

    def to_group(self, source, target, send_sem, recv_sem):
        group = group_of(self.nz)
        slot = lax.rem(self.z, group)
        for i in range(-(group // 2), group // 2):
            if i:
                device = self.z_peer(i % self.nz)[1]
                self.send(source, target.at[slot], send_sem, recv_sem, device)

    def to_column(self, source, target, send_sem, recv_sem):
        for i in z_order(self.nz):
            peer, device = self.z_peer(i)
            self.send(source(peer), target.at[self.z], send_sem, recv_sem, device)


def wait_bytes(buffer, count, sem):
    part = buffer.at[pl.ds(0, count)]
    pltpu.make_async_copy(part, part, sem).wait()


class Refs:
    def __init__(self, names, refs):
        for name, ref in zip(names, refs, strict=True):
            setattr(self, name, ref)


INPUTS = (
    "start",
    "q_hbm",
    "k_hbm",
    "v_hbm",
    "res_hbm",
    "op_hbm",
    "pp_hbm",
    "bias_hbm",
    "gain_hbm",
    "w_in_hbm",
    "w_out_hbm",
    "cot_hbm",
    "mask_hbm",
    "chain_hbm",
    "mask_flat_hbm",
    "chain_flat_hbm",
)
LOADS = (
    "k",
    "v",
    "pp",
    "q",
    "mask",
    "res",
    "chain",
    "bias",
    "gain",
    "w_in",
    "w_out",
    "op",
    "cot",
    "mask_flat",
    "chain_flat",
)


class PairGroup:
    def __init__(self, r, rows, columns, first):
        self.r, self.rows, self.columns, self.first = r, rows, columns, first

    def norm_and_hidden(self):
        r, rows, columns = self.r, self.rows, self.columns
        gain = r.gain[...]
        self.lefts = [r.ab[pl.ds(columns + t, 1), :] for t in rows]
        right = r.ab[pl.ds(0, columns), :]
        spread = jnp.concatenate([jnp.broadcast_to(left, (E, E)) for left in self.lefts], axis=0)
        dots = nt(right.astype(BF), spread.astype(BF)) * (1.0 / E)
        centres = []
        for j, t in enumerate(rows):
            same = r.chain_column[...] == r.chain_flat[self.first + t].astype(F32)
            seed = self.lefts[j] * right + jnp.where(same, r.bias[1:2, :], r.bias[0:1, :])
            mean = dots[:, j * E : (j + 1) * E] + jnp.where(
                same, r.bias_mean[1:2, :], r.bias_mean[0:1, :]
            )
            centres.append(seed - mean)
        self.inverses = [
            lax.rsqrt(jnp.mean(c * c, axis=1, keepdims=True) + 1e-05) for c in centres
        ]
        self.normeds = [c * inverse for c, inverse in zip(centres, self.inverses)]
        scaled = jnp.concatenate([(n * gain).astype(BF) for n in self.normeds], axis=0)
        self.half = nn(scaled, r.w_half[...])

    def activate(self):
        r = self.r
        d_act = jnp.concatenate([r.d_act[t] for t in self.rows], axis=0)
        half = self.half.astype(D_ACT)
        turned = jnp.tanh(half)
        raised = 1.0 + turned
        act = half * raised
        d_hidden = (d_act * (raised + act * (1.0 - turned))).astype(BF)
        act = act.astype(BF)
        for j, t in enumerate(self.rows):
            r.act[t] = act[j * self.columns : (j + 1) * self.columns]
        self.d_scaled = nt(d_hidden, r.w_in[...])

    def finish(self, total):
        r, columns = self.r, self.columns
        gain = r.gain[...]
        for j, t in enumerate(self.rows):
            live = r.mask_flat[self.first + t].astype(F32)
            block = slice(j * columns, (j + 1) * columns)
            d_normed = self.d_scaled[block] * gain
            both = jnp.concatenate([d_normed, d_normed * self.normeds[j]], axis=1).astype(BF)
            both = nn(both, r.means[...])
            d_seed = r.cot[t].astype(F32) + self.inverses[j] * (
                d_normed - both[:, :E] - self.normeds[j] * both[:, E:]
            )
            total = total + d_seed * (self.lefts[j] * live)
            r.grads[pl.ds(columns + t, 1), :] = live * jnp.sum(
                d_seed * r.right_live[...], axis=0, keepdims=True
            )
        return total


def pair_tile(r, tile, columns, first):
    per = min(4, tile)
    groups = [
        PairGroup(r, range(at, at + per), columns, first) for at in range(0, tile, per)
    ]
    total = jnp.zeros((columns, E), F32)
    for i in range(len(groups) + 2):
        if i < len(groups):
            groups[i].norm_and_hidden()
        if 0 <= i - 1 < len(groups):
            groups[i - 1].activate()
        if i >= 2:
            total = groups[i - 2].finish(total)
    return total


def pair_results(r, tile, columns, first):
    right = r.ab[pl.ds(0, columns), :]
    for t in range(tile):
        same = r.chain_column[...] == r.chain_flat[first + t].astype(F32)
        live = r.mask_flat[first + t].astype(F32)
        seed = r.ab[pl.ds(columns + t, 1), :] * right + jnp.where(
            same, r.bias[1:2, :], r.bias[0:1, :]
        )
        y = nn(r.act[t], r.w_out[...])
        r.out[t] = ((seed + y) * (r.live_column[...] * live)).astype(BF)


def kernel(sizes, names, *refs):
    r = Refs(names, refs)
    me = Place(sizes)
    nz, pr, pc, np_ = me.nz, me.pr, me.pc, me.np
    z, q = me.z, me.q
    rb = r.q.shape[0]
    fd = r.pp.shape[0]
    group = group_of(nz)
    wz = W // group
    columns = 8 * np_
    slab_plane = 2 * np_
    slab_tile = slab_plane // pr
    log_np = bits(np_)

    barrier = pltpu.get_barrier_semaphore()
    loads = {}
    for i, name in enumerate(LOADS):
        target = getattr(r, name)
        if name in ("k", "v"):
            target = target.at[z]
        loads[name] = pltpu.make_async_copy(getattr(r, name + "_hbm"), target, r.load_sem.at[i])
    for name in LOADS[:3]:
        loads[name].start()
    me.signal_all(barrier)
    for name in LOADS[3:]:
        loads[name].start()
    me.wait_all(barrier)

    furthest = (nz // 2, nz - 1 - nz // 2, nz - 1 - nz // 2, nz // 2)

    def ring(chain, distance, hop):
        buf = r.k if chain < 2 else r.v
        way = 1 if chain % 2 == 0 else -1
        block = lax.rem(z - way * (distance - hop) + nz, nz)
        peer = lax.rem(z + way * hop + nz, nz)
        own = r.k_hbm if chain < 2 else r.v_hbm
        return pltpu.make_async_remote_copy(
            src_ref=own if distance == hop else buf.at[block],
            dst_ref=buf.at[block],
            send_sem=r.ring_send.at[chain, distance - 1],
            recv_sem=r.ring_recv.at[chain, distance - 1],
            device_id=(peer, me.prow, me.pcol),
            device_id_type=MESH,
        )

    def pass_on(chain, held):
        for hop in (2, 1):
            if held + hop <= furthest[chain]:
                ring(chain, held + hop, hop).start()

    for chain in range(4):
        pass_on(chain, 0)

    loads["pp"].wait()
    row, column = grid_of(wz, W)
    piece = nt(one_hot(column == row + lax.rem(z, group) * wz), r.pp[...]).astype(BF)
    row, column = grid_of(fd, W)
    piece = nn(piece, one_hot(column == row + ((fd * q) & 127))).astype(BF)
    r.ppmsg[...] = piece
    r.ppg[q] = piece
    me.to_plane(lambda peer: r.ppmsg, r.ppg, r.send_sem.at[0], r.recv_sem.at[0])

    row, column = grid_of(8 * np_, rb)
    r.perm[...] = one_hot(column == (row & 3) * np_ + (row >> 3))
    loads["res"].wait()
    rows_twice = nt(r.perm[...], r.res[...]).astype(BF)
    both = nn(rows_twice, r.pp[...])
    row, column = grid_of(8 * np_, E)
    is_left = (row & 7) < 4
    r.presidual[...] = jnp.where(is_left, both[:, :E], both[:, E:])
    for name in ("q", "k", "v", "mask"):
        loads[name].wait()
    r.q_twice[...] = nn(r.perm[...], r.q[...]).astype(BF)

    scale = 1.0 / math.sqrt(E)

    def score(block):
        raw = nt(r.q_twice[...], r.k[block]) * scale
        live = r.mask[pl.ds(block, 1), :]
        r.scores[block] = jnp.where(live > 0, raw, -1e30)

    score(z)

    def arrive(chain, distance):
        if distance <= furthest[chain]:
            ring(chain, distance, 1 if distance % 2 else 2).wait_recv()
            if distance % 2 == 0:
                pass_on(chain, distance)

    def score_at(distance):
        if distance <= furthest[0]:
            score(lax.rem(z - distance + nz, nz))
        if distance <= furthest[1]:
            score(lax.rem(z + distance, nz))

    w0 = r.start[0] + z * slab_plane
    r0 = w0 + ((q - w0) & (np_ - 1))
    k0 = r0 >> log_np
    first = w0 + me.prow * slab_tile
    second_half = jnp.where(me.prow >= pr // 2, 1, 0)

    def make_w2():
        loads["op"].wait()
        wait_bytes(r.ppg, np_ - 1, r.recv_sem.at[0])
        total = jnp.zeros((E, wz), F32)
        for chunk in range(np_):
            at = ((fd * chunk) >> 7) << 7
            total = total + nt(r.op[:, at : at + W], r.ppg[chunk])
        row, column = grid_of(wz, wz)
        turned = nt(one_hot(row == column), total.astype(BF)).astype(BF)
        r.w2msg[...] = turned
        r.w2g[lax.rem(z, group)] = turned
        me.to_group(r.w2msg, r.w2g, r.send_sem.at[1], r.recv_sem.at[1])

    def make_picks():
        row, column = grid_of(pc * 16, 8 * nz)
        sub = row & 15
        right_hit = (sub < 8) & (column == (2 * (row >> 4) + (sub >> 2)) * 8 + 4 + (sub & 3))
        kk = k0 + (sub - 8)
        left_hit = ((sub == 8) | (sub == 9)) & (column == (kk >> 2) * 8 + (kk & 3))
        r.pick[...] = one_hot(right_hit | left_hit)
        row, column = grid_of(columns + slab_tile, 16 * np_)
        right_hit = (row < columns) & (column == (row & (np_ - 1)) * 16 + (row >> log_np))
        left_hit = (row >= columns) & (
            column == ((first + row - columns) & (np_ - 1)) * 16 + 8 + second_half
        )
        r.place_rows[...] = one_hot(right_hit | left_hit)
        row, column = grid_of(16 * np_, columns + slab_tile)
        sub = row & 15
        owner = row >> 4
        right_hit = (sub < 8) & (column == sub * np_ + owner)
        left_hit = (
            (sub == 8 + second_half)
            & (column >= columns)
            & (((first + column - columns) & (np_ - 1)) == owner)
        )
        r.spread_rows[...] = one_hot(right_hit | left_hit)

    def make_pair_constants():
        for name in ("chain", "bias", "gain", "w_in", "w_out", "mask_flat", "chain_flat"):
            loads[name].wait()
        r.w_half[...] = (r.w_in[...].astype(F32) * 0.5).astype(BF)
        r.w_out_half[...] = (r.w_out[...].astype(F32) * 0.5).astype(BF)
        row, column = grid_of(2 * E, 2 * E)
        r.means[...] = jnp.where((row >> 7) == (column >> 7), 1.0 / E, 0.0).astype(BF)
        r.bias_mean[...] = jnp.broadcast_to(jnp.mean(r.bias[...], axis=1, keepdims=True), (2, E))
        row, column = grid_of(rb, rb)
        unit = one_hot(row == column)
        for half in range(2):
            at = pl.ds(2 * me.pcol + half, 1)
            to = pl.ds(half * rb, rb)
            for source, target in ((r.mask, r.live_column), (r.chain, r.chain_column)):
                lanes = jnp.broadcast_to(source[at, :].astype(F32), (E, rb)).astype(BF)
                target[to, :] = nt(unit, lanes)

    def make_d_act(first_row, end_row):
        for t in range(first_row, end_row):
            r.d_act[t] = nt(r.cot[t], r.w_out_half[...]).astype(r.d_act.dtype)

    last = nz // 2
    third = max(1, slab_tile // 4)
    chores = {
        0: (make_pair_constants, make_picks),
        2: (lambda: loads["cot"].wait(), lambda: make_d_act(0, third)),
        4: (make_w2,),
        6: (lambda: make_d_act(third, slab_tile),),
    }
    for chore in chores[0]:
        chore()
    for distance in range(2, last, 2):
        for chain in range(4):
            arrive(chain, distance)
        for chore in chores.pop(distance, ()):
            chore()
        for near in (distance - 1, distance):
            if near % 2:
                for chain in range(2):
                    arrive(chain, near)
            score_at(near)
    for stage in (2, 4, 6):
        for chore in chores.pop(stage, ()):
            chore()
    for chain in (0, 1):
        arrive(chain, last)
        arrive(chain, last - 1)
    score_at(last - 1)
    score_at(last)

    top = r.scores[0]
    for b in range(1, nz):
        top = jnp.maximum(top, r.scores[b])
    top = jnp.max(top, axis=1, keepdims=True)
    def pair_of(distance):
        left = lax.rem(z - distance + nz, nz)
        return left, lax.rem(z + (distance if distance < last else 0), nz)

    below = jnp.zeros((8 * np_, rb), F32)
    for distance in range(1, last + 1):
        shifted = [jnp.exp(r.scores[b] - top) for b in pair_of(distance)]
        below = below + shifted[0] + shifted[1]
        r.weights[distance - 1] = jnp.concatenate(shifted, axis=1).astype(BF)
    below = 1.0 / jnp.sum(below, axis=1, keepdims=True)
    above = jnp.zeros((8 * np_, E), F32)
    for distance in range(1, last + 1):
        if distance % 2 or distance == last:
            for chain in (2, 3):
                arrive(chain, distance)
        both = jnp.concatenate([r.v[b] for b in pair_of(distance)], axis=0)
        above = above + nn(r.weights[distance - 1], both)
    attended = (above * below).astype(BF)
    wait_bytes(r.w2g, group - 1, r.recv_sem.at[1])
    both = nt(attended, r.w2g[...].reshape(W, E))
    terms = jnp.where(is_left, both[:, :E], both[:, E:]) + r.presidual[...]
    r.pmsg[...] = terms.reshape(np_, 8, E)
    me.to_plane(lambda peer: r.pmsg.at[peer], r.pbuf, r.send_sem.at[2], r.recv_sem.at[2])
    r.pbuf[q] = r.pmsg[q]
    wait_bytes(r.pbuf, np_ - 1, r.recv_sem.at[2])
    projected = jnp.sum(r.pbuf[...], axis=0).astype(BF).astype(F32)
    r.tmsg[...] = projected
    r.zbuf[z] = projected
    me.to_column(lambda peer: r.tmsg, r.zbuf, r.send_sem.at[3], r.recv_sem.at[3])
    wait_bytes(r.zbuf, nz - 1, r.recv_sem.at[3])
    chosen = nn(r.pick[...], r.zbuf[...].reshape(8 * nz, E).astype(BF)).astype(BF)
    r.msg[...] = chosen.reshape(pc, 16, E)
    me.to_plane(
        lambda peer: r.msg.at[lax.rem(peer, pc)], r.rbuf, r.send_sem.at[4], r.recv_sem.at[4]
    )
    r.rbuf[q] = r.msg[me.pcol]
    wait_bytes(r.rbuf, np_ - 1, r.recv_sem.at[4])
    r.ab[...] = nn(r.place_rows[...], r.rbuf[...].reshape(16 * np_, E))

    r.right_live[...] = r.ab[pl.ds(0, columns), :] * r.live_column[...]

    total = pair_tile(r, slab_tile, columns, first)
    r.grads[pl.ds(0, columns), :] = total * r.live_column[...]
    gathered = nn(r.spread_rows[...], r.grads[...].astype(BF)).astype(BF)
    r.gmsg[...] = gathered.reshape(np_, 16, E)
    me.to_plane(lambda peer: r.gmsg.at[peer], r.gbuf, r.send_sem.at[5], r.recv_sem.at[5])
    r.gbuf[q] = r.gmsg[q]
    pair_results(r, slab_tile, columns, first)
    store = pltpu.make_async_copy(r.out, r.out_hbm, r.store_sem)
    store.start()
    wait_bytes(r.gbuf, np_ - 1, r.recv_sem.at[5])
    by_column = jnp.sum(r.gbuf[...].astype(F32).reshape(pr, pc, 16, E), axis=0)
    over_columns = jnp.sum(by_column, axis=0)
    left0 = over_columns[8:9, :]
    left1 = over_columns[9:10, :]
    sub, _ = grid_of(8, E)
    for other in range(nz):
        k = 4 * other + (sub & 3)
        lefts = jnp.where(k == k0, left0, jnp.where(k == k0 + 1, left1, 0.0))
        r.zmsg[other] = jnp.where((sub >> 2) == other % 2, by_column[other // 2, 0:8, :], lefts)
    me.to_column(lambda peer: r.zmsg.at[peer], r.hbuf, r.send_sem.at[6], r.recv_sem.at[6])
    r.hbuf[z] = r.zmsg[z]
    wait_bytes(r.hbuf, nz - 1, r.recv_sem.at[6])
    tile = jnp.sum(r.hbuf[...], axis=0).astype(BF).astype(F32)
    r.fmsg[...] = tile
    r.fbuf[q] = tile
    me.to_plane(lambda peer: r.fmsg, r.fbuf, r.send_sem.at[7], r.recv_sem.at[7])
    odd = z & 1
    row, column = grid_of(rb, 8 * np_)
    base = (row & (np_ - 1)) * 8 + (row >> log_np)
    left_pick = one_hot(column == base + 4 * (1 - odd))
    right_pick = one_hot(column == base + 4 * odd)
    for chain in range(4):
        for distance in range(1, furthest[chain] + 1):
            ring(chain, distance, 1 if distance % 2 else 2).wait_send()
    wait_bytes(r.ppg, np_ - 1, r.send_sem.at[0])
    wait_bytes(r.w2g, group - 1, r.send_sem.at[1])
    wait_bytes(r.pbuf, np_ - 1, r.send_sem.at[2])
    wait_bytes(r.zbuf, nz - 1, r.send_sem.at[3])
    wait_bytes(r.rbuf, np_ - 1, r.send_sem.at[4])
    wait_bytes(r.gbuf, np_ - 1, r.send_sem.at[5])
    wait_bytes(r.hbuf, nz - 1, r.send_sem.at[6])
    wait_bytes(r.fbuf, np_ - 1, r.recv_sem.at[7])
    tiles = r.fbuf[...].reshape(8 * np_, E).astype(BF)
    store.wait()
    left = nn(left_pick, tiles).astype(BF)
    right = nn(right_pick, tiles).astype(BF)
    r.lm[...] = (nt(r.pp[:, :E], left) + nt(r.pp[:, E:], right)).astype(BF)
    wait_bytes(r.fbuf, np_ - 1, r.send_sem.at[7])


D_ACT = BF


def fused(sizes, start, operands):
    nz, pr, pc = sizes
    np_ = pr * pc
    q, k, v, res, op, pp, bias, gain, w_in, w_out, cot, mask, chain, mask_flat, chain_flat = operands
    rb = q.shape[0]
    columns = 8 * np_
    tile = 2 * np_ // pr
    group = group_of(nz)
    wz = W // group
    vmem, dma = pltpu.VMEM, pltpu.SemaphoreType.DMA
    steps = max(1, nz // 2)
    scratch = {
        "q": vmem(q.shape, BF),
        "k": vmem((nz, rb, E), BF),
        "v": vmem((nz, rb, E), BF),
        "res": vmem(res.shape, BF),
        "op": vmem(op.shape, BF),
        "pp": vmem(pp.shape, BF),
        "bias": vmem(bias.shape, F32),
        "gain": vmem(gain.shape, F32),
        "w_in": vmem(w_in.shape, BF),
        "w_out": vmem(w_out.shape, BF),
        "cot": vmem(cot.shape, BF),
        "mask": vmem(mask.shape, jnp.int32),
        "chain": vmem(chain.shape, jnp.int32),
        "mask_flat": pltpu.SMEM(mask_flat.shape, jnp.int32),
        "chain_flat": pltpu.SMEM(chain_flat.shape, jnp.int32),
        "scores": vmem((nz, 8 * np_, rb), F32),
        "q_twice": vmem((8 * np_, E), BF),
        "weights": vmem((steps, 8 * np_, 2 * rb), BF),
        "perm": vmem((8 * np_, rb), BF),
        "pick": vmem((pc * 16, 8 * nz), BF),
        "place_rows": vmem((columns + tile, 16 * np_), BF),
        "spread_rows": vmem((16 * np_, columns + tile), BF),
        "presidual": vmem((8 * np_, E), F32),
        "ppmsg": vmem((wz, W), BF),
        "ppg": vmem((np_, wz, W), BF),
        "w2msg": vmem((wz, E), BF),
        "w2g": vmem((group, wz, E), BF),
        "pmsg": vmem((np_, 8, E), F32),
        "pbuf": vmem((np_, 8, E), F32),
        "tmsg": vmem((8, E), F32),
        "zbuf": vmem((nz, 8, E), F32),
        "msg": vmem((pc, 16, E), BF),
        "rbuf": vmem((np_, 16, E), BF),
        "ab": vmem((columns + tile, E), F32),
        "out": vmem(cot.shape, BF),
        "store_sem": dma,
        "w_half": vmem(w_in.shape, BF),
        "w_out_half": vmem(w_out.shape, BF),
        "means": vmem((2 * E, 2 * E), BF),
        "bias_mean": vmem((2, E), F32),
        "live_column": vmem((columns, E), F32),
        "chain_column": vmem((columns, E), F32),
        "right_live": vmem((columns, E), F32),
        "act": vmem(cot.shape[:2] + w_in.shape[1:], BF),
        "d_act": vmem(cot.shape[:2] + w_in.shape[1:], D_ACT),
        "grads": vmem((columns + tile, E), F32),
        "gmsg": vmem((np_, 16, E), BF),
        "gbuf": vmem((np_, 16, E), BF),
        "zmsg": vmem((nz, 8, E), F32),
        "hbuf": vmem((nz, 8, E), F32),
        "fmsg": vmem((8, E), F32),
        "fbuf": vmem((np_, 8, E), F32),
        "load_sem": dma((len(LOADS),)),
        "ring_send": dma((4, steps)),
        "ring_recv": dma((4, steps)),
        "send_sem": dma((8,)),
        "recv_sem": dma((8,)),
    }
    hbm = pl.BlockSpec(memory_space=pltpu.HBM)
    return pl.pallas_call(
        functools.partial(kernel, sizes, INPUTS + ("out_hbm", "lm") + tuple(scratch)),
        out_shape=(
            jax.ShapeDtypeStruct(cot.shape, BF),
            jax.ShapeDtypeStruct((pp.shape[0], rb), BF),
        ),
        in_specs=[pl.BlockSpec(memory_space=pltpu.SMEM)] + [hbm] * len(operands),
        out_specs=(hbm, pl.BlockSpec(memory_space=pltpu.VMEM)),
        scratch_shapes=list(scratch.values()),
        compiler_params=pltpu.CompilerParams(
            collective_id=0, has_side_effects=True, vmem_limit_bytes=58 << 20
        ),
        name="attend_pair_and_gradient",
    )(start, *operands)


def store_kernel(out, lm, out_hbm, lm_hbm, out_vmem, lm_vmem, load_sem, save_sem):
    parts = load_sem.shape[0] - 1
    rows = out.shape[0] // parts
    ways = [(lm, lm_vmem, lm_hbm)]
    for i in range(parts):
        part = pl.ds(i * rows, rows)
        ways.append((out.at[part], out_vmem.at[part], out_hbm.at[part]))
    loads = [pltpu.make_async_copy(w[0], w[1], load_sem.at[i]) for i, w in enumerate(ways)]
    saves = [pltpu.make_async_copy(w[1], w[2], save_sem.at[i]) for i, w in enumerate(ways)]
    for load in loads:
        load.start()
    for load, save in zip(loads, saves):
        load.wait()
        save.start()
    for save in saves:
        save.wait()


def store(out, lm):
    parts = min(8, out.shape[0]) + 1
    return pl.pallas_call(
        store_kernel,
        out_shape=tuple(jax.ShapeDtypeStruct(a.shape, a.dtype) for a in (out, lm)),
        in_specs=[pl.BlockSpec(memory_space=pltpu.HBM)] * 2,
        out_specs=(pl.BlockSpec(memory_space=pltpu.HBM),) * 2,
        scratch_shapes=[
            pltpu.VMEM(out.shape, out.dtype),
            pltpu.VMEM(lm.shape, lm.dtype),
            pltpu.SemaphoreType.DMA((parts,)),
            pltpu.SemaphoreType.DMA((parts,)),
        ],
        compiler_params=pltpu.CompilerParams(vmem_limit_bytes=62 << 20),
        name="store_results",
    )(out, lm)


def body(
    sizes,
    queries,
    keys,
    values,
    residual,
    out_proj,
    pair_proj,
    chain_bias,
    ln_gain,
    w_in,
    w_out,
    pair_cot,
    residue_mask,
    chain_ids,
    slab_start,
):
    nz, rb = sizes[0], queries.shape[0]
    operands = (
        queries,
        keys,
        values,
        residual.T,
        out_proj,
        pair_proj,
        chain_bias,
        ln_gain.reshape(1, E),
        w_in,
        w_out,
        pair_cot,
        residue_mask.reshape(nz, rb),
        chain_ids.reshape(nz, rb),
        residue_mask,
        chain_ids,
    )
    pair_out, lm_grad = store(*fused(sizes, slab_start, operands))
    return pair_out, lm_grad.T


def solution(mesh):
    sizes = tuple(mesh.shape[name] for name in ("lm", "prow", "pcol"))
    return jax.shard_map(
        functools.partial(body, sizes),
        mesh=mesh,
        in_specs=(
            P("lm", ("prow", "pcol")),
            P("lm", ("prow", "pcol")),
            P("lm", ("prow", "pcol")),
            P("lm", ("prow", "pcol")),
            P(("prow", "pcol"), None),
            P(("prow", "pcol"), None),
            P(),
            P(),
            P(),
            P(),
            P(("lm", "prow"), "pcol", None),
            P(),
            P(),
            P(),
        ),
        out_specs=(P(("lm", "prow"), "pcol", None), P("lm", ("prow", "pcol"))),
        check_vma=False,
    )
```

```python
import functools
import math

import jax
import jax.numpy as jnp
from jax import lax
from jax.experimental import pallas as pl
from jax.experimental.pallas import tpu as pltpu
from jax.sharding import PartitionSpec as P

BF = jnp.bfloat16
F32 = jnp.float32
MESH = pl.DeviceIdType.MESH
E = 128
W = 256


def nn(a, b):
    return lax.dot_general(a, b, (((1,), (0,)), ((), ())), preferred_element_type=F32)


def nt(a, b):
    return lax.dot_general(a, b, (((1,), (1,)), ((), ())), preferred_element_type=F32)


def grid_of(rows, columns):
    row = lax.broadcasted_iota(jnp.int32, (rows, columns), 0)
    column = lax.broadcasted_iota(jnp.int32, (rows, columns), 1)
    return row, column


def one_hot(hit):
    return jnp.where(hit, 1.0, 0.0).astype(BF)


def bits(n):
    return n.bit_length() - 1


def plane_hops(pr, pc, m):
    if (pr, pc) != (4, 8):
        return 1
    ring = (0, 1, 2, 1)
    return ring[(m >> 1) & 3] + ring[((m & 1) << 1) | (m >> 4)]


def plane_order(pr, pc):
    return sorted(range(1, pr * pc), key=lambda m: -plane_hops(pr, pc, m))


def plane_greeted(pr, pc):
    return [m for m in plane_order(pr, pc) if plane_hops(pr, pc, m) <= 2]


def plane_witnesses(pr, pc):
    witnesses = [1, 4] if (pr, pc) == (4, 8) else []
    greeted = plane_greeted(pr, pc)
    for m in range(1, pr * pc):
        assert any(m ^ w in greeted or m == w for w in [0] + witnesses)
    return witnesses


def group_of(nz):
    return min(8, nz)


def z_order(nz):
    return sorted(range(1, nz), key=lambda i: -min(i, nz - i))


class Place:
    def __init__(self, sizes):
        self.nz, self.pr, self.pc = sizes
        self.np = self.pr * self.pc
        self.z = lax.axis_index("lm")
        self.prow = lax.axis_index("prow")
        self.pcol = lax.axis_index("pcol")
        self.q = self.prow * self.pc + self.pcol

    def plane_peer(self, m):
        prow = lax.bitwise_xor(self.prow, m // self.pc)
        pcol = lax.bitwise_xor(self.pcol, m % self.pc)
        return lax.bitwise_xor(self.q, m), (self.z, prow, pcol)

    def z_peer(self, i):
        peer = lax.rem(self.z + i, self.nz)
        return peer, (peer, self.prow, self.pcol)

    def near(self):
        return sorted({way * d % self.nz for d in (1, 2) for way in (1, -1)} - {0})

    def greeted(self):
        for i in self.near():
            yield self.z_peer(i)[1]
        for m in plane_greeted(self.pr, self.pc):
            yield self.plane_peer(m)[1]

    def signal_all(self, barrier):
        for device in self.greeted():
            pl.semaphore_signal(barrier, inc=1, device_id=device, device_id_type=MESH)

    def wait_all(self, barrier):
        pl.semaphore_wait(barrier, len(plane_greeted(self.pr, self.pc)) + len(self.near()))

    def send(self, source, target, send_sem, recv_sem, device):
        pltpu.make_async_remote_copy(
            src_ref=source,
            dst_ref=target,
            send_sem=send_sem,
            recv_sem=recv_sem,
            device_id=device,
            device_id_type=MESH,
        ).start()

    def to_plane(self, source, target, send_sem, recv_sem):
        for m in plane_order(self.pr, self.pc):
            peer, device = self.plane_peer(m)
            self.send(source(peer), target.at[self.q], send_sem, recv_sem, device)

    def to_group(self, source, target, send_sem, recv_sem):
        group = group_of(self.nz)
        slot = lax.rem(self.z, group)
        for i in range(-(group // 2), group // 2):
            if i:
                device = self.z_peer(i % self.nz)[1]
                self.send(source, target.at[slot], send_sem, recv_sem, device)

    def to_column(self, source, target, send_sem, recv_sem):
        for i in z_order(self.nz):
            peer, device = self.z_peer(i)
            self.send(source(peer), target.at[self.z], send_sem, recv_sem, device)


def wait_bytes(buffer, count, sem):
    part = buffer.at[pl.ds(0, count)]
    pltpu.make_async_copy(part, part, sem).wait()


class Refs:
    def __init__(self, names, refs):
        for name, ref in zip(names, refs, strict=True):
            setattr(self, name, ref)


INPUTS = (
    "start",
    "q_hbm",
    "k_hbm",
    "v_hbm",
    "res_hbm",
    "op_hbm",
    "pp_hbm",
    "bias_hbm",
    "gain_hbm",
    "w_in_hbm",
    "w_out_hbm",
    "cot_hbm",
    "mask_hbm",
    "chain_hbm",
    "mask_flat_hbm",
    "chain_flat_hbm",
)
LOADS = (
    "k",
    "v",
    "pp",
    "q",
    "mask",
    "res",
    "chain",
    "bias",
    "gain",
    "w_in",
    "w_out",
    "op",
    "cot",
    "mask_flat",
    "chain_flat",
)


class PairGroup:
    def __init__(self, r, rows, columns, first):
        self.r, self.rows, self.columns, self.first = r, rows, columns, first

    def norm_and_hidden(self):
        r, rows, columns = self.r, self.rows, self.columns
        gain = r.gain[...]
        self.lefts = [r.ab[pl.ds(columns + t, 1), :] for t in rows]
        right = r.ab[pl.ds(0, columns), :]
        spread = jnp.concatenate([jnp.broadcast_to(left, (E, E)) for left in self.lefts], axis=0)
        dots = nt(right.astype(BF), spread.astype(BF)) * (1.0 / E)
        centres = []
        for j, t in enumerate(rows):
            same = r.chain_column[...] == r.chain_flat[self.first + t].astype(F32)
            seed = self.lefts[j] * right + jnp.where(same, r.bias[1:2, :], r.bias[0:1, :])
            mean = dots[:, j * E : (j + 1) * E] + jnp.where(
                same, r.bias_mean[1:2, :], r.bias_mean[0:1, :]
            )
            centres.append(seed - mean)
        self.inverses = [
            lax.rsqrt(jnp.mean(c * c, axis=1, keepdims=True) + 1e-05) for c in centres
        ]
        self.normeds = [c * inverse for c, inverse in zip(centres, self.inverses)]
        scaled = jnp.concatenate([(n * gain).astype(BF) for n in self.normeds], axis=0)
        self.half = nn(scaled, r.w_half[...])

    def activate(self):
        r = self.r
        d_act = jnp.concatenate([r.d_act[t] for t in self.rows], axis=0)
        half = self.half.astype(D_ACT)
        turned = jnp.tanh(half)
        raised = 1.0 + turned
        act = half * raised
        d_hidden = (d_act * (raised + act * (1.0 - turned))).astype(BF)
        act = act.astype(BF)
        for j, t in enumerate(self.rows):
            r.act[t] = act[j * self.columns : (j + 1) * self.columns]
        self.d_scaled = nt(d_hidden, r.w_in[...])

    def finish(self, total):
        r, columns = self.r, self.columns
        gain = r.gain[...]
        for j, t in enumerate(self.rows):
            live = r.mask_flat[self.first + t].astype(F32)
            block = slice(j * columns, (j + 1) * columns)
            d_normed = self.d_scaled[block] * gain
            both = jnp.concatenate([d_normed, d_normed * self.normeds[j]], axis=1).astype(BF)
            both = nn(both, r.means[...])
            d_seed = r.cot[t].astype(F32) + self.inverses[j] * (
                d_normed - both[:, :E] - self.normeds[j] * both[:, E:]
            )
            total = total + d_seed * (self.lefts[j] * live)
            r.grads[pl.ds(columns + t, 1), :] = live * jnp.sum(
                d_seed * r.right_live[...], axis=0, keepdims=True
            )
        return total


def pair_tile(r, tile, columns, first):
    per = min(4, tile)
    groups = [
        PairGroup(r, range(at, at + per), columns, first) for at in range(0, tile, per)
    ]
    total = jnp.zeros((columns, E), F32)
    for i in range(len(groups) + 2):
        if i < len(groups):
            groups[i].norm_and_hidden()
        if 0 <= i - 1 < len(groups):
            groups[i - 1].activate()
        if i >= 2:
            total = groups[i - 2].finish(total)
    return total


def pair_results(r, rows, columns, first):
    right = r.ab[pl.ds(0, columns), :]
    for t in rows:
        same = r.chain_column[...] == r.chain_flat[first + t].astype(F32)
        live = r.mask_flat[first + t].astype(F32)
        seed = r.ab[pl.ds(columns + t, 1), :] * right + jnp.where(
            same, r.bias[1:2, :], r.bias[0:1, :]
        )
        y = nn(r.act[t], r.w_out[...])
        r.out[t] = ((seed + y) * (r.live_column[...] * live)).astype(BF)


def kernel(sizes, names, *refs):
    r = Refs(names, refs)
    me = Place(sizes)
    nz, pr, pc, np_ = me.nz, me.pr, me.pc, me.np
    z, q = me.z, me.q
    rb = r.q.shape[0]
    fd = r.pp.shape[0]
    group = group_of(nz)
    wz = W // group
    columns = 8 * np_
    slab_plane = 2 * np_
    slab_tile = slab_plane // pr
    log_np = bits(np_)

    barrier = pltpu.get_barrier_semaphore()
    loads = {}
    for i, name in enumerate(LOADS):
        target = getattr(r, name)
        if name in ("k", "v"):
            target = target.at[z]
        loads[name] = pltpu.make_async_copy(getattr(r, name + "_hbm"), target, r.load_sem.at[i])
    for name in LOADS[:3]:
        loads[name].start()
    me.signal_all(barrier)
    for name in LOADS[3:]:
        loads[name].start()
    me.wait_all(barrier)

    furthest = (nz // 2, nz - 1 - nz // 2, nz - 1 - nz // 2, nz // 2)

    def ring(chain, distance, hop):
        buf = r.k if chain < 2 else r.v
        way = 1 if chain % 2 == 0 else -1
        block = lax.rem(z - way * (distance - hop) + nz, nz)
        peer = lax.rem(z + way * hop + nz, nz)
        own = r.k_hbm if chain < 2 else r.v_hbm
        return pltpu.make_async_remote_copy(
            src_ref=own if distance == hop else buf.at[block],
            dst_ref=buf.at[block],
            send_sem=r.ring_send.at[chain, distance - 1],
            recv_sem=r.ring_recv.at[chain, distance - 1],
            device_id=(peer, me.prow, me.pcol),
            device_id_type=MESH,
        )

    def pass_on(chain, held):
        for hop in (2, 1):
            if held + hop <= furthest[chain]:
                ring(chain, held + hop, hop).start()

    for chain in range(4):
        pass_on(chain, 0)

    witnesses = plane_witnesses(pr, pc)
    for m in witnesses:
        pl.semaphore_signal(
            r.known_sem, inc=1, device_id=me.plane_peer(m)[1], device_id_type=MESH
        )

    loads["pp"].wait()
    row, column = grid_of(wz, W)
    piece = nt(one_hot(column == row + lax.rem(z, group) * wz), r.pp[...]).astype(BF)
    row, column = grid_of(fd, W)
    piece = nn(piece, one_hot(column == row + ((fd * q) & 127))).astype(BF)
    r.ppmsg[...] = piece
    r.ppg[q] = piece

    row, column = grid_of(8 * np_, rb)
    r.perm[...] = one_hot(column == (row & 3) * np_ + (row >> 3))
    loads["res"].wait()
    rows_twice = nt(r.perm[...], r.res[...]).astype(BF)
    both = nn(rows_twice, r.pp[...])
    row, column = grid_of(8 * np_, E)
    is_left = (row & 7) < 4
    r.presidual[...] = jnp.where(is_left, both[:, :E], both[:, E:])
    for name in ("q", "k", "v", "mask"):
        loads[name].wait()
    r.q_twice[...] = nn(r.perm[...], r.q[...]).astype(BF)

    scale = 1.0 / math.sqrt(E)

    def score(block):
        raw = nt(r.q_twice[...], r.k[block]) * scale
        live = r.mask[pl.ds(block, 1), :]
        r.scores[block] = jnp.where(live > 0, raw, -1e30)

    score(z)
    if witnesses:
        pl.semaphore_wait(r.known_sem, len(witnesses))
    me.to_plane(lambda peer: r.ppmsg, r.ppg, r.send_sem.at[0], r.recv_sem.at[0])

    def arrive(chain, distance):
        if distance <= furthest[chain]:
            ring(chain, distance, 1 if distance % 2 else 2).wait_recv()
            if distance % 2 == 0:
                pass_on(chain, distance)

    def score_at(distance):
        if distance <= furthest[0]:
            score(lax.rem(z - distance + nz, nz))
        if distance <= furthest[1]:
            score(lax.rem(z + distance, nz))

    w0 = r.start[0] + z * slab_plane
    r0 = w0 + ((q - w0) & (np_ - 1))
    k0 = r0 >> log_np
    first = w0 + me.prow * slab_tile
    second_half = jnp.where(me.prow >= pr // 2, 1, 0)

    def make_w2():
        loads["op"].wait()
        wait_bytes(r.ppg, np_ - 1, r.recv_sem.at[0])
        total = jnp.zeros((E, wz), F32)
        for chunk in range(np_):
            at = ((fd * chunk) >> 7) << 7
            total = total + nt(r.op[:, at : at + W], r.ppg[chunk])
        row, column = grid_of(wz, wz)
        turned = nt(one_hot(row == column), total.astype(BF)).astype(BF)
        r.w2msg[...] = turned
        r.w2g[lax.rem(z, group)] = turned
        me.to_group(r.w2msg, r.w2g, r.send_sem.at[1], r.recv_sem.at[1])

    def make_picks():
        row, column = grid_of(pc * 16, 8 * nz)
        sub = row & 15
        right_hit = (sub < 8) & (column == (2 * (row >> 4) + (sub >> 2)) * 8 + 4 + (sub & 3))
        kk = k0 + (sub - 8)
        left_hit = ((sub == 8) | (sub == 9)) & (column == (kk >> 2) * 8 + (kk & 3))
        r.pick[...] = one_hot(right_hit | left_hit)
        row, column = grid_of(columns + slab_tile, 16 * np_)
        right_hit = (row < columns) & (column == (row & (np_ - 1)) * 16 + (row >> log_np))
        left_hit = (row >= columns) & (
            column == ((first + row - columns) & (np_ - 1)) * 16 + 8 + second_half
        )
        r.place_rows[...] = one_hot(right_hit | left_hit)
        row, column = grid_of(16 * np_, columns + slab_tile)
        sub = row & 15
        owner = row >> 4
        right_hit = (sub < 8) & (column == sub * np_ + owner)
        left_hit = (
            (sub == 8 + second_half)
            & (column >= columns)
            & (((first + column - columns) & (np_ - 1)) == owner)
        )
        r.spread_rows[...] = one_hot(right_hit | left_hit)

    def make_pair_constants():
        for name in ("chain", "bias", "gain", "w_in", "w_out", "mask_flat", "chain_flat"):
            loads[name].wait()
        r.w_half[...] = (r.w_in[...].astype(F32) * 0.5).astype(BF)
        r.w_out_half[...] = (r.w_out[...].astype(F32) * 0.5).astype(BF)
        row, column = grid_of(2 * E, 2 * E)
        r.means[...] = jnp.where((row >> 7) == (column >> 7), 1.0 / E, 0.0).astype(BF)
        r.bias_mean[...] = jnp.broadcast_to(jnp.mean(r.bias[...], axis=1, keepdims=True), (2, E))
        row, column = grid_of(rb, rb)
        unit = one_hot(row == column)
        for half in range(2):
            at = pl.ds(2 * me.pcol + half, 1)
            to = pl.ds(half * rb, rb)
            for source, target in ((r.mask, r.live_column), (r.chain, r.chain_column)):
                lanes = jnp.broadcast_to(source[at, :].astype(F32), (E, rb)).astype(BF)
                target[to, :] = nt(unit, lanes)

    def make_d_act(first_row, end_row):
        for t in range(first_row, end_row):
            r.d_act[t] = nt(r.cot[t], r.w_out_half[...]).astype(r.d_act.dtype)

    last = nz // 2
    third = max(1, slab_tile // 4)
    chores = {
        0: (make_pair_constants, make_picks),
        2: (lambda: loads["cot"].wait(), lambda: make_d_act(0, third)),
        4: (make_w2,),
        6: (lambda: make_d_act(third, slab_tile),),
    }
    for chore in chores[0]:
        chore()
    for distance in range(2, last, 2):
        for chain in range(4):
            arrive(chain, distance)
        for near in (distance - 1, distance):
            if near % 2:
                for chain in range(2):
                    arrive(chain, near)
            score_at(near)
        for chore in chores.pop(distance, ()):
            chore()
    for stage in (2, 4, 6):
        for chore in chores.pop(stage, ()):
            chore()
    for chain in (0, 1):
        arrive(chain, last)
        arrive(chain, last - 1)
    score_at(last - 1)
    score_at(last)

    top = r.scores[0]
    for b in range(1, nz):
        top = jnp.maximum(top, r.scores[b])
    top = jnp.max(top, axis=1, keepdims=True)
    def pair_of(distance):
        left = lax.rem(z - distance + nz, nz)
        return left, lax.rem(z + (distance if distance < last else 0), nz)

    below = jnp.zeros((8 * np_, rb), F32)
    for distance in range(1, last + 1):
        shifted = [jnp.exp(r.scores[b] - top) for b in pair_of(distance)]
        below = below + shifted[0] + shifted[1]
        r.weights[distance - 1] = jnp.concatenate(shifted, axis=1).astype(BF)
    below = 1.0 / jnp.sum(below, axis=1, keepdims=True)
    above = jnp.zeros((8 * np_, E), F32)
    for distance in range(1, last + 1):
        if distance % 2 or distance == last:
            for chain in (2, 3):
                arrive(chain, distance)
        both = jnp.concatenate([r.v[b] for b in pair_of(distance)], axis=0)
        above = above + nn(r.weights[distance - 1], both)
    attended = (above * below).astype(BF)
    wait_bytes(r.w2g, group - 1, r.recv_sem.at[1])
    both = nt(attended, r.w2g[...].reshape(W, E))
    terms = jnp.where(is_left, both[:, :E], both[:, E:]) + r.presidual[...]
    r.pmsg[...] = terms.reshape(np_, 8, E)
    me.to_plane(lambda peer: r.pmsg.at[peer], r.pbuf, r.send_sem.at[2], r.recv_sem.at[2])
    r.pbuf[q] = r.pmsg[q]
    wait_bytes(r.pbuf, np_ - 1, r.recv_sem.at[2])
    projected = jnp.sum(r.pbuf[...], axis=0).astype(BF).astype(F32)
    r.tmsg[...] = projected
    r.zbuf[z] = projected
    me.to_column(lambda peer: r.tmsg, r.zbuf, r.send_sem.at[3], r.recv_sem.at[3])
    wait_bytes(r.zbuf, nz - 1, r.recv_sem.at[3])
    chosen = nn(r.pick[...], r.zbuf[...].reshape(8 * nz, E).astype(BF)).astype(BF)
    r.msg[...] = chosen.reshape(pc, 16, E)
    me.to_plane(
        lambda peer: r.msg.at[lax.rem(peer, pc)], r.rbuf, r.send_sem.at[4], r.recv_sem.at[4]
    )
    r.rbuf[q] = r.msg[me.pcol]
    wait_bytes(r.rbuf, np_ - 1, r.recv_sem.at[4])
    r.ab[...] = nn(r.place_rows[...], r.rbuf[...].reshape(16 * np_, E))

    r.right_live[...] = r.ab[pl.ds(0, columns), :] * r.live_column[...]

    total = pair_tile(r, slab_tile, columns, first)
    r.grads[pl.ds(0, columns), :] = total * r.live_column[...]
    gathered = nn(r.spread_rows[...], r.grads[...].astype(BF)).astype(BF)
    r.gmsg[...] = gathered.reshape(np_, 16, E)
    me.to_plane(lambda peer: r.gmsg.at[peer], r.gbuf, r.send_sem.at[5], r.recv_sem.at[5])
    r.gbuf[q] = r.gmsg[q]
    split = slab_tile * 3 // 8
    pair_results(r, range(split), columns, first)
    wait_bytes(r.gbuf, np_ - 1, r.recv_sem.at[5])
    by_column = jnp.sum(r.gbuf[...].astype(F32).reshape(pr, pc, 16, E), axis=0)
    over_columns = jnp.sum(by_column, axis=0)
    left0 = over_columns[8:9, :]
    left1 = over_columns[9:10, :]
    sub, _ = grid_of(8, E)
    for other in range(nz):
        k = 4 * other + (sub & 3)
        lefts = jnp.where(k == k0, left0, jnp.where(k == k0 + 1, left1, 0.0))
        r.zmsg[other] = jnp.where((sub >> 2) == other % 2, by_column[other // 2, 0:8, :], lefts)
    me.to_column(lambda peer: r.zmsg.at[peer], r.hbuf, r.send_sem.at[6], r.recv_sem.at[6])
    r.hbuf[z] = r.zmsg[z]
    pair_results(r, range(split, slab_tile), columns, first)
    store = pltpu.make_async_copy(r.out, r.out_hbm, r.store_sem)
    store.start()
    wait_bytes(r.hbuf, nz - 1, r.recv_sem.at[6])
    tile = jnp.sum(r.hbuf[...], axis=0).astype(BF).astype(F32)
    r.fmsg[...] = tile
    r.fbuf[q] = tile
    me.to_plane(lambda peer: r.fmsg, r.fbuf, r.send_sem.at[7], r.recv_sem.at[7])
    odd = z & 1
    row, column = grid_of(rb, 8 * np_)
    base = (row & (np_ - 1)) * 8 + (row >> log_np)
    left_pick = one_hot(column == base + 4 * (1 - odd))
    right_pick = one_hot(column == base + 4 * odd)
    for chain in range(4):
        for distance in range(1, furthest[chain] + 1):
            ring(chain, distance, 1 if distance % 2 else 2).wait_send()
    wait_bytes(r.ppg, np_ - 1, r.send_sem.at[0])
    wait_bytes(r.w2g, group - 1, r.send_sem.at[1])
    wait_bytes(r.pbuf, np_ - 1, r.send_sem.at[2])
    wait_bytes(r.zbuf, nz - 1, r.send_sem.at[3])
    wait_bytes(r.rbuf, np_ - 1, r.send_sem.at[4])
    wait_bytes(r.gbuf, np_ - 1, r.send_sem.at[5])
    wait_bytes(r.hbuf, nz - 1, r.send_sem.at[6])
    wait_bytes(r.fbuf, np_ - 1, r.recv_sem.at[7])
    tiles = r.fbuf[...].reshape(8 * np_, E).astype(BF)
    store.wait()
    left = nn(left_pick, tiles).astype(BF)
    right = nn(right_pick, tiles).astype(BF)
    r.lm[...] = (nt(r.pp[:, :E], left) + nt(r.pp[:, E:], right)).astype(BF)
    wait_bytes(r.fbuf, np_ - 1, r.send_sem.at[7])


D_ACT = BF


def fused(sizes, start, operands):
    nz, pr, pc = sizes
    np_ = pr * pc
    q, k, v, res, op, pp, bias, gain, w_in, w_out, cot, mask, chain, mask_flat, chain_flat = operands
    rb = q.shape[0]
    columns = 8 * np_
    tile = 2 * np_ // pr
    group = group_of(nz)
    wz = W // group
    vmem, dma = pltpu.VMEM, pltpu.SemaphoreType.DMA
    steps = max(1, nz // 2)
    scratch = {
        "q": vmem(q.shape, BF),
        "k": vmem((nz, rb, E), BF),
        "v": vmem((nz, rb, E), BF),
        "res": vmem(res.shape, BF),
        "op": vmem(op.shape, BF),
        "pp": vmem(pp.shape, BF),
        "bias": vmem(bias.shape, F32),
        "gain": vmem(gain.shape, F32),
        "w_in": vmem(w_in.shape, BF),
        "w_out": vmem(w_out.shape, BF),
        "cot": vmem(cot.shape, BF),
        "mask": vmem(mask.shape, jnp.int32),
        "chain": vmem(chain.shape, jnp.int32),
        "mask_flat": pltpu.SMEM(mask_flat.shape, jnp.int32),
        "chain_flat": pltpu.SMEM(chain_flat.shape, jnp.int32),
        "scores": vmem((nz, 8 * np_, rb), F32),
        "q_twice": vmem((8 * np_, E), BF),
        "weights": vmem((steps, 8 * np_, 2 * rb), BF),
        "perm": vmem((8 * np_, rb), BF),
        "pick": vmem((pc * 16, 8 * nz), BF),
        "place_rows": vmem((columns + tile, 16 * np_), BF),
        "spread_rows": vmem((16 * np_, columns + tile), BF),
        "presidual": vmem((8 * np_, E), F32),
        "ppmsg": vmem((wz, W), BF),
        "ppg": vmem((np_, wz, W), BF),
        "w2msg": vmem((wz, E), BF),
        "w2g": vmem((group, wz, E), BF),
        "pmsg": vmem((np_, 8, E), F32),
        "pbuf": vmem((np_, 8, E), F32),
        "tmsg": vmem((8, E), F32),
        "zbuf": vmem((nz, 8, E), F32),
        "msg": vmem((pc, 16, E), BF),
        "rbuf": vmem((np_, 16, E), BF),
        "ab": vmem((columns + tile, E), F32),
        "out": vmem(cot.shape, BF),
        "store_sem": dma,
        "w_half": vmem(w_in.shape, BF),
        "w_out_half": vmem(w_out.shape, BF),
        "means": vmem((2 * E, 2 * E), BF),
        "bias_mean": vmem((2, E), F32),
        "live_column": vmem((columns, E), F32),
        "chain_column": vmem((columns, E), F32),
        "right_live": vmem((columns, E), F32),
        "act": vmem(cot.shape[:2] + w_in.shape[1:], BF),
        "d_act": vmem(cot.shape[:2] + w_in.shape[1:], D_ACT),
        "grads": vmem((columns + tile, E), F32),
        "gmsg": vmem((np_, 16, E), BF),
        "gbuf": vmem((np_, 16, E), BF),
        "zmsg": vmem((nz, 8, E), F32),
        "hbuf": vmem((nz, 8, E), F32),
        "fmsg": vmem((8, E), F32),
        "fbuf": vmem((np_, 8, E), F32),
        "known_sem": pltpu.SemaphoreType.REGULAR,
        "load_sem": dma((len(LOADS),)),
        "ring_send": dma((4, steps)),
        "ring_recv": dma((4, steps)),
        "send_sem": dma((8,)),
        "recv_sem": dma((8,)),
    }
    hbm = pl.BlockSpec(memory_space=pltpu.HBM)
    return pl.pallas_call(
        functools.partial(kernel, sizes, INPUTS + ("out_hbm", "lm") + tuple(scratch)),
        out_shape=(
            jax.ShapeDtypeStruct(cot.shape, BF),
            jax.ShapeDtypeStruct((pp.shape[0], rb), BF),
        ),
        in_specs=[pl.BlockSpec(memory_space=pltpu.SMEM)] + [hbm] * len(operands),
        out_specs=(hbm, pl.BlockSpec(memory_space=pltpu.VMEM)),
        scratch_shapes=list(scratch.values()),
        compiler_params=pltpu.CompilerParams(
            collective_id=0, has_side_effects=True, vmem_limit_bytes=58 << 20
        ),
        name="attend_pair_and_gradient",
    )(start, *operands)


def store_kernel(out, lm, out_hbm, lm_hbm, out_vmem, lm_vmem, load_sem, save_sem):
    parts = load_sem.shape[0] - 1
    rows = out.shape[0] // parts
    ways = [(lm, lm_vmem, lm_hbm)]
    for i in range(parts):
        part = pl.ds(i * rows, rows)
        ways.append((out.at[part], out_vmem.at[part], out_hbm.at[part]))
    loads = [pltpu.make_async_copy(w[0], w[1], load_sem.at[i]) for i, w in enumerate(ways)]
    saves = [pltpu.make_async_copy(w[1], w[2], save_sem.at[i]) for i, w in enumerate(ways)]
    for load in loads:
        load.start()
    for load, save in zip(loads, saves):
        load.wait()
        save.start()
    for save in saves:
        save.wait()


def store(out, lm):
    parts = min(8, out.shape[0]) + 1
    return pl.pallas_call(
        store_kernel,
        out_shape=tuple(jax.ShapeDtypeStruct(a.shape, a.dtype) for a in (out, lm)),
        in_specs=[pl.BlockSpec(memory_space=pltpu.HBM)] * 2,
        out_specs=(pl.BlockSpec(memory_space=pltpu.HBM),) * 2,
        scratch_shapes=[
            pltpu.VMEM(out.shape, out.dtype),
            pltpu.VMEM(lm.shape, lm.dtype),
            pltpu.SemaphoreType.DMA((parts,)),
            pltpu.SemaphoreType.DMA((parts,)),
        ],
        compiler_params=pltpu.CompilerParams(vmem_limit_bytes=62 << 20),
        name="store_results",
    )(out, lm)


def body(
    sizes,
    queries,
    keys,
    values,
    residual,
    out_proj,
    pair_proj,
    chain_bias,
    ln_gain,
    w_in,
    w_out,
    pair_cot,
    residue_mask,
    chain_ids,
    slab_start,
):
    nz, rb = sizes[0], queries.shape[0]
    operands = (
        queries,
        keys,
        values,
        residual.T,
        out_proj,
        pair_proj,
        chain_bias,
        ln_gain.reshape(1, E),
        w_in,
        w_out,
        pair_cot,
        residue_mask.reshape(nz, rb),
        chain_ids.reshape(nz, rb),
        residue_mask,
        chain_ids,
    )
    pair_out, lm_grad = store(*fused(sizes, slab_start, operands))
    return pair_out, lm_grad.T


def solution(mesh):
    sizes = tuple(mesh.shape[name] for name in ("lm", "prow", "pcol"))
    return jax.shard_map(
        functools.partial(body, sizes),
        mesh=mesh,
        in_specs=(
            P("lm", ("prow", "pcol")),
            P("lm", ("prow", "pcol")),
            P("lm", ("prow", "pcol")),
            P("lm", ("prow", "pcol")),
            P(("prow", "pcol"), None),
            P(("prow", "pcol"), None),
            P(),
            P(),
            P(),
            P(),
            P(("lm", "prow"), "pcol", None),
            P(),
            P(),
            P(),
        ),
        out_specs=(P(("lm", "prow"), "pcol", None), P("lm", ("prow", "pcol"))),
        check_vma=False,
    )
```

```python
import functools
import math

import jax
import jax.numpy as jnp
from jax import lax
from jax.experimental import pallas as pl
from jax.experimental.pallas import tpu as pltpu
from jax.sharding import PartitionSpec as P

BF = jnp.bfloat16
F32 = jnp.float32
MESH = pl.DeviceIdType.MESH
E = 128
W = 256


def nn(a, b):
    return lax.dot_general(a, b, (((1,), (0,)), ((), ())), preferred_element_type=F32)


def nt(a, b):
    return lax.dot_general(a, b, (((1,), (1,)), ((), ())), preferred_element_type=F32)


def grid_of(rows, columns):
    row = lax.broadcasted_iota(jnp.int32, (rows, columns), 0)
    column = lax.broadcasted_iota(jnp.int32, (rows, columns), 1)
    return row, column


def one_hot(hit):
    return jnp.where(hit, 1.0, 0.0).astype(BF)


def bits(n):
    return n.bit_length() - 1


def plane_hops(pr, pc, m):
    if (pr, pc) != (4, 8):
        return 1
    ring = (0, 1, 2, 1)
    return ring[(m >> 1) & 3] + ring[((m & 1) << 1) | (m >> 4)]


def plane_order(pr, pc):
    return sorted(range(1, pr * pc), key=lambda m: -plane_hops(pr, pc, m))


def plane_greeted(pr, pc):
    return [m for m in plane_order(pr, pc) if plane_hops(pr, pc, m) <= 2]


def plane_witnesses(pr, pc):
    witnesses = [1, 4] if (pr, pc) == (4, 8) else []
    greeted = plane_greeted(pr, pc)
    for m in range(1, pr * pc):
        assert any(m ^ w in greeted or m == w for w in [0] + witnesses)
    return witnesses


def group_of(nz):
    return min(8, nz)


def z_order(nz):
    return sorted(range(1, nz), key=lambda i: -min(i, nz - i))


class Place:
    def __init__(self, sizes):
        self.nz, self.pr, self.pc = sizes
        self.np = self.pr * self.pc
        self.z = lax.axis_index("lm")
        self.prow = lax.axis_index("prow")
        self.pcol = lax.axis_index("pcol")
        self.q = self.prow * self.pc + self.pcol

    def plane_peer(self, m):
        prow = lax.bitwise_xor(self.prow, m // self.pc)
        pcol = lax.bitwise_xor(self.pcol, m % self.pc)
        return lax.bitwise_xor(self.q, m), (self.z, prow, pcol)

    def z_peer(self, i):
        peer = lax.rem(self.z + i, self.nz)
        return peer, (peer, self.prow, self.pcol)

    def near(self):
        return sorted({way * d % self.nz for d in (1, 2) for way in (1, -1)} - {0})

    def greeted(self):
        for i in self.near():
            yield self.z_peer(i)[1]
        for m in plane_greeted(self.pr, self.pc):
            yield self.plane_peer(m)[1]

    def signal_all(self, barrier):
        for device in self.greeted():
            pl.semaphore_signal(barrier, inc=1, device_id=device, device_id_type=MESH)

    def wait_all(self, barrier):
        pl.semaphore_wait(barrier, len(plane_greeted(self.pr, self.pc)) + len(self.near()))

    def send(self, source, target, send_sem, recv_sem, device):
        pltpu.make_async_remote_copy(
            src_ref=source,
            dst_ref=target,
            send_sem=send_sem,
            recv_sem=recv_sem,
            device_id=device,
            device_id_type=MESH,
        ).start()

    def to_plane(self, source, target, send_sem, recv_sem):
        for m in plane_order(self.pr, self.pc):
            peer, device = self.plane_peer(m)
            self.send(source(peer), target.at[self.q], send_sem, recv_sem, device)

    def to_group(self, source, target, send_sem, recv_sem):
        group = group_of(self.nz)
        slot = lax.rem(self.z, group)
        for i in range(-(group // 2), group // 2):
            if i:
                device = self.z_peer(i % self.nz)[1]
                self.send(source, target.at[slot], send_sem, recv_sem, device)

    def to_column(self, source, target, send_sem, recv_sem):
        for i in z_order(self.nz):
            peer, device = self.z_peer(i)
            self.send(source(peer), target.at[self.z], send_sem, recv_sem, device)


def wait_bytes(buffer, count, sem):
    part = buffer.at[pl.ds(0, count)]
    pltpu.make_async_copy(part, part, sem).wait()


class Refs:
    def __init__(self, names, refs):
        for name, ref in zip(names, refs, strict=True):
            setattr(self, name, ref)


INPUTS = (
    "start",
    "q_hbm",
    "k_hbm",
    "v_hbm",
    "res_hbm",
    "op_hbm",
    "pp_hbm",
    "bias_hbm",
    "gain_hbm",
    "w_in_hbm",
    "w_out_hbm",
    "cot_hbm",
    "mask_hbm",
    "chain_hbm",
    "mask_flat_hbm",
    "chain_flat_hbm",
)
LOADS = (
    "k",
    "v",
    "pp",
    "q",
    "mask",
    "res",
    "chain",
    "bias",
    "gain",
    "w_in",
    "w_out",
    "op",
    "cot",
    "mask_flat",
    "chain_flat",
)


class PairGroup:
    def __init__(self, r, rows, columns, first):
        self.r, self.rows, self.columns, self.first = r, rows, columns, first

    def norm_and_hidden(self):
        r, rows, columns = self.r, self.rows, self.columns
        gain = r.gain[...]
        self.lefts = [r.ab[pl.ds(columns + t, 1), :] for t in rows]
        right = r.ab[pl.ds(0, columns), :]
        spread = jnp.concatenate([jnp.broadcast_to(left, (E, E)) for left in self.lefts], axis=0)
        dots = nt(right.astype(BF), spread.astype(BF)) * (1.0 / E)
        centres = []
        for j, t in enumerate(rows):
            same = r.chain_column[...] == r.chain_flat[self.first + t].astype(F32)
            seed = self.lefts[j] * right + jnp.where(same, r.bias[1:2, :], r.bias[0:1, :])
            mean = dots[:, j * E : (j + 1) * E] + jnp.where(
                same, r.bias_mean[1:2, :], r.bias_mean[0:1, :]
            )
            centres.append(seed - mean)
        self.inverses = [
            lax.rsqrt(jnp.mean(c * c, axis=1, keepdims=True) + 1e-05) for c in centres
        ]
        self.normeds = [c * inverse for c, inverse in zip(centres, self.inverses)]
        scaled = jnp.concatenate([(n * gain).astype(BF) for n in self.normeds], axis=0)
        self.half = nn(scaled, r.w_half[...])

    def activate(self):
        r = self.r
        d_act = jnp.concatenate([r.d_act[t] for t in self.rows], axis=0)
        half = self.half.astype(D_ACT)
        turned = jnp.tanh(half)
        raised = 1.0 + turned
        act = half * raised
        d_hidden = (d_act * (raised + act * (1.0 - turned))).astype(BF)
        act = act.astype(BF)
        for j, t in enumerate(self.rows):
            r.act[t] = act[j * self.columns : (j + 1) * self.columns]
        self.d_scaled = nt(d_hidden, r.w_in[...])

    def finish(self, total):
        r, columns = self.r, self.columns
        gain = r.gain[...]
        for j, t in enumerate(self.rows):
            live = r.mask_flat[self.first + t].astype(F32)
            block = slice(j * columns, (j + 1) * columns)
            d_normed = self.d_scaled[block] * gain
            both = jnp.concatenate([d_normed, d_normed * self.normeds[j]], axis=1).astype(BF)
            both = nn(both, r.means[...])
            d_seed = r.cot[t].astype(F32) + self.inverses[j] * (
                d_normed - both[:, :E] - self.normeds[j] * both[:, E:]
            )
            total = total + d_seed * (self.lefts[j] * live)
            r.grads[pl.ds(columns + t, 1), :] = live * jnp.sum(
                d_seed * r.right_live[...], axis=0, keepdims=True
            )
        return total


def pair_tile(r, tile, columns, first):
    per = min(4, tile)
    groups = [
        PairGroup(r, range(at, at + per), columns, first) for at in range(0, tile, per)
    ]
    total = jnp.zeros((columns, E), F32)
    for i in range(len(groups) + 2):
        if i < len(groups):
            groups[i].norm_and_hidden()
        if 0 <= i - 1 < len(groups):
            groups[i - 1].activate()
        if i >= 2:
            total = groups[i - 2].finish(total)
    return total


def pair_results(r, rows, columns, first):
    right = r.ab[pl.ds(0, columns), :]
    for t in rows:
        same = r.chain_column[...] == r.chain_flat[first + t].astype(F32)
        live = r.mask_flat[first + t].astype(F32)
        seed = r.ab[pl.ds(columns + t, 1), :] * right + jnp.where(
            same, r.bias[1:2, :], r.bias[0:1, :]
        )
        y = nn(r.act[t], r.w_out[...])
        r.out[t] = ((seed + y) * (r.live_column[...] * live)).astype(BF)


def kernel(sizes, names, *refs):
    r = Refs(names, refs)
    me = Place(sizes)
    nz, pr, pc, np_ = me.nz, me.pr, me.pc, me.np
    z, q = me.z, me.q
    rb = r.q.shape[0]
    fd = r.pp.shape[0]
    group = group_of(nz)
    wz = W // group
    columns = 8 * np_
    slab_plane = 2 * np_
    slab_tile = slab_plane // pr
    log_np = bits(np_)

    barrier = pltpu.get_barrier_semaphore()
    loads = {}
    for i, name in enumerate(LOADS):
        target = getattr(r, name)
        if name in ("k", "v"):
            target = target.at[z]
        loads[name] = pltpu.make_async_copy(getattr(r, name + "_hbm"), target, r.load_sem.at[i])
    for name in LOADS[:3]:
        loads[name].start()
    me.signal_all(barrier)
    for name in LOADS[3:]:
        loads[name].start()
    me.wait_all(barrier)

    furthest = (nz // 2, nz - 1 - nz // 2, nz - 1 - nz // 2, nz // 2)

    def ring(chain, distance, hop):
        buf = r.k if chain < 2 else r.v
        way = 1 if chain % 2 == 0 else -1
        block = lax.rem(z - way * (distance - hop) + nz, nz)
        peer = lax.rem(z + way * hop + nz, nz)
        own = r.k_hbm if chain < 2 else r.v_hbm
        return pltpu.make_async_remote_copy(
            src_ref=own if distance == hop else buf.at[block],
            dst_ref=buf.at[block],
            send_sem=r.ring_send.at[chain, distance - 1],
            recv_sem=r.ring_recv.at[chain, distance - 1],
            device_id=(peer, me.prow, me.pcol),
            device_id_type=MESH,
        )

    def pass_on(chain, held):
        for hop in (2, 1):
            if held + hop <= furthest[chain]:
                ring(chain, held + hop, hop).start()

    for chain in range(4):
        pass_on(chain, 0)

    witnesses = plane_witnesses(pr, pc)
    for m in witnesses:
        pl.semaphore_signal(
            r.known_sem, inc=1, device_id=me.plane_peer(m)[1], device_id_type=MESH
        )

    loads["pp"].wait()
    row, column = grid_of(wz, W)
    piece = nt(one_hot(column == row + lax.rem(z, group) * wz), r.pp[...]).astype(BF)
    row, column = grid_of(fd, W)
    piece = nn(piece, one_hot(column == row + ((fd * q) & 127))).astype(BF)
    r.ppmsg[...] = piece
    r.ppg[q] = piece

    row, column = grid_of(8 * np_, rb)
    r.perm[...] = one_hot(column == (row & 3) * np_ + (row >> 3))
    loads["res"].wait()
    rows_twice = nt(r.perm[...], r.res[...]).astype(BF)
    both = nn(rows_twice, r.pp[...])
    row, column = grid_of(8 * np_, E)
    is_left = (row & 7) < 4
    r.presidual[...] = jnp.where(is_left, both[:, :E], both[:, E:])
    for name in ("q", "k", "v", "mask"):
        loads[name].wait()
    r.q_twice[...] = nn(r.perm[...], r.q[...]).astype(BF)

    scale = 1.0 / math.sqrt(E)

    def score(block):
        raw = nt(r.q_twice[...], r.k[block]) * scale
        live = r.mask[pl.ds(block, 1), :]
        r.scores[block] = jnp.where(live > 0, raw, -1e30)

    score(z)
    if witnesses:
        pl.semaphore_wait(r.known_sem, len(witnesses))
    me.to_plane(lambda peer: r.ppmsg, r.ppg, r.send_sem.at[0], r.recv_sem.at[0])

    def arrive(chain, distance):
        if distance <= furthest[chain]:
            ring(chain, distance, 1 if distance % 2 else 2).wait_recv()
            if distance % 2 == 0:
                pass_on(chain, distance)

    def score_at(distance):
        if distance <= furthest[0]:
            score(lax.rem(z - distance + nz, nz))
        if distance <= furthest[1]:
            score(lax.rem(z + distance, nz))

    w0 = r.start[0] + z * slab_plane
    r0 = w0 + ((q - w0) & (np_ - 1))
    k0 = r0 >> log_np
    first = w0 + me.prow * slab_tile
    second_half = jnp.where(me.prow >= pr // 2, 1, 0)

    def make_w2():
        loads["op"].wait()
        wait_bytes(r.ppg, np_ - 1, r.recv_sem.at[0])
        total = jnp.zeros((E, wz), F32)
        for chunk in range(np_):
            at = ((fd * chunk) >> 7) << 7
            total = total + nt(r.op[:, at : at + W], r.ppg[chunk])
        row, column = grid_of(wz, wz)
        turned = nt(one_hot(row == column), total.astype(BF)).astype(BF)
        r.w2msg[...] = turned
        r.w2g[lax.rem(z, group)] = turned
        me.to_group(r.w2msg, r.w2g, r.send_sem.at[1], r.recv_sem.at[1])

    def make_picks():
        row, column = grid_of(pc * 16, 8 * nz)
        sub = row & 15
        right_hit = (sub < 8) & (column == (2 * (row >> 4) + (sub >> 2)) * 8 + 4 + (sub & 3))
        kk = k0 + (sub - 8)
        left_hit = ((sub == 8) | (sub == 9)) & (column == (kk >> 2) * 8 + (kk & 3))
        r.pick[...] = one_hot(right_hit | left_hit)
        row, column = grid_of(columns + slab_tile, 16 * np_)
        right_hit = (row < columns) & (column == (row & (np_ - 1)) * 16 + (row >> log_np))
        left_hit = (row >= columns) & (
            column == ((first + row - columns) & (np_ - 1)) * 16 + 8 + second_half
        )
        r.place_rows[...] = one_hot(right_hit | left_hit)
        row, column = grid_of(16 * np_, columns + slab_tile)
        sub = row & 15
        owner = row >> 4
        right_hit = (sub < 8) & (column == sub * np_ + owner)
        left_hit = (
            (sub == 8 + second_half)
            & (column >= columns)
            & (((first + column - columns) & (np_ - 1)) == owner)
        )
        r.spread_rows[...] = one_hot(right_hit | left_hit)

    def make_pair_constants():
        for name in ("chain", "bias", "gain", "w_in", "w_out", "mask_flat", "chain_flat"):
            loads[name].wait()
        r.w_half[...] = (r.w_in[...].astype(F32) * 0.5).astype(BF)
        r.w_out_half[...] = (r.w_out[...].astype(F32) * 0.5).astype(BF)
        row, column = grid_of(2 * E, 2 * E)
        r.means[...] = jnp.where((row >> 7) == (column >> 7), 1.0 / E, 0.0).astype(BF)
        r.bias_mean[...] = jnp.broadcast_to(jnp.mean(r.bias[...], axis=1, keepdims=True), (2, E))
        row, column = grid_of(rb, rb)
        unit = one_hot(row == column)
        for half in range(2):
            at = pl.ds(2 * me.pcol + half, 1)
            to = pl.ds(half * rb, rb)
            for source, target in ((r.mask, r.live_column), (r.chain, r.chain_column)):
                lanes = jnp.broadcast_to(source[at, :].astype(F32), (E, rb)).astype(BF)
                target[to, :] = nt(unit, lanes)

    def make_d_act(first_row, end_row):
        for t in range(first_row, end_row):
            r.d_act[t] = nt(r.cot[t], r.w_out_half[...]).astype(r.d_act.dtype)

    last = nz // 2
    half_tile = slab_tile // 2
    chores = {
        0: (make_pair_constants, make_picks),
        2: (lambda: loads["cot"].wait(), lambda: make_d_act(0, half_tile)),
        4: (make_w2,),
        6: (lambda: make_d_act(half_tile, slab_tile),),
    }
    for chore in chores[0]:
        chore()
    for distance in range(2, last, 2):
        for chain in range(4):
            arrive(chain, distance)
        for near in (distance - 1, distance):
            if near % 2:
                for chain in range(2):
                    arrive(chain, near)
            score_at(near)
        for chore in chores.pop(distance, ()):
            chore()
    for stage in (2, 4, 6):
        for chore in chores.pop(stage, ()):
            chore()

    def blocks_at(distance):
        left = lax.rem(z - distance + nz, nz)
        if distance in (0, last):
            return [left]
        return [left, lax.rem(z + distance, nz)]

    def attend(distances):
        blocks = [b for distance in distances for b in blocks_at(distance)]
        top = r.scores[blocks[0]]
        for b in blocks[1:]:
            top = jnp.maximum(top, r.scores[b])
        top = jnp.max(top, axis=1, keepdims=True)
        pairs = [blocks[i : i + 2] for i in range(0, len(blocks), 2)]
        below = jnp.zeros((8 * np_, rb), F32)
        weights = []
        for pair in pairs:
            shifted = [jnp.exp(r.scores[b] - top) for b in pair]
            for part in shifted:
                below = below + part
            weights.append(jnp.concatenate(shifted, axis=1).astype(BF))
        below = jnp.sum(below, axis=1, keepdims=True)
        for distance in distances:
            if distance % 2 or distance == last:
                for chain in (2, 3):
                    arrive(chain, distance)
        above = jnp.zeros((8 * np_, E), F32)
        for pair, weight in zip(pairs, weights):
            above = above + nn(weight, jnp.concatenate([r.v[b] for b in pair], axis=0))
        return top, below, above

    top, below, above = attend(range(last - 1))
    for chain in (0, 1):
        arrive(chain, last)
        arrive(chain, last - 1)
    score_at(last - 1)
    score_at(last)
    top_late, below_late, above_late = attend((last, last - 1))
    highest = jnp.maximum(top, top_late)
    early, late = jnp.exp(top - highest), jnp.exp(top_late - highest)
    below = 1.0 / (below * early + below_late * late)
    attended = ((above * early + above_late * late) * below).astype(BF)
    wait_bytes(r.w2g, group - 1, r.recv_sem.at[1])
    both = nt(attended, r.w2g[...].reshape(W, E))
    terms = jnp.where(is_left, both[:, :E], both[:, E:]) + r.presidual[...]
    r.pmsg[...] = terms.reshape(np_, 8, E)
    me.to_plane(lambda peer: r.pmsg.at[peer], r.pbuf, r.send_sem.at[2], r.recv_sem.at[2])
    r.pbuf[q] = r.pmsg[q]
    wait_bytes(r.pbuf, np_ - 1, r.recv_sem.at[2])
    projected = jnp.sum(r.pbuf[...], axis=0).astype(BF).astype(F32)
    r.tmsg[...] = projected
    r.zbuf[z] = projected
    me.to_column(lambda peer: r.tmsg, r.zbuf, r.send_sem.at[3], r.recv_sem.at[3])
    wait_bytes(r.zbuf, nz - 1, r.recv_sem.at[3])
    chosen = nn(r.pick[...], r.zbuf[...].reshape(8 * nz, E).astype(BF)).astype(BF)
    r.msg[...] = chosen.reshape(pc, 16, E)
    me.to_plane(
        lambda peer: r.msg.at[lax.rem(peer, pc)], r.rbuf, r.send_sem.at[4], r.recv_sem.at[4]
    )
    r.rbuf[q] = r.msg[me.pcol]
    wait_bytes(r.rbuf, np_ - 1, r.recv_sem.at[4])
    r.ab[...] = nn(r.place_rows[...], r.rbuf[...].reshape(16 * np_, E))

    r.right_live[...] = r.ab[pl.ds(0, columns), :] * r.live_column[...]

    total = pair_tile(r, slab_tile, columns, first)
    r.grads[pl.ds(0, columns), :] = total * r.live_column[...]
    gathered = nn(r.spread_rows[...], r.grads[...].astype(BF)).astype(BF)
    r.gmsg[...] = gathered.reshape(np_, 16, E)
    me.to_plane(lambda peer: r.gmsg.at[peer], r.gbuf, r.send_sem.at[5], r.recv_sem.at[5])
    r.gbuf[q] = r.gmsg[q]
    split = slab_tile * 3 // 8
    pair_results(r, range(split), columns, first)
    wait_bytes(r.gbuf, np_ - 1, r.recv_sem.at[5])
    by_column = jnp.sum(r.gbuf[...].astype(F32).reshape(pr, pc, 16, E), axis=0)
    over_columns = jnp.sum(by_column, axis=0)
    left0 = over_columns[8:9, :]
    left1 = over_columns[9:10, :]
    sub, _ = grid_of(8, E)
    for other in range(nz):
        k = 4 * other + (sub & 3)
        lefts = jnp.where(k == k0, left0, jnp.where(k == k0 + 1, left1, 0.0))
        r.zmsg[other] = jnp.where((sub >> 2) == other % 2, by_column[other // 2, 0:8, :], lefts)
    me.to_column(lambda peer: r.zmsg.at[peer], r.hbuf, r.send_sem.at[6], r.recv_sem.at[6])
    r.hbuf[z] = r.zmsg[z]
    pair_results(r, range(split, slab_tile), columns, first)
    store = pltpu.make_async_copy(r.out, r.out_hbm, r.store_sem)
    store.start()
    wait_bytes(r.hbuf, nz - 1, r.recv_sem.at[6])
    tile = jnp.sum(r.hbuf[...], axis=0).astype(BF).astype(F32)
    r.fmsg[...] = tile
    r.fbuf[q] = tile
    me.to_plane(lambda peer: r.fmsg, r.fbuf, r.send_sem.at[7], r.recv_sem.at[7])
    odd = z & 1
    row, column = grid_of(2 * rb, 8 * np_)
    half = jnp.where(row < rb, 1 - odd, odd)
    base = (row & (np_ - 1)) * 8 + ((row >> log_np) & 3)
    halves = one_hot(column == base + 4 * half)
    for chain in range(4):
        for distance in range(1, furthest[chain] + 1):
            ring(chain, distance, 1 if distance % 2 else 2).wait_send()
    wait_bytes(r.ppg, np_ - 1, r.send_sem.at[0])
    wait_bytes(r.w2g, group - 1, r.send_sem.at[1])
    wait_bytes(r.pbuf, np_ - 1, r.send_sem.at[2])
    wait_bytes(r.zbuf, nz - 1, r.send_sem.at[3])
    wait_bytes(r.rbuf, np_ - 1, r.send_sem.at[4])
    wait_bytes(r.gbuf, np_ - 1, r.send_sem.at[5])
    wait_bytes(r.hbuf, nz - 1, r.send_sem.at[6])
    wait_bytes(r.fbuf, np_ - 1, r.recv_sem.at[7])
    tiles = r.fbuf[...].reshape(8 * np_, E).astype(BF)
    store.wait()
    halves = nn(halves, tiles).astype(BF)
    halves = jnp.concatenate([halves[:rb], halves[rb:]], axis=1)
    r.lm[...] = nt(r.pp[...], halves).astype(BF)
    wait_bytes(r.fbuf, np_ - 1, r.send_sem.at[7])


D_ACT = BF


def fused(sizes, start, operands):
    nz, pr, pc = sizes
    np_ = pr * pc
    q, k, v, res, op, pp, bias, gain, w_in, w_out, cot, mask, chain, mask_flat, chain_flat = operands
    rb = q.shape[0]
    columns = 8 * np_
    tile = 2 * np_ // pr
    group = group_of(nz)
    wz = W // group
    vmem, dma = pltpu.VMEM, pltpu.SemaphoreType.DMA
    steps = max(1, nz // 2)
    scratch = {
        "q": vmem(q.shape, BF),
        "k": vmem((nz, rb, E), BF),
        "v": vmem((nz, rb, E), BF),
        "res": vmem(res.shape, BF),
        "op": vmem(op.shape, BF),
        "pp": vmem(pp.shape, BF),
        "bias": vmem(bias.shape, F32),
        "gain": vmem(gain.shape, F32),
        "w_in": vmem(w_in.shape, BF),
        "w_out": vmem(w_out.shape, BF),
        "cot": vmem(cot.shape, BF),
        "mask": vmem(mask.shape, jnp.int32),
        "chain": vmem(chain.shape, jnp.int32),
        "mask_flat": pltpu.SMEM(mask_flat.shape, jnp.int32),
        "chain_flat": pltpu.SMEM(chain_flat.shape, jnp.int32),
        "scores": vmem((nz, 8 * np_, rb), F32),
        "q_twice": vmem((8 * np_, E), BF),
        "perm": vmem((8 * np_, rb), BF),
        "pick": vmem((pc * 16, 8 * nz), BF),
        "place_rows": vmem((columns + tile, 16 * np_), BF),
        "spread_rows": vmem((16 * np_, columns + tile), BF),
        "presidual": vmem((8 * np_, E), F32),
        "ppmsg": vmem((wz, W), BF),
        "ppg": vmem((np_, wz, W), BF),
        "w2msg": vmem((wz, E), BF),
        "w2g": vmem((group, wz, E), BF),
        "pmsg": vmem((np_, 8, E), F32),
        "pbuf": vmem((np_, 8, E), F32),
        "tmsg": vmem((8, E), F32),
        "zbuf": vmem((nz, 8, E), F32),
        "msg": vmem((pc, 16, E), BF),
        "rbuf": vmem((np_, 16, E), BF),
        "ab": vmem((columns + tile, E), F32),
        "out": vmem(cot.shape, BF),
        "store_sem": dma,
        "w_half": vmem(w_in.shape, BF),
        "w_out_half": vmem(w_out.shape, BF),
        "means": vmem((2 * E, 2 * E), BF),
        "bias_mean": vmem((2, E), F32),
        "live_column": vmem((columns, E), F32),
        "chain_column": vmem((columns, E), F32),
        "right_live": vmem((columns, E), F32),
        "act": vmem(cot.shape[:2] + w_in.shape[1:], BF),
        "d_act": vmem(cot.shape[:2] + w_in.shape[1:], D_ACT),
        "grads": vmem((columns + tile, E), F32),
        "gmsg": vmem((np_, 16, E), BF),
        "gbuf": vmem((np_, 16, E), BF),
        "zmsg": vmem((nz, 8, E), F32),
        "hbuf": vmem((nz, 8, E), F32),
        "fmsg": vmem((8, E), F32),
        "fbuf": vmem((np_, 8, E), F32),
        "known_sem": pltpu.SemaphoreType.REGULAR,
        "load_sem": dma((len(LOADS),)),
        "ring_send": dma((4, steps)),
        "ring_recv": dma((4, steps)),
        "send_sem": dma((8,)),
        "recv_sem": dma((8,)),
    }
    hbm = pl.BlockSpec(memory_space=pltpu.HBM)
    return pl.pallas_call(
        functools.partial(kernel, sizes, INPUTS + ("out_hbm", "lm") + tuple(scratch)),
        out_shape=(
            jax.ShapeDtypeStruct(cot.shape, BF),
            jax.ShapeDtypeStruct((pp.shape[0], rb), BF),
        ),
        in_specs=[pl.BlockSpec(memory_space=pltpu.SMEM)] + [hbm] * len(operands),
        out_specs=(hbm, pl.BlockSpec(memory_space=pltpu.VMEM)),
        scratch_shapes=list(scratch.values()),
        compiler_params=pltpu.CompilerParams(
            collective_id=0, has_side_effects=True, vmem_limit_bytes=58 << 20
        ),
        name="attend_pair_and_gradient",
    )(start, *operands)


def store_kernel(out, lm, out_hbm, lm_hbm, out_vmem, lm_vmem, load_sem, save_sem):
    parts = load_sem.shape[0] - 1
    rows = out.shape[0] // parts
    ways = [(lm, lm_vmem, lm_hbm)]
    for i in range(parts):
        part = pl.ds(i * rows, rows)
        ways.append((out.at[part], out_vmem.at[part], out_hbm.at[part]))
    loads = [pltpu.make_async_copy(w[0], w[1], load_sem.at[i]) for i, w in enumerate(ways)]
    saves = [pltpu.make_async_copy(w[1], w[2], save_sem.at[i]) for i, w in enumerate(ways)]
    for load in loads:
        load.start()
    for load, save in zip(loads, saves):
        load.wait()
        save.start()
    for save in saves:
        save.wait()


def store(out, lm):
    parts = min(8, out.shape[0]) + 1
    return pl.pallas_call(
        store_kernel,
        out_shape=tuple(jax.ShapeDtypeStruct(a.shape, a.dtype) for a in (out, lm)),
        in_specs=[pl.BlockSpec(memory_space=pltpu.HBM)] * 2,
        out_specs=(pl.BlockSpec(memory_space=pltpu.HBM),) * 2,
        scratch_shapes=[
            pltpu.VMEM(out.shape, out.dtype),
            pltpu.VMEM(lm.shape, lm.dtype),
            pltpu.SemaphoreType.DMA((parts,)),
            pltpu.SemaphoreType.DMA((parts,)),
        ],
        compiler_params=pltpu.CompilerParams(vmem_limit_bytes=62 << 20),
        name="store_results",
    )(out, lm)


def body(
    sizes,
    queries,
    keys,
    values,
    residual,
    out_proj,
    pair_proj,
    chain_bias,
    ln_gain,
    w_in,
    w_out,
    pair_cot,
    residue_mask,
    chain_ids,
    slab_start,
):
    nz, rb = sizes[0], queries.shape[0]
    operands = (
        queries,
        keys,
        values,
        residual.T,
        out_proj,
        pair_proj,
        chain_bias,
        ln_gain.reshape(1, E),
        w_in,
        w_out,
        pair_cot,
        residue_mask.reshape(nz, rb),
        chain_ids.reshape(nz, rb),
        residue_mask,
        chain_ids,
    )
    pair_out, lm_grad = store(*fused(sizes, slab_start, operands))
    return pair_out, lm_grad.T


def solution(mesh):
    sizes = tuple(mesh.shape[name] for name in ("lm", "prow", "pcol"))
    return jax.shard_map(
        functools.partial(body, sizes),
        mesh=mesh,
        in_specs=(
            P("lm", ("prow", "pcol")),
            P("lm", ("prow", "pcol")),
            P("lm", ("prow", "pcol")),
            P("lm", ("prow", "pcol")),
            P(("prow", "pcol"), None),
            P(("prow", "pcol"), None),
            P(),
            P(),
            P(),
            P(),
            P(("lm", "prow"), "pcol", None),
            P(),
            P(),
            P(),
        ),
        out_specs=(P(("lm", "prow"), "pcol", None), P("lm", ("prow", "pcol"))),
        check_vma=False,
    )
```

```python
import functools
import math

import jax
import jax.numpy as jnp
from jax import lax
from jax.experimental import pallas as pl
from jax.experimental.pallas import tpu as pltpu
from jax.sharding import PartitionSpec as P

BF = jnp.bfloat16
F32 = jnp.float32
MESH = pl.DeviceIdType.MESH
E = 128
W = 256


def nn(a, b):
    return lax.dot_general(a, b, (((1,), (0,)), ((), ())), preferred_element_type=F32)


def nt(a, b):
    return lax.dot_general(a, b, (((1,), (1,)), ((), ())), preferred_element_type=F32)


def grid_of(rows, columns):
    row = lax.broadcasted_iota(jnp.int32, (rows, columns), 0)
    column = lax.broadcasted_iota(jnp.int32, (rows, columns), 1)
    return row, column


def one_hot(hit):
    return jnp.where(hit, 1.0, 0.0).astype(BF)


def bits(n):
    return n.bit_length() - 1


def plane_hops(pr, pc, m):
    if (pr, pc) != (4, 8):
        return 1
    ring = (0, 1, 2, 1)
    return ring[(m >> 1) & 3] + ring[((m & 1) << 1) | (m >> 4)]


def plane_order(pr, pc):
    return sorted(range(1, pr * pc), key=lambda m: -plane_hops(pr, pc, m))


def plane_greeted(pr, pc):
    return [m for m in plane_order(pr, pc) if plane_hops(pr, pc, m) <= 2]


def plane_witnesses(pr, pc):
    witnesses = [1, 4] if (pr, pc) == (4, 8) else []
    greeted = plane_greeted(pr, pc)
    for m in range(1, pr * pc):
        assert any(m ^ w in greeted or m == w for w in [0] + witnesses)
    return witnesses


def group_of(nz):
    return min(8, nz)


def z_order(nz):
    return sorted(range(1, nz), key=lambda i: -min(i, nz - i))


class Place:
    def __init__(self, sizes):
        self.nz, self.pr, self.pc = sizes
        self.np = self.pr * self.pc
        self.z = lax.axis_index("lm")
        self.prow = lax.axis_index("prow")
        self.pcol = lax.axis_index("pcol")
        self.q = self.prow * self.pc + self.pcol

    def plane_peer(self, m):
        prow = lax.bitwise_xor(self.prow, m // self.pc)
        pcol = lax.bitwise_xor(self.pcol, m % self.pc)
        return lax.bitwise_xor(self.q, m), (self.z, prow, pcol)

    def z_peer(self, i):
        peer = lax.rem(self.z + i, self.nz)
        return peer, (peer, self.prow, self.pcol)

    def near(self):
        return sorted({way * d % self.nz for d in (1, 2) for way in (1, -1)} - {0})

    def greeted(self):
        for i in self.near():
            yield self.z_peer(i)[1]
        for m in plane_greeted(self.pr, self.pc):
            yield self.plane_peer(m)[1]

    def signal_all(self, barrier):
        for device in self.greeted():
            pl.semaphore_signal(barrier, inc=1, device_id=device, device_id_type=MESH)

    def wait_all(self, barrier):
        pl.semaphore_wait(barrier, len(plane_greeted(self.pr, self.pc)) + len(self.near()))

    def send(self, source, target, send_sem, recv_sem, device):
        pltpu.make_async_remote_copy(
            src_ref=source,
            dst_ref=target,
            send_sem=send_sem,
            recv_sem=recv_sem,
            device_id=device,
            device_id_type=MESH,
        ).start()

    def to_plane(self, source, target, send_sem, recv_sem, offsets=None):
        for m in plane_order(self.pr, self.pc) if offsets is None else offsets:
            peer, device = self.plane_peer(m)
            self.send(source(peer), target.at[self.q], send_sem, recv_sem, device)

    def to_group(self, source, target, send_sem, recv_sem):
        group = group_of(self.nz)
        slot = lax.rem(self.z, group)
        for i in range(-(group // 2), group // 2):
            if i:
                device = self.z_peer(i % self.nz)[1]
                self.send(source, target.at[slot], send_sem, recv_sem, device)

    def to_column(self, source, target, send_sem, recv_sem):
        for i in z_order(self.nz):
            peer, device = self.z_peer(i)
            self.send(source(peer), target.at[self.z], send_sem, recv_sem, device)


def wait_bytes(buffer, count, sem):
    part = buffer.at[pl.ds(0, count)]
    pltpu.make_async_copy(part, part, sem).wait()


class Refs:
    def __init__(self, names, refs):
        for name, ref in zip(names, refs, strict=True):
            setattr(self, name, ref)


INPUTS = (
    "start",
    "q_hbm",
    "k_hbm",
    "v_hbm",
    "res_hbm",
    "op_hbm",
    "pp_hbm",
    "bias_hbm",
    "gain_hbm",
    "w_in_hbm",
    "w_out_hbm",
    "cot_hbm",
    "mask_hbm",
    "chain_hbm",
    "mask_flat_hbm",
    "chain_flat_hbm",
)
LOADS = (
    "k",
    "v",
    "pp",
    "q",
    "mask",
    "res",
    "chain",
    "bias",
    "gain",
    "w_in",
    "w_out",
    "op",
    "cot",
    "mask_flat",
    "chain_flat",
)


class PairGroup:
    def __init__(self, r, rows, columns, first):
        self.r, self.rows, self.columns, self.first = r, rows, columns, first

    def norm_and_hidden(self):
        r, rows, columns = self.r, self.rows, self.columns
        gain = r.gain[...]
        self.lefts = [r.ab[pl.ds(columns + t, 1), :] for t in rows]
        right = r.ab[pl.ds(0, columns), :]
        spread = jnp.concatenate([jnp.broadcast_to(left, (E, E)) for left in self.lefts], axis=0)
        dots = nt(right.astype(BF), spread.astype(BF)) * (1.0 / E)
        centres = []
        for j, t in enumerate(rows):
            same = r.chain_column[...] == r.chain_flat[self.first + t].astype(F32)
            seed = self.lefts[j] * right + jnp.where(same, r.bias[1:2, :], r.bias[0:1, :])
            mean = dots[:, j * E : (j + 1) * E] + jnp.where(
                same, r.bias_mean[1:2, :], r.bias_mean[0:1, :]
            )
            centres.append(seed - mean)
        self.inverses = [
            lax.rsqrt(jnp.mean(c * c, axis=1, keepdims=True) + 1e-05) for c in centres
        ]
        self.normeds = [c * inverse for c, inverse in zip(centres, self.inverses)]
        scaled = jnp.concatenate([(n * gain).astype(BF) for n in self.normeds], axis=0)
        self.half = nn(scaled, r.w_half[...])

    def activate(self):
        r = self.r
        d_act = jnp.concatenate([r.d_act[t] for t in self.rows], axis=0)
        half = self.half.astype(D_ACT)
        turned = jnp.tanh(half)
        raised = 1.0 + turned
        act = half * raised
        d_hidden = (d_act * (raised + act * (1.0 - turned))).astype(BF)
        act = act.astype(BF)
        for j, t in enumerate(self.rows):
            r.act[t] = act[j * self.columns : (j + 1) * self.columns]
        self.d_scaled = nt(d_hidden, r.w_in[...])

    def finish(self, total):
        r, columns = self.r, self.columns
        gain = r.gain[...]
        for j, t in enumerate(self.rows):
            live = r.mask_flat[self.first + t].astype(F32)
            block = slice(j * columns, (j + 1) * columns)
            d_normed = self.d_scaled[block] * gain
            both = jnp.concatenate([d_normed, d_normed * self.normeds[j]], axis=1).astype(BF)
            both = nn(both, r.means[...])
            d_seed = r.cot[t].astype(F32) + self.inverses[j] * (
                d_normed - both[:, :E] - self.normeds[j] * both[:, E:]
            )
            total = total + d_seed * (self.lefts[j] * live)
            r.grads[pl.ds(columns + t, 1), :] = live * jnp.sum(
                d_seed * r.right_live[...], axis=0, keepdims=True
            )
        return total


def pair_tile(r, tile, columns, first):
    per = min(4, tile)
    groups = [
        PairGroup(r, range(at, at + per), columns, first) for at in range(0, tile, per)
    ]
    total = jnp.zeros((columns, E), F32)
    for i in range(len(groups) + 2):
        if i < len(groups):
            groups[i].norm_and_hidden()
        if 0 <= i - 1 < len(groups):
            groups[i - 1].activate()
        if i >= 2:
            total = groups[i - 2].finish(total)
    return total


def pair_results(r, rows, columns, first):
    right = r.ab[pl.ds(0, columns), :]
    for t in rows:
        same = r.chain_column[...] == r.chain_flat[first + t].astype(F32)
        live = r.mask_flat[first + t].astype(F32)
        seed = r.ab[pl.ds(columns + t, 1), :] * right + jnp.where(
            same, r.bias[1:2, :], r.bias[0:1, :]
        )
        y = nn(r.act[t], r.w_out[...])
        r.out[t] = ((seed + y) * (r.live_column[...] * live)).astype(BF)


def kernel(sizes, names, *refs):
    r = Refs(names, refs)
    me = Place(sizes)
    nz, pr, pc, np_ = me.nz, me.pr, me.pc, me.np
    z, q = me.z, me.q
    rb = r.q.shape[0]
    fd = r.pp.shape[0]
    group = group_of(nz)
    wz = W // group
    columns = 8 * np_
    slab_plane = 2 * np_
    slab_tile = slab_plane // pr
    log_np = bits(np_)

    barrier = pltpu.get_barrier_semaphore()
    loads = {}
    for i, name in enumerate(LOADS):
        target = getattr(r, name)
        if name in ("k", "v"):
            target = target.at[z]
        loads[name] = pltpu.make_async_copy(getattr(r, name + "_hbm"), target, r.load_sem.at[i])
    for name in LOADS[:3]:
        loads[name].start()
    me.signal_all(barrier)
    for name in LOADS[3:]:
        loads[name].start()
    me.wait_all(barrier)

    furthest = (nz // 2, nz - 1 - nz // 2, nz - 1 - nz // 2, nz // 2)

    def ring(chain, distance, hop):
        buf = r.k if chain < 2 else r.v
        way = 1 if chain % 2 == 0 else -1
        block = lax.rem(z - way * (distance - hop) + nz, nz)
        peer = lax.rem(z + way * hop + nz, nz)
        own = r.k_hbm if chain < 2 else r.v_hbm
        return pltpu.make_async_remote_copy(
            src_ref=own if distance == hop else buf.at[block],
            dst_ref=buf.at[block],
            send_sem=r.ring_send.at[chain, distance - 1],
            recv_sem=r.ring_recv.at[chain, distance - 1],
            device_id=(peer, me.prow, me.pcol),
            device_id_type=MESH,
        )

    def pass_on(chain, held):
        for hop in (2, 1):
            if held + hop <= furthest[chain]:
                ring(chain, held + hop, hop).start()

    for chain in range(4):
        pass_on(chain, 0)

    witnesses = plane_witnesses(pr, pc)
    for m in witnesses:
        pl.semaphore_signal(
            r.known_sem, inc=1, device_id=me.plane_peer(m)[1], device_id_type=MESH
        )

    loads["pp"].wait()
    row, column = grid_of(wz, W)
    piece = nt(one_hot(column == row + lax.rem(z, group) * wz), r.pp[...]).astype(BF)
    row, column = grid_of(fd, W)
    piece = nn(piece, one_hot(column == row + ((fd * q) & 127))).astype(BF)
    r.ppmsg[...] = piece
    r.ppg[q] = piece
    greeted = plane_greeted(pr, pc)

    def share_piece(offsets):
        me.to_plane(lambda peer: r.ppmsg, r.ppg, r.send_sem.at[0], r.recv_sem.at[0], offsets)

    share_piece(greeted)

    row, column = grid_of(8 * np_, rb)
    r.perm[...] = one_hot(column == (row & 3) * np_ + (row >> 3))
    loads["res"].wait()
    rows_twice = nt(r.perm[...], r.res[...]).astype(BF)
    both = nn(rows_twice, r.pp[...])
    row, column = grid_of(8 * np_, E)
    is_left = (row & 7) < 4
    r.presidual[...] = jnp.where(is_left, both[:, :E], both[:, E:])
    for name in ("q", "k", "v", "mask"):
        loads[name].wait()
    r.q_twice[...] = nn(r.perm[...], r.q[...]).astype(BF)

    scale = 1.0 / math.sqrt(E)

    def score(block):
        raw = nt(r.q_twice[...], r.k[block]) * scale
        live = r.mask[pl.ds(block, 1), :]
        r.scores[block] = jnp.where(live > 0, raw, -1e30)

    score(z)
    if witnesses:
        pl.semaphore_wait(r.known_sem, len(witnesses))
        share_piece([m for m in plane_order(pr, pc) if m not in greeted])

    def arrive(chain, distance):
        if distance <= furthest[chain]:
            ring(chain, distance, 1 if distance % 2 else 2).wait_recv()
            if distance % 2 == 0:
                pass_on(chain, distance)

    def score_at(distance):
        if distance <= furthest[0]:
            score(lax.rem(z - distance + nz, nz))
        if distance <= furthest[1]:
            score(lax.rem(z + distance, nz))

    w0 = r.start[0] + z * slab_plane
    r0 = w0 + ((q - w0) & (np_ - 1))
    k0 = r0 >> log_np
    first = w0 + me.prow * slab_tile
    second_half = jnp.where(me.prow >= pr // 2, 1, 0)

    def make_w2():
        loads["op"].wait()
        wait_bytes(r.ppg, np_ - 1, r.recv_sem.at[0])
        total = jnp.zeros((E, wz), F32)
        for chunk in range(np_):
            at = ((fd * chunk) >> 7) << 7
            total = total + nt(r.op[:, at : at + W], r.ppg[chunk])
        row, column = grid_of(wz, wz)
        turned = nt(one_hot(row == column), total.astype(BF)).astype(BF)
        r.w2msg[...] = turned
        r.w2g[lax.rem(z, group)] = turned
        me.to_group(r.w2msg, r.w2g, r.send_sem.at[1], r.recv_sem.at[1])

    def make_picks():
        row, column = grid_of(pc * 16, 8 * nz)
        sub = row & 15
        right_hit = (sub < 8) & (column == (2 * (row >> 4) + (sub >> 2)) * 8 + 4 + (sub & 3))
        kk = k0 + (sub - 8)
        left_hit = ((sub == 8) | (sub == 9)) & (column == (kk >> 2) * 8 + (kk & 3))
        r.pick[...] = one_hot(right_hit | left_hit)
        row, column = grid_of(columns + slab_tile, 16 * np_)
        right_hit = (row < columns) & (column == (row & (np_ - 1)) * 16 + (row >> log_np))
        left_hit = (row >= columns) & (
            column == ((first + row - columns) & (np_ - 1)) * 16 + 8 + second_half
        )
        r.place_rows[...] = one_hot(right_hit | left_hit)
        row, column = grid_of(16 * np_, columns + slab_tile)
        sub = row & 15
        owner = row >> 4
        right_hit = (sub < 8) & (column == sub * np_ + owner)
        left_hit = (
            (sub == 8 + second_half)
            & (column >= columns)
            & (((first + column - columns) & (np_ - 1)) == owner)
        )
        r.spread_rows[...] = one_hot(right_hit | left_hit)

    def make_pair_constants():
        for name in ("chain", "bias", "gain", "w_in", "w_out", "mask_flat", "chain_flat"):
            loads[name].wait()
        r.w_half[...] = (r.w_in[...].astype(F32) * 0.5).astype(BF)
        r.w_out_half[...] = (r.w_out[...].astype(F32) * 0.5).astype(BF)
        row, column = grid_of(2 * E, 2 * E)
        r.means[...] = jnp.where((row >> 7) == (column >> 7), 1.0 / E, 0.0).astype(BF)
        r.bias_mean[...] = jnp.broadcast_to(jnp.mean(r.bias[...], axis=1, keepdims=True), (2, E))
        row, column = grid_of(rb, rb)
        unit = one_hot(row == column)
        for half in range(2):
            at = pl.ds(2 * me.pcol + half, 1)
            to = pl.ds(half * rb, rb)
            for source, target in ((r.mask, r.live_column), (r.chain, r.chain_column)):
                lanes = jnp.broadcast_to(source[at, :].astype(F32), (E, rb)).astype(BF)
                target[to, :] = nt(unit, lanes)

    def make_d_act(first_row, end_row):
        for t in range(first_row, end_row):
            r.d_act[t] = nt(r.cot[t], r.w_out_half[...]).astype(r.d_act.dtype)

    last = nz // 2
    half_tile = slab_tile // 2
    chores = {
        0: (make_pair_constants, make_picks),
        2: (lambda: loads["cot"].wait(), lambda: make_d_act(0, half_tile)),
        4: (make_w2,),
        6: (lambda: make_d_act(half_tile, slab_tile),),
    }
    for chore in chores[0]:
        chore()
    for distance in range(2, last, 2):
        for chain in range(4):
            arrive(chain, distance)
        for near in (distance - 1, distance):
            if near % 2:
                for chain in range(2):
                    arrive(chain, near)
            score_at(near)
        for chore in chores.pop(distance, ()):
            chore()
    for stage in (2, 4, 6):
        for chore in chores.pop(stage, ()):
            chore()

    def blocks_at(distance):
        left = lax.rem(z - distance + nz, nz)
        if distance in (0, last):
            return [left]
        return [left, lax.rem(z + distance, nz)]

    def attend(distances):
        blocks = [b for distance in distances for b in blocks_at(distance)]
        top = r.scores[blocks[0]]
        for b in blocks[1:]:
            top = jnp.maximum(top, r.scores[b])
        top = jnp.max(top, axis=1, keepdims=True)
        pairs = [blocks[i : i + 2] for i in range(0, len(blocks), 2)]
        below = jnp.zeros((8 * np_, rb), F32)
        weights = []
        for pair in pairs:
            shifted = [jnp.exp(r.scores[b] - top) for b in pair]
            for part in shifted:
                below = below + part
            weights.append(jnp.concatenate(shifted, axis=1).astype(BF))
        below = jnp.sum(below, axis=1, keepdims=True)
        for distance in distances:
            if distance % 2 or distance == last:
                for chain in (2, 3):
                    arrive(chain, distance)
        above = jnp.zeros((8 * np_, E), F32)
        for pair, weight in zip(pairs, weights):
            above = above + nn(weight, jnp.concatenate([r.v[b] for b in pair], axis=0))
        return top, below, above

    top, below, above = attend(range(last - 1))
    for chain in (0, 1):
        arrive(chain, last)
        arrive(chain, last - 1)
    score_at(last - 1)
    score_at(last)
    top_late, below_late, above_late = attend((last, last - 1))
    highest = jnp.maximum(top, top_late)
    early, late = jnp.exp(top - highest), jnp.exp(top_late - highest)
    below = 1.0 / (below * early + below_late * late)
    attended = ((above * early + above_late * late) * below).astype(BF)
    wait_bytes(r.w2g, group - 1, r.recv_sem.at[1])
    both = nt(attended, r.w2g[...].reshape(W, E))
    terms = jnp.where(is_left, both[:, :E], both[:, E:]) + r.presidual[...]
    r.pmsg[...] = terms.reshape(np_, 8, E)
    me.to_plane(lambda peer: r.pmsg.at[peer], r.pbuf, r.send_sem.at[2], r.recv_sem.at[2])
    r.pbuf[q] = r.pmsg[q]
    wait_bytes(r.pbuf, np_ - 1, r.recv_sem.at[2])
    projected = jnp.sum(r.pbuf[...], axis=0).astype(BF).astype(F32)
    r.tmsg[...] = projected
    r.zbuf[z] = projected
    me.to_column(lambda peer: r.tmsg, r.zbuf, r.send_sem.at[3], r.recv_sem.at[3])
    wait_bytes(r.zbuf, nz - 1, r.recv_sem.at[3])
    chosen = nn(r.pick[...], r.zbuf[...].reshape(8 * nz, E).astype(BF)).astype(BF)
    r.msg[...] = chosen.reshape(pc, 16, E)
    me.to_plane(
        lambda peer: r.msg.at[lax.rem(peer, pc)], r.rbuf, r.send_sem.at[4], r.recv_sem.at[4]
    )
    r.rbuf[q] = r.msg[me.pcol]
    wait_bytes(r.rbuf, np_ - 1, r.recv_sem.at[4])
    r.ab[...] = nn(r.place_rows[...], r.rbuf[...].reshape(16 * np_, E))

    r.right_live[...] = r.ab[pl.ds(0, columns), :] * r.live_column[...]

    total = pair_tile(r, slab_tile, columns, first)
    r.grads[pl.ds(0, columns), :] = total * r.live_column[...]
    gathered = nn(r.spread_rows[...], r.grads[...].astype(BF)).astype(BF)
    r.gmsg[...] = gathered.reshape(np_, 16, E)
    me.to_plane(lambda peer: r.gmsg.at[peer], r.gbuf, r.send_sem.at[5], r.recv_sem.at[5])
    r.gbuf[q] = r.gmsg[q]
    split = slab_tile * 3 // 8
    pair_results(r, range(split), columns, first)
    wait_bytes(r.gbuf, np_ - 1, r.recv_sem.at[5])
    by_column = jnp.sum(r.gbuf[...].astype(F32).reshape(pr, pc, 16, E), axis=0)
    over_columns = jnp.sum(by_column, axis=0)
    left0 = over_columns[8:9, :]
    left1 = over_columns[9:10, :]
    sub, _ = grid_of(8, E)
    for other in range(nz):
        k = 4 * other + (sub & 3)
        lefts = jnp.where(k == k0, left0, jnp.where(k == k0 + 1, left1, 0.0))
        r.zmsg[other] = jnp.where((sub >> 2) == other % 2, by_column[other // 2, 0:8, :], lefts)
    me.to_column(lambda peer: r.zmsg.at[peer], r.hbuf, r.send_sem.at[6], r.recv_sem.at[6])
    r.hbuf[z] = r.zmsg[z]
    pair_results(r, range(split, slab_tile), columns, first)
    store = pltpu.make_async_copy(r.out, r.out_hbm, r.store_sem)
    store.start()
    wait_bytes(r.hbuf, nz - 1, r.recv_sem.at[6])
    tile = jnp.sum(r.hbuf[...], axis=0).astype(BF).astype(F32)
    r.fmsg[...] = tile
    r.fbuf[q] = tile
    me.to_plane(lambda peer: r.fmsg, r.fbuf, r.send_sem.at[7], r.recv_sem.at[7])
    odd = z & 1
    row, column = grid_of(2 * rb, 8 * np_)
    half = jnp.where(row < rb, 1 - odd, odd)
    base = (row & (np_ - 1)) * 8 + ((row >> log_np) & 3)
    halves = one_hot(column == base + 4 * half)
    for chain in range(4):
        for distance in range(1, furthest[chain] + 1):
            ring(chain, distance, 1 if distance % 2 else 2).wait_send()
    wait_bytes(r.ppg, np_ - 1, r.send_sem.at[0])
    wait_bytes(r.w2g, group - 1, r.send_sem.at[1])
    wait_bytes(r.pbuf, np_ - 1, r.send_sem.at[2])
    wait_bytes(r.zbuf, nz - 1, r.send_sem.at[3])
    wait_bytes(r.rbuf, np_ - 1, r.send_sem.at[4])
    wait_bytes(r.gbuf, np_ - 1, r.send_sem.at[5])
    wait_bytes(r.hbuf, nz - 1, r.send_sem.at[6])
    wait_bytes(r.fbuf, np_ - 1, r.recv_sem.at[7])
    tiles = r.fbuf[...].reshape(8 * np_, E).astype(BF)
    store.wait()
    halves = nn(halves, tiles).astype(BF)
    halves = jnp.concatenate([halves[:rb], halves[rb:]], axis=1)
    r.lm[...] = nt(r.pp[...], halves).astype(BF)
    wait_bytes(r.fbuf, np_ - 1, r.send_sem.at[7])


D_ACT = BF


def fused(sizes, start, operands):
    nz, pr, pc = sizes
    np_ = pr * pc
    q, k, v, res, op, pp, bias, gain, w_in, w_out, cot, mask, chain, mask_flat, chain_flat = operands
    rb = q.shape[0]
    columns = 8 * np_
    tile = 2 * np_ // pr
    group = group_of(nz)
    wz = W // group
    vmem, dma = pltpu.VMEM, pltpu.SemaphoreType.DMA
    steps = max(1, nz // 2)
    scratch = {
        "q": vmem(q.shape, BF),
        "k": vmem((nz, rb, E), BF),
        "v": vmem((nz, rb, E), BF),
        "res": vmem(res.shape, BF),
        "op": vmem(op.shape, BF),
        "pp": vmem(pp.shape, BF),
        "bias": vmem(bias.shape, F32),
        "gain": vmem(gain.shape, F32),
        "w_in": vmem(w_in.shape, BF),
        "w_out": vmem(w_out.shape, BF),
        "cot": vmem(cot.shape, BF),
        "mask": vmem(mask.shape, jnp.int32),
        "chain": vmem(chain.shape, jnp.int32),
        "mask_flat": pltpu.SMEM(mask_flat.shape, jnp.int32),
        "chain_flat": pltpu.SMEM(chain_flat.shape, jnp.int32),
        "scores": vmem((nz, 8 * np_, rb), F32),
        "q_twice": vmem((8 * np_, E), BF),
        "perm": vmem((8 * np_, rb), BF),
        "pick": vmem((pc * 16, 8 * nz), BF),
        "place_rows": vmem((columns + tile, 16 * np_), BF),
        "spread_rows": vmem((16 * np_, columns + tile), BF),
        "presidual": vmem((8 * np_, E), F32),
        "ppmsg": vmem((wz, W), BF),
        "ppg": vmem((np_, wz, W), BF),
        "w2msg": vmem((wz, E), BF),
        "w2g": vmem((group, wz, E), BF),
        "pmsg": vmem((np_, 8, E), F32),
        "pbuf": vmem((np_, 8, E), F32),
        "tmsg": vmem((8, E), F32),
        "zbuf": vmem((nz, 8, E), F32),
        "msg": vmem((pc, 16, E), BF),
        "rbuf": vmem((np_, 16, E), BF),
        "ab": vmem((columns + tile, E), F32),
        "out": vmem(cot.shape, BF),
        "store_sem": dma,
        "w_half": vmem(w_in.shape, BF),
        "w_out_half": vmem(w_out.shape, BF),
        "means": vmem((2 * E, 2 * E), BF),
        "bias_mean": vmem((2, E), F32),
        "live_column": vmem((columns, E), F32),
        "chain_column": vmem((columns, E), F32),
        "right_live": vmem((columns, E), F32),
        "act": vmem(cot.shape[:2] + w_in.shape[1:], BF),
        "d_act": vmem(cot.shape[:2] + w_in.shape[1:], D_ACT),
        "grads": vmem((columns + tile, E), F32),
        "gmsg": vmem((np_, 16, E), BF),
        "gbuf": vmem((np_, 16, E), BF),
        "zmsg": vmem((nz, 8, E), F32),
        "hbuf": vmem((nz, 8, E), F32),
        "fmsg": vmem((8, E), F32),
        "fbuf": vmem((np_, 8, E), F32),
        "known_sem": pltpu.SemaphoreType.REGULAR,
        "load_sem": dma((len(LOADS),)),
        "ring_send": dma((4, steps)),
        "ring_recv": dma((4, steps)),
        "send_sem": dma((8,)),
        "recv_sem": dma((8,)),
    }
    hbm = pl.BlockSpec(memory_space=pltpu.HBM)
    return pl.pallas_call(
        functools.partial(kernel, sizes, INPUTS + ("out_hbm", "lm") + tuple(scratch)),
        out_shape=(
            jax.ShapeDtypeStruct(cot.shape, BF),
            jax.ShapeDtypeStruct((pp.shape[0], rb), BF),
        ),
        in_specs=[pl.BlockSpec(memory_space=pltpu.SMEM)] + [hbm] * len(operands),
        out_specs=(hbm, pl.BlockSpec(memory_space=pltpu.VMEM)),
        scratch_shapes=list(scratch.values()),
        compiler_params=pltpu.CompilerParams(
            collective_id=0, has_side_effects=True, vmem_limit_bytes=58 << 20
        ),
        name="attend_pair_and_gradient",
    )(start, *operands)


def store_kernel(out, lm, out_hbm, lm_hbm, out_vmem, lm_vmem, load_sem, save_sem):
    parts = load_sem.shape[0] - 1
    rows = out.shape[0] // parts
    ways = [(lm, lm_vmem, lm_hbm)]
    for i in range(parts):
        part = pl.ds(i * rows, rows)
        ways.append((out.at[part], out_vmem.at[part], out_hbm.at[part]))
    loads = [pltpu.make_async_copy(w[0], w[1], load_sem.at[i]) for i, w in enumerate(ways)]
    saves = [pltpu.make_async_copy(w[1], w[2], save_sem.at[i]) for i, w in enumerate(ways)]
    for load in loads:
        load.start()
    for load, save in zip(loads, saves):
        load.wait()
        save.start()
    for save in saves:
        save.wait()


def store(out, lm):
    parts = min(8, out.shape[0]) + 1
    return pl.pallas_call(
        store_kernel,
        out_shape=tuple(jax.ShapeDtypeStruct(a.shape, a.dtype) for a in (out, lm)),
        in_specs=[pl.BlockSpec(memory_space=pltpu.HBM)] * 2,
        out_specs=(pl.BlockSpec(memory_space=pltpu.HBM),) * 2,
        scratch_shapes=[
            pltpu.VMEM(out.shape, out.dtype),
            pltpu.VMEM(lm.shape, lm.dtype),
            pltpu.SemaphoreType.DMA((parts,)),
            pltpu.SemaphoreType.DMA((parts,)),
        ],
        compiler_params=pltpu.CompilerParams(vmem_limit_bytes=62 << 20),
        name="store_results",
    )(out, lm)


def body(
    sizes,
    queries,
    keys,
    values,
    residual,
    out_proj,
    pair_proj,
    chain_bias,
    ln_gain,
    w_in,
    w_out,
    pair_cot,
    residue_mask,
    chain_ids,
    slab_start,
):
    nz, rb = sizes[0], queries.shape[0]
    operands = (
        queries,
        keys,
        values,
        residual.T,
        out_proj,
        pair_proj,
        chain_bias,
        ln_gain.reshape(1, E),
        w_in,
        w_out,
        pair_cot,
        residue_mask.reshape(nz, rb),
        chain_ids.reshape(nz, rb),
        residue_mask,
        chain_ids,
    )
    pair_out, lm_grad = store(*fused(sizes, slab_start, operands))
    return pair_out, lm_grad.T


def solution(mesh):
    sizes = tuple(mesh.shape[name] for name in ("lm", "prow", "pcol"))
    return jax.shard_map(
        functools.partial(body, sizes),
        mesh=mesh,
        in_specs=(
            P("lm", ("prow", "pcol")),
            P("lm", ("prow", "pcol")),
            P("lm", ("prow", "pcol")),
            P("lm", ("prow", "pcol")),
            P(("prow", "pcol"), None),
            P(("prow", "pcol"), None),
            P(),
            P(),
            P(),
            P(),
            P(("lm", "prow"), "pcol", None),
            P(),
            P(),
            P(),
        ),
        out_specs=(P(("lm", "prow"), "pcol", None), P("lm", ("prow", "pcol"))),
        check_vma=False,
    )
```
